32 devices in a mesh: seq: 8 (over z, x), batch: 4 (over y, core).
Axes of the slice: x: 2, y: 2, z: 4, core: 2. Of those that a mesh axis runs over, the one named last changes fastest.
Arguments:
- tokens: bfloat16 [8, 1024, 768], P('batch', 'seq'), may hold values from -6 to 6
- cotangent: bfloat16 [8, 1024, 768], P('batch', 'seq'), may hold values from -6 to 6
- lengths: int32 [8, 3], P('batch'), may hold values from 1 to 960, 1024 in all within a row
- attn_in: bfloat16 [2, 768, 2304], P(None, None, 'batch'), may hold values from -0.21875 to 0.21875
- attn_out: bfloat16 [2, 768, 768], P(None, None, 'batch'), may hold values from -1.25 to 1.25
- mlp_in: bfloat16 [2, 768, 3072], P(None, None, 'batch'), may hold values from -0.21875 to 0.21875
- mlp_out: bfloat16 [2, 3072, 768], P(None, None, 'batch'), may hold values from -0.109375 to 0.109375
- norm_gains: bfloat16 [2, 2, 768], P(None, None, 'batch'), may hold values from 0.5 to 1.5
- norm_biases: bfloat16 [2, 2, 768], P(None, None, 'batch'), may hold values from -1.5 to 1.5
- feature_maps: bfloat16 [2, 2, 64, 768], P(None, None, None, 'batch'), may hold values from -1.5 to 1.5
Outputs:
- block_output: bfloat16 [8, 1024, 768], P('batch', 'seq')
- grad_tokens: bfloat16 [8, 1024, 768], P('batch', 'seq')
- grad_attn_in: float32 [2, 768, 2304], P(None, None, 'batch')
- grad_attn_out: float32 [2, 768, 768], P(None, None, 'batch')
- grad_mlp_in: float32 [2, 768, 3072], P(None, None, 'batch')
- grad_mlp_out: float32 [2, 3072, 768], P(None, None, 'batch')
- grad_norm_gains: float32 [2, 2, 768], P(None, None, 'batch')
- grad_norm_biases: float32 [2, 2, 768], P(None, None, 'batch')
- grad_feature_maps: float32 [2, 2, 64, 768], P(None, None, None, 'batch')
- grad_mlp_norm_biases: float32 [2, 768], P(None, 'batch')
The draws below stay inside these ranges and needn't reach their ends.
Inputs may be any that keep to these rules, and one draw needn't show every extreme that they name: `lengths`: the 3 sequences of a row lie end to end and fill its 1024 positions; the longest has exactly 960 positions.
All inputs are finite; a program needn't handle non-finite values.
Results may differ from the reference program's by a relative error of at most 0.025.
Values may be sent and summed in bfloat16 or wider, within the bound.
A program may use at most 320 MiB of HBM per device.

```python
import math
import jax
import jax.numpy as jnp
import numpy as np
from jax import lax

D = 768
H = 12
HD = 64
FF = 3072
LAYERS = 2
SEQS = 3
TOK_DEV = 128
SEQ_LEN = 1024
ROWS = 8


def levels(key, shape, split, low, high):
    factor_of = 1.0
    for dim, blocks in split:
        steps = jax.random.uniform(jax.random.fold_in(jax.random.fold_in(key, 6), dim), (blocks,), jnp.float32, low / len(split), high / len(split))
        factor_of = factor_of * jnp.repeat(jnp.exp(steps), shape[dim] // blocks).reshape((-1,) + (1,) * (len(shape) - 1 - dim))
    return factor_of


def profile(number_of, total, bound, slope):
    loads = [(1 << 20) // math.isqrt(rank ** slope) + 1 for rank in range(2, number_of + 1)]
    spare, given = total - bound - (number_of - 1), [1] * (number_of - 1)
    while spare > 0:
        candidates = [i for i in range(number_of - 1) if given[i] < bound]
        whole, left = sum([loads[i] for i in candidates]), spare
        for i in candidates:
            extra = min(bound - given[i], max(1, left * loads[i] // whole), spare)
            given[i] = given[i] + extra
            spare = spare - extra
    return np.array([bound] + given)


def uneven(own_key, amount, total, limit, slope):
    if amount == 2:
        one = jax.random.randint(own_key, (), max(1, total - limit), min(limit, total - 1) + 1)
        return jnp.stack([one, total - one])
    sizes = jnp.asarray(profile(amount, total, limit, slope), jnp.int32)
    couples = (amount - 1) // 2
    giver, sink = sizes[1:1 + 2 * couples:2], sizes[2:2 + 2 * couples:2]
    slack = jnp.minimum(giver - 1, limit - sink)
    passed = jax.random.randint(jax.random.fold_in(own_key, 1), (couples,), 0, 1 << 20) % (slack + 1)
    sizes = sizes.at[1:1 + 2 * couples:2].set(giver - passed).at[2:2 + 2 * couples:2].set(sink + passed)
    return sizes[jax.random.permutation(jax.random.fold_in(own_key, 2), amount)]


def scatter_about(own_key, dims, scale, most, cuts=(), kind=jnp.bfloat16):
    result = scale * jax.random.normal(own_key, dims, jnp.float32)
    if cuts:
        result = result * levels(own_key, dims, cuts, -0.22, 0.18)
    return jnp.clip(result, -most, most).astype(kind)


def setup_inputs(seed: int = 0) -> dict:
    splits = jax.random.split(jax.random.key(seed), 11)
    return {
        "tokens": scatter_about(splits[0], (ROWS, SEQ_LEN, D), 1.0, 6.0, ((0, 4), (1, 8))),
        "cotangent": scatter_about(splits[1], (ROWS, SEQ_LEN, D), 1.0, 6.0, ((0, 4), (1, 8))),
        "lengths": jax.vmap(lambda own: uneven(own, SEQS, SEQ_LEN, SEQ_LEN - TOK_DEV // 2, 0))(jax.random.split(splits[2], ROWS)).reshape((ROWS, SEQS)).astype(jnp.int32),
        "attn_in": scatter_about(splits[3], (LAYERS, D, 3 * D), D ** -0.5, 0.21875, ((2, 4),)),
        "attn_out": scatter_about(splits[4], (LAYERS, D, D), (D // 32) ** -0.5, 1.25, ((2, 4),)),
        "mlp_in": scatter_about(splits[5], (LAYERS, D, FF), D ** -0.5, 0.21875, ((2, 4),)),
        "mlp_out": scatter_about(splits[6], (LAYERS, FF, D), FF ** -0.5, 0.109375, ((2, 4),)),
        "norm_gains": jnp.clip(1.0 + 0.1 * jax.random.normal(splits[7], (LAYERS, 2, D), jnp.float32), 0.5, 1.5).astype(jnp.bfloat16),
        "norm_biases": scatter_about(splits[8], (LAYERS, 2, D), 0.3, 1.5, ((2, 4),)),
        "feature_maps": scatter_about(splits[9], (LAYERS, 2, HD, H * HD), (HD // 4) ** -0.5, 1.5, ((3, 4),)),
    }


@jax.custom_vjp
def low(v):
    return lax.optimization_barrier(v.astype(jnp.bfloat16)).astype(jnp.float32)

@jax.custom_vjp
def low_back(v):
    return v

def low_keep(v):
    return (low(v), None)

def low_pass(kept, grad):
    return (grad,)

def back_keep(v):
    return (v, None)

def back_low(kept, grad):
    return (low(grad),)
low.defvjp(low_keep, low_pass)
low_back.defvjp(back_keep, back_low)
EPSILON = 1e-05
HIGH = lax.Precision.HIGHEST

def layer_norm(inputs, norm_gain, norm_shift):
    average = lax.optimization_barrier(jnp.mean(inputs, axis=-1, keepdims=True))
    centred = inputs - average
    spread = lax.optimization_barrier(jnp.mean(centred * centred, axis=-1, keepdims=True))
    return centred * lax.rsqrt(spread + EPSILON) * norm_gain + norm_shift

def feature(inputs, maps):
    logits = jnp.einsum('shd,hde->she', inputs, maps, precision=HIGH)
    return jnp.concatenate([jax.nn.softmax(logits, axis=-1), jax.nn.softmax(-logits, axis=-1)], axis=-1)

def attend_row(feat_query, feat_key, value_part, segment_ids):
    block = min(512, SEQ_LEN)
    count = SEQ_LEN // block
    lower = jnp.tril(jnp.ones((block, block), jnp.float32))

    def step(carry, pieces):
        state_sum, state_norm, carry_segment = carry
        block_query, block_key, block_value, block_segment = pieces
        same = (block_segment[:, None] == block_segment[None, :]).astype(jnp.float32) * lower
        scores = jnp.einsum('ihf,jhf->hij', block_query, block_key, precision=HIGH) * same[None]
        in_chain = (block_segment == carry_segment).astype(jnp.float32)
        numerator = jnp.einsum('hij,jhd->ihd', scores, block_value, precision=HIGH)
        numerator = numerator + in_chain[:, None, None] * jnp.einsum('ihf,hfd->ihd', block_query, state_sum, precision=HIGH)
        denominator = jnp.transpose(lax.optimization_barrier(jnp.sum(scores, axis=2)))
        denominator = denominator + in_chain[:, None] * jnp.einsum('ihf,hf->ih', block_query, state_norm, precision=HIGH)
        attended = numerator / denominator[:, :, None]
        last_segment = block_segment[-1]
        carried = (last_segment == carry_segment).astype(jnp.float32)
        in_last = (block_segment == last_segment).astype(jnp.float32)
        masked_key = block_key * in_last[:, None, None]
        state_sum = carried * state_sum + jnp.einsum('jhf,jhd->hfd', masked_key, block_value, precision=HIGH)
        state_norm = carried * state_norm + lax.optimization_barrier(jnp.sum(masked_key, axis=0))
        return ((state_sum, state_norm, last_segment), attended)
    initial = (jnp.zeros((H, 2 * HD, HD), jnp.float32), jnp.zeros((H, 2 * HD), jnp.float32), jnp.array(-1, jnp.int32))
    pieces = (feat_query.reshape(count, block, H, 2 * HD), feat_key.reshape(count, block, H, 2 * HD), value_part.reshape(count, block, H, HD), segment_ids.reshape(count, block))
    final_carry, attended = lax.scan(jax.checkpoint(step), initial, pieces)
    return attended.reshape(SEQ_LEN, H * HD)

def forward_row(hidden, segment_ids, params):
    attn_in, attn_out, mlp_in, mlp_out, gains, shifts, maps = params
    for layer in range(LAYERS):
        normed = low(layer_norm(hidden, gains[layer, 0], shifts[layer, 0]))
        projected = low_back(jnp.dot(normed, attn_in[layer], precision=HIGH, preferred_element_type=jnp.float32))
        query_part = projected[:, :D].reshape(SEQ_LEN, H, HD)
        key_part = projected[:, D:2 * D].reshape(SEQ_LEN, H, HD)
        value_part = projected[:, 2 * D:].reshape(SEQ_LEN, H, HD)
        layer_maps = jnp.transpose(maps[layer].reshape(2, HD, H, HD), (0, 2, 1, 3))
        feat_query = feature(query_part, layer_maps[0])
        feat_key = feature(key_part, layer_maps[1])
        attended = attend_row(feat_query, feat_key, value_part, segment_ids)
        hidden = hidden + low_back(jnp.dot(low(attended), attn_out[layer], precision=HIGH, preferred_element_type=jnp.float32))
        normed = low(layer_norm(hidden, gains[layer, 1], shifts[layer, 1]))
        upward = low_back(jnp.dot(normed, mlp_in[layer], precision=HIGH, preferred_element_type=jnp.float32))
        activated_hidden = low(jax.nn.gelu(upward, approximate=True))
        hidden = hidden + low_back(jnp.dot(activated_hidden, mlp_out[layer], precision=HIGH, preferred_element_type=jnp.float32))
    return hidden

def reference(tokens, cotangent, lengths, attn_in, attn_out, mlp_in, mlp_out, norm_gains, norm_biases, feature_maps):
    params = (attn_in.astype(jnp.float32), attn_out.astype(jnp.float32), mlp_in.astype(jnp.float32), mlp_out.astype(jnp.float32), norm_gains.astype(jnp.float32), norm_biases.astype(jnp.float32), feature_maps.astype(jnp.float32))
    positions = jnp.arange(SEQ_LEN, dtype=jnp.int32)

    def per_row(totals, row_data):
        row_tokens, row_cotangent, row_lengths = row_data
        starts = (jnp.cumsum(row_lengths) - row_lengths).astype(jnp.int32)
        segment_ids = (lax.optimization_barrier(jnp.sum((starts[None, :] <= positions[:, None]).astype(jnp.int32), axis=1)) - 1).astype(jnp.int32)

        def forward_fixed(hidden, weight_tree):
            return forward_row(hidden, segment_ids, weight_tree)
        output, pullback = jax.vjp(forward_fixed, row_tokens.astype(jnp.float32), params)
        grad_input, grad_params = pullback(row_cotangent.astype(jnp.float32))
        totals = jax.tree.map(jnp.add, totals, grad_params)
        return (totals, (output.astype(jnp.bfloat16), grad_input.astype(jnp.bfloat16)))
    zero_grads = jax.tree.map(jnp.zeros_like, params)
    totals, outputs = lax.scan(per_row, zero_grads, (tokens, cotangent, lengths))
    return (outputs[0], outputs[1], totals[0], totals[1], totals[2], totals[3], totals[4], totals[5], totals[6], totals[5][:, 1])
```

```python
import functools

import jax
import jax.numpy as jnp
from jax import lax
from jax.experimental import pallas as pl
from jax.experimental.pallas import tpu as pltpu
from jax.sharding import PartitionSpec as P

D = 768
H = 12
HD = 64
EPSILON = 1e-05
HIGH = lax.Precision.HIGH
BF = jnp.bfloat16
MESH = pl.DeviceIdType.MESH


def greet(peers):
    bar = pltpu.get_barrier_semaphore()
    for p in peers:
        pl.semaphore_signal(bar, inc=1, device_id=p, device_id_type=MESH)
    pl.semaphore_wait(bar, len(peers))

def remote(src, dst, ss, rs, dev):
    return pltpu.make_async_remote_copy(src_ref=src, dst_ref=dst, send_sem=ss, recv_sem=rs, device_id=dev, device_id_type=MESH)

def arrive(ref, sem):
    pltpu.make_async_copy(ref, ref, sem).wait()

def reduce_kernel(n, N, R, g_ref, o_ref, own, recvC, recvY, recvX, recvZ1, recvZ2, recvH, fin, out32,
                  lsem, csem, ysem, xsem, z1sem, z2sem, hsem, a2sem, a1sem, bsem, osem):
    s = lax.axis_index("seq"); b = lax.axis_index("batch")
    xl = s % 2; z = s // 2; b0 = z % 2; b1 = (z // 2) % 2
    levels = [l for l in range(2, 10) if (1 << l) < n // 2]
    par = b % 2; yy = b // 2
    core_dev = (s, b + 1 - 2 * par); y_dev = (s, (b + 2) % 4); x_dev = (s + 1 - 2 * xl, b)
    z1_dev = (s + 2 * (1 - 2 * b0), b); z2_dev = (s + 4 * (1 - 2 * b1), b)
    h_dev = lambda l: (s + (2 << l) * (1 - 2 * ((z // (1 << l)) % 2)), b)
    greet([core_dev, y_dev, x_dev, z1_dev, z2_dev] + [h_dev(l) for l in levels])
    ds = lambda i, k: pl.ds(pl.multiple_of(i * k, k), k)
    xc = ds(xl, 384); xo = ds(1 - xl, 384)
    Q = R // 4
    half = ds(b0, R // 2); quarter = pl.ds(pl.multiple_of(b0 * (R // 2) + b1 * Q, Q), Q)
    cC = lambda c: remote(g_ref.at[c, 1 - par], recvC.at[c], csem.at[0, c], csem.at[1, c], core_dev)
    cL = lambda c: pltpu.make_async_copy(g_ref.at[c, par], own.at[c % 8], lsem.at[c % 8])
    cY = lambda c: remote(recvC.at[c, 1 - yy], recvY.at[c], ysem.at[0, c], ysem.at[1, c], y_dev)
    cX = lambda c: remote(recvY.at[c, :, xo], recvX.at[c], xsem.at[0, c], xsem.at[1, c], x_dev)
    cZ1 = lambda c: remote(recvX.at[c, ds(1 - b0, R // 2)], recvZ1.at[c], z1sem.at[0, c], z1sem.at[1, c], z1_dev)
    cZ2 = lambda c: remote(recvZ1.at[c, ds(1 - b1, Q)], recvZ2.at[c], z2sem.at[0, c], z2sem.at[1, c], z2_dev)
    cH = lambda c, i: remote(recvH.at[c, len(levels)], recvH.at[c, i], hsem.at[0, c], hsem.at[1, c], h_dev(levels[i]))
    cA2 = lambda c: remote(fin.at[c, quarter, xc], fin.at[c, quarter, xc], a2sem.at[0, c], a2sem.at[1, c], z2_dev)
    cA1 = lambda c: remote(fin.at[c, half, xc], fin.at[c, half, xc], a1sem.at[0, c], a1sem.at[1, c], z1_dev)
    cB = lambda c: remote(fin.at[c, :, xc], fin.at[c, :, xc], bsem.at[0, c], bsem.at[1, c], x_dev)
    cO = lambda c: pltpu.make_async_copy(out32.at[c % 2], o_ref.at[c], osem.at[c % 2])
    f32 = jnp.float32; bf = BF
    def add(a, b_): return (a.astype(f32) + b_.astype(f32)).astype(bf)
    def when(c, fn):
        @pl.when((c >= 0) & (c < N))
        def _(): fn(c)
    def stage0(c):
        cL(c).start(); cC(c).start()
    def stageY(c):
        cL(c).wait(); cC(c).wait_recv()
        recvC[c, 1 - yy] = add(recvC[c, 1 - yy], own[c % 8, 1 - yy])
        cY(c).start()
        recvC[c, yy] = add(recvC[c, yy], own[c % 8, yy])
    def stageX(c):
        cY(c).wait_recv()
        recvY[c, :, xo] = add(recvY[c, :, xo], recvC[c, yy, :, xo])
        cX(c).start()
        recvY[c, :, xc] = add(recvY[c, :, xc], recvC[c, yy, :, xc])
    def stageZ1(c):
        cX(c).wait_recv()
        recvX[c] = add(recvX[c], recvY[c, :, xc])
        cZ1(c).start()
    def stageZ2(c):
        cZ1(c).wait_recv()
        recvZ1[c] = add(recvZ1[c], recvX[c, half])
        cZ2(c).start()
    def stageA2(c):
        cZ2(c).wait_recv()
        t = add(recvZ2[c], recvZ1[c, ds(b1, Q)])
        for i in range(len(levels)):
            recvH[c, len(levels)] = t
            cH(c, i).start(); cH(c, i).wait()
            t = add(t, recvH[c, i])
        fin[c, quarter, xc] = t
        cA2(c).start()
    def stageA1(c):
        cA2(c).wait_recv(); cA1(c).start()
    def stageB(c):
        cA1(c).wait_recv(); cB(c).start()
    def stageO(c):
        cB(c).wait_recv()
        @pl.when(c >= 2)
        def _(): cO(c - 2).wait()
        out32[c % 2] = fin[c].astype(f32)
        cO(c).start()
    def drain(c, carry):
        for f in (cC, cY, cX, cZ1, cZ2, cA2, cA1, cB): f(c).wait_send()
        return carry
    stages = [stage0, stageY, stageX, stageZ1, stageZ2, stageA2, stageA1, stageB, stageO]
    def step(t, carry):
        for i, f in enumerate(stages): when(t - i, f)
        return carry
    lax.fori_loop(0, N + 8, step, 0)
    for c in range(max(0, N - 2), N): cO(c).wait()
    lax.fori_loop(0, N, drain, 0)

def reduce_grads(n, g):
    N, _, _, R, _ = g.shape
    bf = BF
    nl = len([l for l in range(2, 10) if (1 << l) < n // 2])
    S = lambda: pltpu.SemaphoreType.DMA((2, N))
    V = lambda *shp: pltpu.VMEM(shp, bf)
    return pl.pallas_call(functools.partial(reduce_kernel, n, N, R), name="reduce_grads",
        out_shape=jax.ShapeDtypeStruct((N, R, D), jnp.float32),
        in_specs=[pl.BlockSpec(memory_space=pl.ANY)], out_specs=pl.BlockSpec(memory_space=pl.ANY),
        scratch_shapes=[V(8, 2, R, D), V(N, 2, R, D), V(N, R, D), V(N, R, 384), V(N, R // 2, 384), V(N, R // 4, 384),
            V(N if nl else 1, nl + 1, R // 4, 384), V(N, R, D), pltpu.VMEM((2, R, D), jnp.float32),
            pltpu.SemaphoreType.DMA((8,))] + [S() for _ in range(9)] + [pltpu.SemaphoreType.DMA((2,))],
        compiler_params=pltpu.CompilerParams(collective_id=1, has_side_effects=True, vmem_limit_bytes=62*2**20))(g)

def offsets(c, b):
    if c < 3:
        return b * 576 + c * 192
    if c < 4:
        return 2304 + b * 192
    if c < 8:
        return 3072 + b * 768 + (c - 4) * 192
    return 6144 + (c - 8) * 768 + b * 192


def gather_kernel(
    w_ref, s_ref, o_ref, t_ref, lsem, ysem, xsem, own_sem, near_sem, far_sem, small_sem
):
    s = lax.axis_index("seq")
    b = lax.axis_index("batch")
    xl = s % 2
    core = b + 1 - 2 * (b % 2)
    far = (b + 2) % 4
    layers = w_ref.shape[0]
    core_dev, y_dev, x_dev = (s, core), (s, far), (s + 1 - 2 * xl, b)
    others = [(s, (b + k) % 4) for k in range(1, 4)]
    greet([core_dev, y_dev, x_dev, (s, (far + 1 - 2 * (far % 2)))])
    smalls = [
        remote(s_ref, t_ref.at[b], small_sem.at[0, k], small_sem.at[1, 2 - k], dev)
        for k, dev in enumerate(others)
    ]
    small_here = pltpu.make_async_copy(s_ref, t_ref.at[b], lsem.at[layers * 12])
    for copy in smalls + [small_here]:
        copy.start()

    def rows(c, who, part, size):
        return pl.ds(pl.multiple_of(offsets(c % 12, who) + part * 96, 32), size)

    def same(c, who, part, size, sem, dev):
        place = o_ref.at[c // 12, rows(c, who, part, size)]
        return remote(place, place, sem.at[0, c], sem.at[1, c], dev)

    def here(c):
        return w_ref.at[c // 12, pl.ds((c % 12) * 192, 192)]

    def out_y(c):
        src = w_ref.at[c // 12, pl.ds(pl.multiple_of((c % 12) * 192 + xl * 96, 32), 96)]
        return remote(src, o_ref.at[c // 12, rows(c, b, xl, 96)], ysem.at[0, c], ysem.at[1, c], y_dev)

    def out_core(c):
        return remote(here(c), o_ref.at[c // 12, rows(c, b, 0, 192)], own_sem.at[0, c], own_sem.at[1, c], core_dev)

    def stay(c):
        return pltpu.make_async_copy(here(c), o_ref.at[c // 12, rows(c, b, 0, 192)], lsem.at[c])

    out_x = lambda c: same(c, far, xl, 96, xsem, x_dev)
    near = lambda c: same(c, far, xl, 96, near_sem, core_dev)
    last = lambda c: same(c, far, 1 - xl, 96, far_sem, core_dev)
    count = layers * 12
    for c in range(count):
        out_y(c).start()
        out_core(c).start()
        stay(c).start()
    for c in range(count + 1):
        if c < count:
            out_y(c).wait_recv()
            out_x(c).start()
            near(c).start()
        if c >= 1:
            out_x(c - 1).wait_recv()
            last(c - 1).start()
    for c in range(count):
        stay(c).wait()
        for copy in (out_core(c), near(c), last(c)):
            copy.wait()
        out_y(c).wait_send()
        out_x(c).wait_send()
    small_here.wait()
    for copy in smalls:
        copy.wait()


def gather_weights(w, small):
    layers = w.shape[0]
    pair = lambda: pltpu.SemaphoreType.DMA((2, layers * 12))
    return pl.pallas_call(
        gather_kernel,
        name="gather_weights",
        out_shape=(
            jax.ShapeDtypeStruct((layers, 9216, D), BF),
            jax.ShapeDtypeStruct((4,) + small.shape, BF),
        ),
        in_specs=[pl.BlockSpec(memory_space=pl.ANY)] * 2,
        out_specs=[pl.BlockSpec(memory_space=pl.ANY)] * 2,
        scratch_shapes=[pltpu.SemaphoreType.DMA((layers * 12 + 1,))]
        + [pair() for _ in range(5)]
        + [pltpu.SemaphoreType.DMA((2, 3))],
        compiler_params=pltpu.CompilerParams(collective_id=0, has_side_effects=True),
    )(w, small)


def layer_norm(inputs, norm_gain, norm_shift):
    average = jnp.mean(inputs, axis=-1, keepdims=True)
    centred = inputs - average
    spread = jnp.mean(centred * centred, axis=-1, keepdims=True)
    return centred * lax.rsqrt(spread + EPSILON) * norm_gain + norm_shift


def activate(inputs):
    return jax.nn.gelu(inputs, approximate=True)


def feature(inputs, maps):
    logits = jnp.einsum("mshd,hde->mshe", inputs, maps, precision=HIGH)
    return jnp.concatenate(
        [jax.nn.softmax(logits, axis=-1), jax.nn.softmax(-logits, axis=-1)], axis=-1
    )


def shards(tokens, cotangent, lengths, attn_in, attn_out, mlp_in, mlp_out, norm_gains, norm_biases, feature_maps):
    micro_count, tok_rows, _ = tokens.shape
    layer_count = attn_in.shape[0]
    n = lax.axis_size("seq")
    me = lax.axis_index("seq")
    first_position = me * tok_rows
    positions = first_position + jnp.arange(tok_rows, dtype=jnp.int32)
    starts = jnp.cumsum(lengths, axis=1) - lengths
    seg = lambda p: jnp.sum((starts[:, None, :] <= p[None, :, None]).astype(jnp.int32), axis=2) - 1
    segment_ids = seg(positions)
    firsts = jnp.arange(n, dtype=jnp.int32) * tok_rows
    prior_all = seg(firsts - 1)
    final_all = seg(firsts + tok_rows - 1)
    prior_segment = seg((first_position - 1)[None])
    final_segment = segment_ids[:, -1:]
    in_chain = (segment_ids == prior_segment).astype(jnp.float32)
    in_last = (segment_ids == final_segment).astype(jnp.float32)
    order = jnp.arange(n)
    take = ((final_all == prior_segment) & (order < me)[None]).astype(jnp.float32)
    give = ((prior_all == final_segment) & (order > me)[None]).astype(jnp.float32)
    lower = jnp.tril(jnp.ones((tok_rows, tok_rows), jnp.float32))
    same_mask = (segment_ids[:, :, None] == segment_ids[:, None, :]).astype(jnp.float32) * lower[None]

    packed = jnp.concatenate(
        [
            jnp.swapaxes(attn_in, 1, 2),
            jnp.swapaxes(attn_out, 1, 2),
            mlp_in,
            jnp.transpose(mlp_out.reshape(layer_count, 4, 768, 192), (0, 1, 3, 2)).reshape(layer_count, 768, 768),
        ],
        axis=1,
    )
    small = jnp.concatenate([norm_gains[:, :, None], norm_biases[:, :, None], feature_maps], axis=2)
    small = jnp.pad(small.reshape(layer_count * 2 * 66, 192), ((0, (-layer_count * 132) % 16), (0, 64)))
    weights, smalls = gather_weights(packed, small)
    smalls = smalls[:, : layer_count * 132, :192].reshape(4, layer_count, 2, 66, 192)
    smalls = jnp.transpose(smalls, (1, 2, 3, 0, 4)).reshape(layer_count, 2, 66, 768).astype(jnp.float32)

    def prepare(projected, raw_maps):
        layer_maps = jnp.transpose(raw_maps.reshape(2, HD, H, HD), (0, 2, 1, 3))
        query_part = projected[..., :D].reshape(micro_count, tok_rows, H, HD)
        key_part = projected[..., D : 2 * D].reshape(micro_count, tok_rows, H, HD)
        value_part = projected[..., 2 * D :].reshape(micro_count, tok_rows, H, HD)
        return (feature(query_part, layer_maps[0]), feature(key_part, layer_maps[1]), value_part)

    def summarize(feat_key, value_part):
        masked_key = feat_key * in_last[:, :, None, None]
        return (
            jnp.einsum("mjhf,mjhd->mhfd", masked_key, value_part, precision=HIGH),
            jnp.sum(masked_key, axis=1),
        )

    def exchange(state, pick):
        both = jnp.concatenate([state[0], state[1][..., None]], axis=-1).astype(BF)
        every = lax.all_gather(both.reshape(micro_count, H * 2 * HD * (HD + 1)), "seq")
        got = jnp.einsum("kmx,mk->mx", every, pick.astype(BF), preferred_element_type=jnp.float32)
        got = got.reshape(micro_count, H, 2 * HD, HD + 1)
        return got[..., :HD], got[..., HD]

    def read_out(feat_query, feat_key, value_part, state_sum, state_norm):
        scores = jnp.einsum("mihf,mjhf->mhij", feat_query, feat_key, precision=HIGH) * same_mask[:, None]
        numerator = jnp.einsum("mhij,mjhd->mihd", scores, value_part, precision=HIGH)
        numerator = numerator + in_chain[:, :, None, None] * jnp.einsum(
            "mihf,mhfd->mihd", feat_query, state_sum, precision=HIGH
        )
        denominator = jnp.transpose(jnp.sum(scores, axis=3), (0, 2, 1))
        denominator = denominator + in_chain[:, :, None] * jnp.einsum(
            "mihf,mhf->mih", feat_query, state_norm, precision=HIGH
        )
        return (numerator / denominator[..., None]).reshape(micro_count, tok_rows, H * HD)

    F32 = jnp.float32
    hidden = tokens.astype(F32)
    saved = []
    parts = [
        (weights[l, :2304], weights[l, 2304:3072], weights[l, 3072:6144].reshape(4, 768, 768), weights[l, 6144:].reshape(4, 768, 768))
        for l in range(layer_count)
    ]
    for layer in range(layer_count):
        w_in, w_out, w_up, w_down = parts[layer]
        gains, shifts, maps = smalls[layer, :, 0], smalls[layer, :, 1], smalls[layer, :, 2:]
        normed_first, norm_first_back = jax.vjp(layer_norm, hidden, gains[0], shifts[0])
        normed_attn = normed_first.astype(BF)
        projected = jnp.einsum("mrd,cd->mrc", normed_attn, w_in, preferred_element_type=F32)
        features, prepare_back = jax.vjp(prepare, projected, maps)
        local_state, summary_back = jax.vjp(summarize, features[1], features[2])
        incoming = exchange(local_state, take)
        attended, reread_output = jax.vjp(read_out, features[0], features[1], features[2], incoming[0], incoming[1])
        attended_low = attended.astype(BF)
        middle = hidden + jnp.einsum("mri,oi->mro", attended_low, w_out, preferred_element_type=F32)
        normed_second, norm_second_back = jax.vjp(layer_norm, middle, gains[1], shifts[1])
        normed_mlp = normed_second.astype(BF)
        upward = jnp.einsum("mrd,kdc->mrkc", normed_mlp, w_up, preferred_element_type=F32)
        activated_full, gelu_back = jax.vjp(activate, upward)
        activated = activated_full.astype(BF)
        hidden = middle + jnp.einsum("mrkc,koc->mro", activated, w_down, preferred_element_type=F32)
        saved.append(
            (norm_first_back, normed_attn, prepare_back, summary_back, reread_output, attended_low, norm_second_back, normed_mlp, gelu_back, activated)
        )
    block_output = hidden.astype(BF)
    grad_hidden = cotangent.astype(F32)
    chunks = [None] * layer_count
    small_grads = [None] * layer_count
    for layer in reversed(range(layer_count)):
        (norm_first_back, normed_attn, prepare_back, summary_back, reread_output, attended_low, norm_second_back, normed_mlp, gelu_back, activated) = saved[layer]
        w_in, w_out, w_up, w_down = parts[layer]
        grad_low = grad_hidden.astype(BF)
        g_down = jnp.einsum("mro,mrkc->koc", grad_low, activated, preferred_element_type=F32)
        grad_activated = jnp.einsum("mro,koc->mrkc", grad_low, w_down, preferred_element_type=F32)
        grad_upward = gelu_back(grad_activated)[0].astype(BF)
        g_up = jnp.einsum("mrd,mrkc->kdc", normed_mlp, grad_upward, preferred_element_type=F32)
        grad_normed_mlp = jnp.einsum("mrkc,kdc->mrd", grad_upward, w_up, preferred_element_type=F32)
        grad_middle_norm, gg2, gb2 = norm_second_back(grad_normed_mlp)
        grad_middle = grad_hidden + grad_middle_norm
        grad_branch = grad_middle.astype(BF)
        g_out = jnp.einsum("mro,mri->oi", grad_branch, attended_low, preferred_element_type=F32)
        grad_attended = jnp.einsum("mro,oi->mri", grad_branch, w_out, preferred_element_type=F32)
        gq, gk, gv, gs, gn = reread_output(grad_attended)
        outgoing = exchange((gs, gn), give)
        gk_more, gv_more = summary_back(outgoing)
        grad_projected, g_maps = prepare_back((gq, gk + gk_more, gv + gv_more))
        grad_projected_low = grad_projected.astype(BF)
        g_in = jnp.einsum("mrc,mrd->cd", grad_projected_low, normed_attn, preferred_element_type=F32)
        grad_normed_attn = jnp.einsum("mrc,cd->mrd", grad_projected_low, w_in, preferred_element_type=F32)
        grad_hidden_norm, gg1, gb1 = norm_first_back(grad_normed_attn)
        grad_hidden = grad_middle + grad_hidden_norm
        chunks[layer] = jnp.concatenate(
            [
                jnp.transpose(g_in.astype(BF).reshape(4, 3, 192, D), (1, 0, 2, 3)),
                g_out.astype(BF).reshape(1, 4, 192, D),
                jnp.transpose(g_up.astype(BF).reshape(4, 4, 192, D), (1, 0, 2, 3)),
                g_down.astype(BF).reshape(4, 4, 192, D),
            ]
        )
        small_grads[layer] = jnp.concatenate(
            [jnp.stack([gg1, gg2])[:, None], jnp.stack([gb1, gb2])[:, None], g_maps], axis=1
        )
    small_grads = jnp.stack(small_grads).reshape(-1, 4, 192)
    small_rows = jnp.transpose(small_grads, (1, 0, 2)).reshape(1, 4, -1, D).astype(BF)
    small_count = small_rows.shape[2]
    small_rows = jnp.pad(small_rows, ((0, 0), (0, 0), (0, 192 - small_count), (0, 0)))
    everything = jnp.concatenate(chunks[::-1] + [small_rows])
    everything = jnp.swapaxes(everything.reshape(-1, 2, 2, 192, D), 1, 2)
    total = reduce_grads(n, everything)
    big = total[:-1].reshape(layer_count, 12, 192, D)[::-1]
    small_total = total[-1, :small_count].reshape(layer_count, 2, 66, 192)
    grad_in = jnp.swapaxes(big[:, :3].reshape(layer_count, 576, D), 1, 2)
    grad_out = jnp.swapaxes(big[:, 3], 1, 2)
    grad_up = big[:, 4:8].reshape(layer_count, D, D)
    grad_down = jnp.transpose(big[:, 8:], (0, 1, 3, 2)).reshape(layer_count, 3072, 192)
    return (
        block_output,
        grad_hidden.astype(BF),
        grad_in,
        grad_out,
        grad_up,
        grad_down,
        small_total[:, :, 0],
        small_total[:, :, 1],
        small_total[:, :, 2:],
        small_total[:, 1, 1],
    )


def solution(mesh):
    in_specs = (
        P("batch", "seq", None),
        P("batch", "seq", None),
        P("batch", None),
        P(None, None, "batch"),
        P(None, None, "batch"),
        P(None, None, "batch"),
        P(None, None, "batch"),
        P(None, None, "batch"),
        P(None, None, "batch"),
        P(None, None, None, "batch"),
    )
    out_specs = (
        P("batch", "seq", None),
        P("batch", "seq", None),
        P(None, None, "batch"),
        P(None, None, "batch"),
        P(None, None, "batch"),
        P(None, None, "batch"),
        P(None, None, "batch"),
        P(None, None, "batch"),
        P(None, None, None, "batch"),
        P(None, "batch"),
    )
    return jax.shard_map(shards, mesh=mesh, in_specs=in_specs, out_specs=out_specs, check_vma=False)
```

```python
import functools

import jax
import jax.numpy as jnp
from jax import lax
from jax.experimental import pallas as pl
from jax.experimental.pallas import tpu as pltpu
from jax.sharding import PartitionSpec as P

D = 768
H = 12
HD = 64
EPSILON = 1e-05
GELU = 0.7978845608028654
STATE_ROWS = 896
F32 = jnp.float32
BF = jnp.bfloat16
MESH = pl.DeviceIdType.MESH


def greet(peers):
    bar = pltpu.get_barrier_semaphore()
    for p in peers:
        pl.semaphore_signal(bar, inc=1, device_id=p, device_id_type=MESH)
    pl.semaphore_wait(bar, len(peers))

def remote(src, dst, ss, rs, dev):
    return pltpu.make_async_remote_copy(src_ref=src, dst_ref=dst, send_sem=ss, recv_sem=rs, device_id=dev, device_id_type=MESH)

def arrive(ref, sem):
    pltpu.make_async_copy(ref, ref, sem).wait()

def offsets(c, b):
    if c < 3:
        return b * 576 + c * 192
    if c < 4:
        return 2304 + b * 192
    if c < 8:
        return 3072 + b * 768 + (c - 4) * 192
    return 6144 + (c - 8) * 768 + b * 192


def small_kernel(s_ref, t_ref, sem, here_sem):
    s = lax.axis_index("seq")
    b = lax.axis_index("batch")
    others = [(s, (b + k) % 4) for k in range(1, 4)]
    greet(others)
    copies = [remote(s_ref, t_ref.at[b], sem.at[0, k], sem.at[1, 2 - k], dev) for k, dev in enumerate(others)]
    for copy in copies:
        copy.start()
    t_ref[b] = s_ref[...]
    for copy in copies:
        copy.wait()


def gather_small(small):
    return pl.pallas_call(
        small_kernel,
        name="gather_small",
        out_shape=jax.ShapeDtypeStruct((4,) + small.shape, BF),
        in_specs=[pl.BlockSpec(memory_space=pltpu.VMEM)],
        out_specs=pl.BlockSpec(memory_space=pltpu.VMEM),
        scratch_shapes=[pltpu.SemaphoreType.DMA((2, 3)), pltpu.SemaphoreType.DMA((1,))],
        compiler_params=pltpu.CompilerParams(collective_id=2, has_side_effects=True),
    )(small)


def nn(a, b):
    return lax.dot_general(a, b, (((1,), (0,)), ((), ())), preferred_element_type=F32)


def nt(a, b):
    return lax.dot_general(a, b, (((1,), (1,)), ((), ())), preferred_element_type=F32)


def normalize(v):
    centred = v - jnp.mean(v, axis=-1, keepdims=True)
    return centred * lax.rsqrt(jnp.mean(centred * centred, axis=-1, keepdims=True) + EPSILON)


def span(i, k):
    return pl.ds(pl.multiple_of(i * k, k), k)


def owners(n):
    group = max(16, STATE_ROWS // n)
    return group, STATE_ROWS // group


def parts_of(v):
    high = v.astype(BF)
    return high, (v - high.astype(F32)).astype(BF)


class Exchange:
    def __init__(self, n, seq, batch, state, taken, sums, got, sem):
        self.n, self.seq, self.batch = n, seq, batch
        self.state, self.taken, self.sums, self.got, self.sem = state, taken, sums, got, sem
        self.group, self.count = owners(n)

    def outgoing(self, d):
        peer = (self.seq + d) % self.n
        return peer, remote(
            self.state.at[:, span(peer % self.count, self.group)], self.taken.at[self.seq],
            self.sem.at[0], self.sem.at[1], (peer, self.batch),
        )

    def returning(self, d):
        peer = (self.seq + d) % self.n
        return remote(
            self.sums.at[peer], self.got.at[:, span(self.seq % self.count, self.group)],
            self.sem.at[2], self.sem.at[3], (peer, self.batch),
        )

    def owned(self, fn):
        if self.count == self.n:
            fn()
        else:
            pl.when(self.seq < self.count)(fn)

    def send(self):
        for d in range(1, self.n):
            peer, copy = self.outgoing(d)
            if self.count == self.n:
                copy.start()
            else:
                pl.when(peer < self.count)(copy.start)

        def keep():
            self.taken[self.seq] = self.state[:, span(self.seq % self.count, self.group)]

        self.owned(keep)

    def turn(self, coef):
        def work():
            arrive(self.taken.at[pl.ds(0, self.n - 1)], self.sem.at[1])

            def one(p, carry):
                for r in range(2):
                    def add(k, total):
                        return total + coef[(r * self.n + p) * self.n + k] * self.taken[k, r].astype(F32)

                    zero = jnp.zeros((self.group, 128), F32)
                    if self.n <= 8:
                        total = zero
                        for k in range(self.n):
                            total = add(k, total)
                    else:
                        total = lax.fori_loop(0, self.n, add, zero)
                    self.sums[p, r] = total.astype(BF)
                return carry

            lax.fori_loop(0, self.n, one, 0)
            for d in range(1, self.n):
                self.returning(d).start()
            self.got[:, span(self.seq % self.count, self.group)] = self.sums[self.seq]

        self.owned(work)

    def receive(self):
        if self.count == self.n:
            arrive(self.got.at[:, pl.ds(0, self.group * (self.n - 1))], self.sem.at[3])
        else:
            @pl.when(self.seq < self.count)
            def _():
                arrive(self.got.at[:, pl.ds(0, self.group * (self.count - 1))], self.sem.at[3])

            @pl.when(self.seq >= self.count)
            def _():
                arrive(self.got.at[:, pl.ds(0, self.group * self.count)], self.sem.at[3])

    def finish(self):
        if self.count == self.n:
            arrive(self.state.at[:, pl.ds(0, self.group * (self.n - 1))], self.sem.at[0])
            arrive(self.sums.at[pl.ds(0, self.n - 1)], self.sem.at[2])
        else:
            @pl.when(self.seq < self.count)
            def _():
                arrive(self.state.at[:, pl.ds(0, self.group * (self.count - 1))], self.sem.at[0])
                arrive(self.sums.at[pl.ds(0, self.n - 1)], self.sem.at[2])

            @pl.when(self.seq >= self.count)
            def _():
                arrive(self.state.at[:, pl.ds(0, self.group * self.count)], self.sem.at[0])


def forward_kernel(
    n, tok, w_ref, norms, maps, mask, chain, last, coef,
    o_w, o_h, o_mid, o_na, o_nm, o_qkv, o_phi, o_att, o_rz, o_act, o_dg, o_got, o_lo, o_attl, o_out,
    w, h, mid, na, nm, qkv, phi, att, attl, rz, act, dg, got, proj, pq, num, zz, norm_sum, state, taken, sums, qlo, mu, means,
    lsem, ysem, xsem, own_sem, near_sem, far_sem, esem, msem, ssem,
):
    s = lax.axis_index("seq")
    b = lax.axis_index("batch")
    xl = s % 2
    core = b + 1 - 2 * (b % 2)
    far = (b + 2) % 4
    layers = 2
    core_dev, y_dev, x_dev = (s, core), (s, far), (s + 1 - 2 * xl, b)
    greet([core_dev, y_dev] + [((s + d) % n, b) for d in range(1, n)])

    def rows(c, who, part, size):
        return pl.ds(pl.multiple_of(offsets(c % 12, who) + part * 96, 32), size)

    def same(c, who, part, size, sem, dev):
        place = w.at[c // 12, rows(c, who, part, size)]
        return remote(place, place, sem.at[0, c], sem.at[1, c], dev)

    def here(c):
        return w_ref.at[c // 12, pl.ds((c % 12) * 192, 192)]

    def out_y(c):
        src = w_ref.at[c // 12, pl.ds(pl.multiple_of((c % 12) * 192 + xl * 96, 32), 96)]
        return remote(src, w.at[c // 12, rows(c, b, xl, 96)], ysem.at[0, c], ysem.at[1, c], y_dev)

    def out_core(c):
        return remote(here(c), w.at[c // 12, rows(c, b, 0, 192)], own_sem.at[0, c], own_sem.at[1, c], core_dev)

    def stay(c):
        return pltpu.make_async_copy(here(c), w.at[c // 12, rows(c, b, 0, 192)], lsem.at[c])

    out_x = lambda c: same(c, far, xl, 96, xsem, x_dev)
    near = lambda c: same(c, far, xl, 96, near_sem, core_dev)
    rest = lambda c: same(c, far, 1 - xl, 96, far_sem, core_dev)
    count = layers * 12
    for c in range(count):
        out_y(c).start()
        out_core(c).start()
        stay(c).start()

    place = [0]

    def pump(k=1):
        for _ in range(k):
            c = place[0]
            if c > count:
                return
            if c < count:
                out_y(c).wait_recv()
                out_x(c).start()
                near(c).start()
            if c >= 1:
                out_x(c - 1).wait_recv()
                rest(c - 1).start()
            place[0] += 1

    def need(lo, hi):
        while place[0] <= hi:
            pump()
        for c in range(lo, hi):
            stay(c).wait()
            for copy in (out_core(c), near(c), rest(c)):
                copy.wait_recv()

    def mean_copy(l, d):
        peer = (s + d) % n
        return remote(means.at[l, s], means.at[l, s], msem.at[l, 0], msem.at[l, 1], (peer, b))

    stores = []

    def store(src, dst, i):
        copy = pltpu.make_async_copy(src, dst, ssem.at[i])
        copy.start()
        stores.append(copy)
        return copy

    left = lax.broadcasted_iota(jnp.int32, (128, 128), 1) < 64
    lanes = lax.broadcasted_iota(jnp.int32, (128, 128), 1)
    rows_i = lax.broadcasted_iota(jnp.int32, (128, 128), 0)
    ones = jnp.ones((128, 128), BF)
    h[0] = tok[...].astype(F32)
    phi_store = act_store = dg_store = None
    for l in range(layers):
        base = l * 12
        na[l] = (normalize(h[l]) * norms[l, 0, 0:1] + norms[l, 0, 1:2]).astype(BF)
        own = [jnp.mean(na[l, r * 128 : (r + 1) * 128].astype(F32), axis=0, keepdims=True) for r in range(2)]
        means[l, s] = jnp.concatenate(own + [jnp.zeros((6, D), F32)], axis=0)
        for d in range(1, n):
            mean_copy(l, d).start()
        need(base, base + 3)
        for t in range(9):
            piece = nt(na[l], w[l, t * 256 : (t + 1) * 256])
            if t < 6:
                proj[:, t * 256 : (t + 1) * 256] = piece
            else:
                if t == 6:
                    arrive(means.at[l, pl.ds(0, n - 1)], msem.at[l, 1])
                    mean = lax.fori_loop(0, n, lambda k, v: v + means[l, k], jnp.zeros((8, D), F32)) / n
                    mean = jnp.concatenate([mean, mean], axis=0).astype(BF)
                shift = nt(mean, w[l, t * 256 : (t + 1) * 256])[:8]
                mu[:, (t - 6) * 256 : (t - 5) * 256] = shift
                piece = jnp.concatenate([piece[:128] - shift[:1], piece[128:] - shift[1:2]], axis=0)
            qkv[l, :, t * 256 : (t + 1) * 256] = piece.astype(BF)
            if t == 4:
                pump()
        if phi_store is not None:
            phi_store.wait()
            stores[:] = [c for c in stores if c is not phi_store]
        norm_sum[...] = jnp.zeros_like(norm_sum)

        def value(hp, r):
            return jnp.concatenate([qkv[l, pl.ds(r * 128, 128), pl.ds(pl.multiple_of(1536 + hp * 128, 128), 128)], ones], axis=1)

        def features(hp, carry):
            for which in range(2):
                x = proj[:, pl.ds(pl.multiple_of(which * 768 + hp * 128, 128), 128)]
                high = x.astype(BF)
                low = (x - high.astype(F32)).astype(BF)
                qlo[l, :, pl.ds(pl.multiple_of(which * 768 + hp * 128, 128), 128)] = low
                m = maps[l, which, hp]
                logits = nt(m, high) + nt(m, low)
                for half in range(2):
                    t = logits[64 * half : 64 * half + 64]
                    up = jnp.exp(t - jnp.max(t, axis=0, keepdims=True))
                    down = jnp.exp(jnp.min(t, axis=0, keepdims=True) - t)
                    at = pl.multiple_of(hp * 256 + half * 128, 128)
                    phi[which, pl.ds(at, 64)] = (up * (1.0 / jnp.sum(up, axis=0, keepdims=True))).astype(BF)
                    phi[which, pl.ds(at + 64, 64)] = (down * (1.0 / jnp.sum(down, axis=0, keepdims=True))).astype(BF)
            for r in range(2):
                v = value(hp, r)
                got_ = []
                for half in range(2):
                    key = phi[1, pl.ds(pl.multiple_of(hp * 256 + half * 128, 128), 128), r * 128 : (r + 1) * 128]
                    both = nn((key.astype(F32) * last[r]).astype(BF), v)
                    got_.append(both[:, :128])
                    norm_sum[r] += jnp.where(lanes % 64 == hp * 2 + half, both[:, 128:], 0.0)
                state[l, r, span(hp, 128)] = jnp.where(left, got_[0], got_[1]).astype(BF)
            return carry

        lax.fori_loop(0, 6, features, 0)
        for r in range(2):
            state[l, r, 768:896] = norm_sum[r].astype(BF)
        swap = Exchange(n, s, b, state.at[l], taken.at[l], sums.at[l], got.at[l], esem.at[l])
        swap.send()
        phi_store = store(phi, o_phi.at[l], l * 16 + 0)
        store(na.at[l], o_na.at[l], l * 16 + 1)
        store(qlo.at[l], o_lo.at[l], l * 16 + 13)
        store(qkv.at[l], o_qkv.at[l], l * 16 + 2)
        store(h.at[l], o_h.at[l], l * 16 + 3)
        pump()

        def scores(hp, carry):
            for r in range(2):
                v = value(hp, r)
                both = []
                for half in range(2):
                    at = pl.ds(pl.multiple_of(hp * 256 + half * 128, 128), 128)
                    query = phi[0, at, r * 128 : (r + 1) * 128].astype(F32).T.astype(BF)
                    pq[r * 128 : (r + 1) * 128, at] = query
                    key = phi[1, at, r * 128 : (r + 1) * 128]
                    both.append(nn((nn(query, key) * mask[r]).astype(BF), v))
                at = span(hp, 128)
                num[r * 128 : (r + 1) * 128, at] = jnp.where(left, both[0][:, :128], both[1][:, :128])
                zz[r * 128 : (r + 1) * 128, at] = jnp.where(left, both[0][:, 128:], both[1][:, 128:])
            return carry

        lax.fori_loop(0, 3, scores, 0)
        swap.turn(coef)
        lax.fori_loop(3, 6, scores, 0)
        pump()
        swap.receive()

        def finish(hp, carry):
            at = span(hp, 128)
            for r in range(2):
                both = []
                for half in range(2):
                    query = pq[r * 128 : (r + 1) * 128, pl.ds(pl.multiple_of(hp * 256 + half * 128, 128), 128)]
                    pick = (rows_i == hp * 2 + half).astype(BF)
                    column = nn(got[l, r, 768:896], pick).astype(BF)
                    both.append(nn(query, jnp.concatenate([got[l, r, at], column], axis=1)))
                c = chain[r]
                z = zz[r * 128 : (r + 1) * 128, at] + c * jnp.where(left, both[0][:, 128:], both[1][:, 128:])
                top = num[r * 128 : (r + 1) * 128, at] + c * jnp.where(left, both[0][:, :128], both[1][:, :128])
                inverse = 1.0 / z
                out = top * inverse
                rz[l, r * 128 : (r + 1) * 128, at] = inverse
                att[l, r * 128 : (r + 1) * 128, at] = out
                attl[l, r * 128 : (r + 1) * 128, at] = (out + mu[r : r + 1, at]).astype(BF)
            return carry

        lax.fori_loop(0, 6, finish, 0)
        store(got.at[l], o_got.at[l], l * 16 + 4)
        store(rz.at[l], o_rz.at[l], l * 16 + 5)
        store(att.at[l], o_att.at[l], l * 16 + 6)
        store(attl.at[l], o_attl.at[l], l * 16 + 7)
        need(base + 3, base + 4)
        for t in range(3):
            at = slice(t * 256, (t + 1) * 256)
            mid[l, :, at] = h[l, :, at] + nt(attl[l], w[l, 2304 + t * 256 : 2304 + (t + 1) * 256])
        nm[l] = (normalize(mid[l]) * norms[l, 1, 0:1] + norms[l, 1, 1:2]).astype(BF)
        store(mid.at[l], o_mid.at[l], l * 16 + 8)
        store(nm.at[l], o_nm.at[l], l * 16 + 9)
        need(base + 4, base + 8)
        if act_store is not None:
            for copy in (act_store, dg_store):
                copy.wait()
                stores[:] = [c for c in stores if c is not copy]
        for k in range(4):
            for t in range(3):
                at = slice(t * 256, (t + 1) * 256)
                u = nn(nm[l], w[l, 3072 + k * 768 : 3072 + (k + 1) * 768, at])
                square = u * u
                bend = jnp.tanh(GELU * u * (1.0 + 0.044715 * square))
                act[k, :, at] = (0.5 * u * (1.0 + bend)).astype(BF)
                slope = 0.5 * (1.0 + bend) + 0.5 * u * (1.0 - bend * bend) * GELU * (1.0 + 0.134145 * square)
                dg[k, :, at] = slope.astype(BF)
            pump()
        act_store = store(act, o_act.at[l], l * 16 + 10)
        dg_store = store(dg, o_dg.at[l], l * 16 + 11)
        for k in range(4):
            need(base + 8 + k, base + 9 + k)
            for t in range(3):
                at = slice(t * 256, (t + 1) * 256)
                first = 6144 + k * 768 + t * 256
                y = nt(act[k], w[l, first : first + 256])
                before = mid[l, :, at] if k == 0 else h[l + 1, :, at]
                h[l + 1, :, at] = before + y
        store(w.at[l], o_w.at[l], l * 16 + 12)
    o_out[...] = h[layers].astype(BF)
    for copy in stores:
        copy.wait()
    for l in range(layers):
        arrive(means.at[l, pl.ds(0, n - 1)], msem.at[l, 0])
        Exchange(n, s, b, state.at[l], taken.at[l], sums.at[l], got.at[l], esem.at[l]).finish()
    for c in range(count):
        for copy in (out_y(c), out_x(c), out_core(c), near(c), rest(c)):
            copy.wait_send()


def forward(n, tok, w, norms, maps, mask, chain, last, coef):
    group, _ = owners(n)
    m = tok.shape[0]
    hbm = lambda shape, kind: jax.ShapeDtypeStruct(shape, kind)
    outs = (
        hbm((2, 9216, D), BF), hbm((2, m, D), F32), hbm((2, m, D), F32), hbm((2, m, D), BF), hbm((2, m, D), BF),
        hbm((2, m, 2304), BF), hbm((2, 2, 1536, m), BF), hbm((2, m, D), F32), hbm((2, m, D), F32),
        hbm((2, 4, m, D), BF), hbm((2, 4, m, D), BF), hbm((2, 2, STATE_ROWS, 128), BF), hbm((2, m, 1536), BF), hbm((2, m, D), BF), hbm((m, D), BF),
    )
    vmem = pl.BlockSpec(memory_space=pltpu.VMEM)
    anywhere = pl.BlockSpec(memory_space=pl.ANY)
    pair = lambda: pltpu.SemaphoreType.DMA((2, 24))
    V = lambda kind, *shape: pltpu.VMEM(shape, kind)
    return pl.pallas_call(
        functools.partial(forward_kernel, n),
        name="forward",
        out_shape=outs,
        in_specs=[vmem, anywhere, vmem, vmem, vmem, vmem, vmem, pl.BlockSpec(memory_space=pltpu.SMEM)],
        out_specs=[anywhere] * 14 + [vmem],
        scratch_shapes=[
            V(BF, 2, 9216, D), V(F32, 3, m, D), V(F32, 2, m, D), V(BF, 2, m, D), V(BF, 2, m, D), V(BF, 2, m, 2304),
            V(BF, 2, 1536, m), V(F32, 2, m, D), V(BF, 2, m, D), V(F32, 2, m, D), V(BF, 4, m, D), V(BF, 4, m, D),
            V(BF, 2, 2, STATE_ROWS, 128), V(F32, m, 1536), V(BF, m, 1536), V(F32, m, D), V(F32, m, D), V(F32, 2, 128, 128),
            V(BF, 2, 2, STATE_ROWS, 128), V(BF, 2, n, 2, group, 128), V(BF, 2, n, 2, group, 128), V(BF, 2, m, 1536), V(F32, 8, D), V(F32, 2, n, 8, D),
            pltpu.SemaphoreType.DMA((24,)), pair(), pair(), pair(), pair(), pair(),
            pltpu.SemaphoreType.DMA((2, 4)), pltpu.SemaphoreType.DMA((2, 2)), pltpu.SemaphoreType.DMA((32,)),
        ],
        compiler_params=pltpu.CompilerParams(collective_id=0, has_side_effects=True, vmem_limit_bytes=63 * 2**20),
    )(tok, w, norms, maps, mask, chain, last, coef)


def norm_back(y, v, gain):
    centred = v - jnp.mean(v, axis=-1, keepdims=True)
    scale = lax.rsqrt(jnp.mean(centred * centred, axis=-1, keepdims=True) + EPSILON)
    n = centred * scale
    yg = y * gain
    back = scale * (yg - jnp.mean(yg, axis=-1, keepdims=True) - n * jnp.mean(yg * n, axis=-1, keepdims=True))
    return back, jnp.sum(n * y, axis=0, keepdims=True), jnp.sum(y, axis=0, keepdims=True)


def softmax_back(s, g):
    s = s.astype(F32)
    plus, minus = s[:64], s[64:]
    mean = lambda p, v: jnp.sum(p * v, axis=0, keepdims=True) / jnp.sum(p, axis=0, keepdims=True)
    up = plus * (g[:64] - mean(plus, g[:64]))
    down = minus * (g[64:] - mean(minus, g[64:]))
    return up - down


CHUNK = 192


def backward_kernel(
    n, count,
    cot, norms, maps, mask, chain, last, coef,
    i_w, i_h, i_mid, i_na, i_nm, i_qkv, i_phi, i_att, i_rz, i_act, i_dg, i_got, i_lo, i_attl,
    o_grad, o_tok,
    recv_c, recv_y, recv_x, recv_1, recv_2, recv_h, g, wbuf, actb, dgb, nm, mid, att, rz, qkv, phi, got, na, h, qlo, attl,
    gh, du, gatt, gphik, gvt, dqkvt, flip, dn, gm, gnorm, norm_sum, state, taken, sums, back,
    csem, ysem, xsem, z1sem, z2sem, hsem, a2sem, a1sem, bsem, osem, esem, wsem, asem, lsem,
):
    s = lax.axis_index("seq")
    b = lax.axis_index("batch")
    xl, z = s % 2, s // 2
    b0, b1 = z % 2, (z // 2) % 2
    par, yy = b % 2, b // 2
    levels = [v for v in range(2, 10) if (1 << v) < n // 2]
    core_dev, y_dev, x_dev = (s, b + 1 - 2 * par), (s, (b + 2) % 4), (s + 1 - 2 * xl, b)
    z1_dev, z2_dev = (s + 2 * (1 - 2 * b0), b), (s + 4 * (1 - 2 * b1), b)
    h_dev = lambda v: (s + (2 << v) * (1 - 2 * ((z // (1 << v)) % 2)), b)
    greet([core_dev, y_dev] + [((s + d) % n, b) for d in range(1, n)])

    quarter_rows = CHUNK // 4
    xc, xo = span(xl, 384), span(1 - xl, 384)
    half = span(b0, CHUNK // 2)
    quarter = pl.ds(pl.multiple_of(b0 * (CHUNK // 2) + b1 * quarter_rows, 16), quarter_rows)
    fin = recv_y
    cC = lambda c: remote(g.at[c % 2, 1 - par], recv_c.at[c], csem.at[0, c], csem.at[1, c], core_dev)
    cY = lambda c: remote(recv_c.at[c, 1 - yy], recv_y.at[c], ysem.at[0, c], ysem.at[1, c], y_dev)
    cX = lambda c: remote(recv_y.at[c, :, xo], recv_x.at[c], xsem.at[0, c], xsem.at[1, c], x_dev)
    cZ1 = lambda c: remote(recv_x.at[c, span(1 - b0, CHUNK // 2)], recv_1.at[c], z1sem.at[0, c], z1sem.at[1, c], z1_dev)
    cZ2 = lambda c: remote(recv_1.at[c, span(1 - b1, quarter_rows)], recv_2.at[c], z2sem.at[0, c], z2sem.at[1, c], z2_dev)
    cH = lambda c, i: remote(recv_h.at[c, len(levels)], recv_h.at[c, i], hsem.at[0, c, i], hsem.at[1, c, i], h_dev(levels[i]))
    cA2 = lambda c: remote(fin.at[c, quarter, xc], fin.at[c, quarter, xc], a2sem.at[0, c], a2sem.at[1, c], z2_dev)
    cA1 = lambda c: remote(fin.at[c, half, xc], fin.at[c, half, xc], a1sem.at[0, c], a1sem.at[1, c], z1_dev)
    cB = lambda c: remote(fin.at[c, :, xc], fin.at[c, :, xc], bsem.at[0, c], bsem.at[1, c], x_dev)
    cO = lambda c: pltpu.make_async_copy(fin.at[c], o_grad.at[c], osem.at[c])

    def add(a, b_):
        return (a.astype(F32) + b_.astype(F32)).astype(BF)

    def absorb(c):
        cC(c).wait_recv()
        recv_c[c] = add(recv_c[c], g[c % 2, par])

    def stage_y(c):
        cY(c).start()

    def stage_x(c):
        cY(c).wait_recv()
        recv_y[c, :, xo] = add(recv_y[c, :, xo], recv_c[c, yy, :, xo])
        cX(c).start()
        recv_y[c, :, xc] = add(recv_y[c, :, xc], recv_c[c, yy, :, xc])

    def stage_z1(c):
        cX(c).wait_recv()
        recv_x[c] = add(recv_x[c], recv_y[c, :, xc])
        cZ1(c).start()

    def stage_z2(c):
        cZ1(c).wait_recv()
        recv_1[c] = add(recv_1[c], recv_x[c, half])
        cZ2(c).start()

    def stage_a2(c):
        cZ2(c).wait_recv()
        cX(c).wait_send()
        t = add(recv_2[c], recv_1[c, span(b1, quarter_rows)])
        for i in range(len(levels)):
            recv_h[c, len(levels)] = t
            cH(c, i).start()
            cH(c, i).wait()
            t = add(t, recv_h[c, i])
        fin[c, quarter, xc] = t
        cA2(c).start()

    def stage_a1(c):
        cA2(c).wait_recv()
        cA1(c).start()

    def stage_b(c):
        cA1(c).wait_recv()
        cB(c).start()

    def stage_o(c):
        cB(c).wait_recv()
        cO(c).start()

    stages = [stage_y, stage_x, stage_z1, stage_z2, stage_a2, stage_a1, stage_b, stage_o]

    def step(t):
        for i, stage in enumerate(stages):
            c = t - i
            if isinstance(c, int):
                if 0 <= c < count:
                    stage(c)
            else:
                pl.when((c >= 0) & (c < count))(functools.partial(stage, c))

    slot = [0]

    def pump(k=1):
        for _ in range(k):
            step(slot[0])
            slot[0] += 1

    def produce(c, block):
        @pl.when(c >= 2)
        def _():
            cC(c - 2).wait_send()

        for k in range(4):
            g[c % 2, k % 2, k // 2] = block(k).astype(BF)
        cC(c).start()

    def produced(c):
        pl.when(c >= 0)(functools.partial(absorb, c))

    left = lax.broadcasted_iota(jnp.int32, (128, 128), 1) < 64
    lanes = lax.broadcasted_iota(jnp.int32, (128, 128), 1)
    parts = []
    for l in (1, 0):
        parts += [(l, 6144), (l, 7680), (l, 3072), (l, 4608), (l, 1536), (l, 0)]

    def fetch(i):
        if i < len(parts):
            l, first = parts[i]
            return pltpu.make_async_copy(i_w.at[l, pl.ds(first, 1536)], wbuf.at[i % 2], wsem.at[i % 2])
        return None

    def fetch_start(i):
        if i < len(parts):
            fetch(i).start()

    mlp_loads = lambda l: [
        pltpu.make_async_copy(src.at[l], dst, lsem.at[i]) for i, (src, dst) in enumerate(((i_nm, nm), (i_mid, mid)))
    ]
    att_loads = lambda l: [
        pltpu.make_async_copy(src.at[l], dst, lsem.at[i + 2])
        for i, (src, dst) in enumerate(
            ((i_att, att), (i_rz, rz), (i_qkv, qkv), (i_phi, phi), (i_got, got), (i_na, na), (i_h, h), (i_lo, qlo), (i_attl, attl))
        )
    ]
    act_load = lambda l, k: pltpu.make_async_copy(i_act.at[l, k], actb.at[k % 2], asem.at[0, k % 2])
    dg_load = lambda l, k: pltpu.make_async_copy(i_dg.at[l, k], dgb.at[k % 2], asem.at[1, k % 2])

    def start(copies):
        for copy in copies:
            copy.start()

    def wait(copies):
        for copy in copies:
            copy.wait()

    def transposed(src):
        for t in range(6):
            flip[t * 128 : (t + 1) * 128] = src(t).T.astype(BF)

    fetch_start(0)
    fetch_start(1)
    for k in range(2):
        act_load(1, k).start()
        dg_load(1, k).start()
    start(mlp_loads(1))
    start(att_loads(1))
    gh[...] = cot[...].astype(F32)
    for l in (1, 0):
        c0 = (1 - l) * 12
        w0 = (1 - l) * 6
        transposed(lambda t: gh[:, t * 128 : (t + 1) * 128])
        for k in range(4):
            if k % 2 == 0:
                fetch(w0 + k // 2).wait()
            act_load(l, k).wait()
            dg_load(l, k).wait()
            low = gh[...].astype(BF)
            for t in range(3):
                at = slice(t * 256, (t + 1) * 256)
                du[k, :, at] = (nn(low, wbuf[(k // 2) % 2, (k % 2) * 768 : (k % 2 + 1) * 768, at]) * dgb[k % 2, :, at].astype(F32)).astype(BF)
            produce(c0 + k, lambda q, k=k: nn(flip[q * 192 : (q + 1) * 192], actb[k % 2]))
            produced(c0 + k - 1)
            if k < 2:
                act_load(l, k + 2).start()
                dg_load(l, k + 2).start()
            if k % 2 == 1:
                fetch_start(w0 + 2 + k // 2)
            if k == 2 or (k > 0 and l == 0):
                pump()
        wait(mlp_loads(l))
        for k in range(4):
            if k % 2 == 0:
                fetch(w0 + 2 + k // 2).wait()
            for t in range(3):
                at = slice(t * 256, (t + 1) * 256)
                term = nt(du[k], wbuf[(k // 2) % 2, (k % 2) * 768 + t * 256 : (k % 2) * 768 + (t + 1) * 256])
                if k == 0:
                    dn[:, at] = term
                else:
                    dn[:, at] += term
            if k % 2 == 1:
                fetch_start(w0 + 4 + k // 2)
        transposed(lambda t: nm[:, t * 128 : (t + 1) * 128].astype(F32))

        def up_chunk(j, carry):
            produce(c0 + 4 + j, lambda q: nn(flip[span(j, 192)], du[q]))
            produced(c0 + 3 + j)
            return carry

        lax.fori_loop(0, 2, up_chunk, 0)
        pump()
        lax.fori_loop(2, 4, up_chunk, 0)
        pump()
        grad, gg, gb = norm_back(dn[...], mid[...], norms[l, 1, 0:1])
        gnorm[l * 4 + 2 : l * 4 + 3] = gg
        gnorm[l * 4 + 3 : l * 4 + 4] = gb
        gh[...] += grad
        if l == 1:
            start(mlp_loads(0))
            for k in range(2):
                act_load(0, k).start()
                dg_load(0, k).start()
        wait(att_loads(l))
        transposed(lambda t: gh[:, t * 128 : (t + 1) * 128])
        produce(c0 + 8, lambda q: nn(flip[q * 192 : (q + 1) * 192], attl[...]))
        produced(c0 + 7)
        fetch(w0 + 4).wait()
        low = gh[...].astype(BF)
        for t in range(3):
            at = slice(t * 256, (t + 1) * 256)
            gatt[:, at] = nn(low, wbuf[0, 768:1536, at]) * rz[:, at]
        norm_sum[...] = jnp.zeros_like(norm_sum)

        def attention(hp, carry):
            at = span(hp, 128)
            deltas = []
            for r in range(2):
                rr = slice(r * 128, (r + 1) * 128)
                gp = gatt[rr, at]
                gpb = gp.astype(BF)
                gpt = gp.T.astype(BF)
                gp = gpb.astype(F32)
                ga = gp * att[rr, at]
                v = qkv[rr, pl.ds(pl.multiple_of(1536 + hp * 128, 128), 128)]
                states, pair = [], []
                for k in range(2):
                    keep = left if k == 0 else jnp.logical_not(left)
                    ghalf = jnp.where(keep, gp, 0.0).astype(BF)
                    c = jnp.sum(jnp.where(keep, ga, 0.0), axis=1, keepdims=True)
                    c_high = c.astype(BF).astype(F32)
                    csel = jnp.where(lanes == hp * 2 + k, -c_high, jnp.where(lanes == hp * 2 + k + 64, c_high - c, 0.0)).astype(BF)
                    fat = pl.ds(pl.multiple_of(hp * 256 + k * 128, 128), 128)
                    phq, phk = phi[0, fat, rr], phi[1, fat, rr]
                    da, da_low = parts_of((nt(ghalf, v) - c) * mask[r])
                    a = (nn(phq.astype(F32).T.astype(BF), phk) * mask[r]).astype(BF)
                    far = nt(
                        jnp.concatenate([got[r, at], got[r, 768:896]], axis=1), jnp.concatenate([ghalf, csel], axis=1)
                    )
                    gq = nt(phk, da) + nt(phk, da_low) + chain[r] * far
                    gphik[fat, rr] = nn(phq, da) + nn(phq, da_low)
                    gvt[pl.ds(pl.multiple_of(hp * 128 + k * 64, 64), 64), rr] = nn(gpt, a)[k * 64 : (k + 1) * 64]
                    here = nn((phq.astype(F32) * chain[r]).astype(BF), jnp.concatenate([gpb, csel], axis=1))
                    states.append(here[:, :128])
                    norm_sum[r] += here[:, 128:]
                    pair.append(softmax_back(phq, gq))
                state[r, at] = jnp.where(left, states[0], states[1]).astype(BF)
                deltas.append(jnp.concatenate(pair, axis=0))
            delta, delta_low = parts_of(jnp.concatenate(deltas, axis=1))
            dqkvt[at] = nn(maps[l, 0, hp], delta).astype(BF)
            gm[l, 0, hp] = nn(delta, qkv[:, at]) + nn(delta_low, qkv[:, at]) + nn(delta, qlo[:, at])
            return carry

        lax.fori_loop(0, 3, attention, 0)
        pump()
        lax.fori_loop(3, 6, attention, 0)
        for r in range(2):
            state[r, 768:896] = norm_sum[r].astype(BF)
        swap = Exchange(n, s, b, state, taken, sums, back, esem.at[l])
        swap.send()
        produced(c0 + 8)
        pump()
        swap.turn(coef)
        pump()
        swap.receive()

        def keys(hp, carry):
            at = span(hp, 128)
            deltas = []
            for r in range(2):
                rr = slice(r * 128, (r + 1) * 128)
                v = qkv[rr, pl.ds(pl.multiple_of(1536 + hp * 128, 128), 128)].astype(F32)
                turned = back[r, at].astype(F32).T.astype(BF)
                both = jnp.concatenate([back[r, at], back[r, 768:896]], axis=1)
                pair = []
                for k in range(2):
                    keep = left if k == 0 else jnp.logical_not(left)
                    vhalf = jnp.where(keep, v, 0.0).astype(BF)
                    pick = (lanes % 64 == hp * 2 + k).astype(BF)
                    fat = pl.ds(pl.multiple_of(hp * 256 + k * 128, 128), 128)
                    phk = phi[1, fat, rr]
                    gk = gphik[fat, rr] + last[r] * nt(both, jnp.concatenate([vhalf, pick], axis=1))
                    more = last[r] * nn(turned, phk)[k * 64 : (k + 1) * 64]
                    hat = pl.multiple_of(hp * 128 + k * 64, 64)
                    dqkvt[pl.ds(1536 + hat, 64), rr] = (gvt[pl.ds(hat, 64), rr] + more).astype(BF)
                    pair.append(softmax_back(phk, gk))
                deltas.append(jnp.concatenate(pair, axis=0))
            delta, delta_low = parts_of(jnp.concatenate(deltas, axis=1))
            key_at = pl.ds(pl.multiple_of(768 + hp * 128, 128), 128)
            dqkvt[key_at] = nn(maps[l, 1, hp], delta).astype(BF)
            gm[l, 1, hp] = nn(delta, qkv[:, key_at]) + nn(delta_low, qkv[:, key_at]) + nn(delta, qlo[:, key_at])
            return carry

        lax.fori_loop(0, 6, keys, 0)
        swap.finish()
        pump()

        def in_chunk(j, carry):
            produce(c0 + 9 + j, lambda q: nn(dqkvt[pl.ds(pl.multiple_of(q * 576 + j * 192, 64), 192)], na[...]))

            @pl.when(j > 0)
            def _():
                absorb(c0 + 8 + j)

            return carry

        lax.fori_loop(0, 3, in_chunk, 0)
        fetch(w0 + 5).wait()
        for t in range(9):
            piece = jnp.concatenate(
                [dqkvt[t * 256 : t * 256 + 128].astype(F32).T, dqkvt[t * 256 + 128 : t * 256 + 256].astype(F32).T], axis=1
            ).astype(BF)
            place = wbuf[1, t * 256 : (t + 1) * 256] if t < 6 else wbuf[0, (t - 6) * 256 : (t - 5) * 256]
            term = nn(piece, place)
            if t == 0:
                dn[...] = term
            else:
                dn[...] += term
        fetch_start(w0 + 6)
        fetch_start(w0 + 7)
        grad, gg, gb = norm_back(dn[...], h[...], norms[l, 0, 0:1])
        gnorm[l * 4 : l * 4 + 1] = gg
        gnorm[l * 4 + 1 : l * 4 + 2] = gb
        gh[...] += grad
        if l == 1:
            start(att_loads(0))
        pump()
    o_tok[...] = gh[...].astype(BF)
    c = count - 1
    cC(c - 2).wait_send()
    for k in range(4):
        into = g.at[c % 2, k % 2, k // 2]
        into[...] = jnp.zeros((CHUNK, D), BF)
        into[128:144] = jnp.concatenate([gnorm[...], jnp.zeros((8, D), F32)], axis=0).astype(BF)
        for l in range(2):
            for which in range(2):
                tiles = [None, None]
                for head in range(3 * k, 3 * k + 3):
                    side = head % 2
                    block = gm[l, which, head // 2][side * 64 : (side + 1) * 64]
                    block = jnp.where(left[:64] if side == 0 else jnp.logical_not(left[:64]), block, 0.0)
                    tile = (head % 3) // 2
                    tiles[tile] = block if tiles[tile] is None else tiles[tile] + block
                for tile in range(2):
                    first = (which * 2 + tile) * 128
                    into[l * 64 : (l + 1) * 64, first : first + 128] = tiles[tile].astype(BF)
    cC(c).start()
    absorb(c - 1)
    absorb(c)

    def tail(t, carry):
        step(t)
        return carry

    lax.fori_loop(slot[0], count + len(stages) - 1, tail, 0)
    cC(count - 2).wait_send()
    cC(count - 1).wait_send()

    def drain(c, carry):
        for copy in (cY, cZ1, cZ2, cA2, cA1, cB):
            copy(c).wait_send()
        cO(c).wait()
        return carry

    lax.fori_loop(0, count, drain, 0)


def backward(n, cot, norms, maps, mask, chain, last, coef, saved):
    group, _ = owners(n)
    m = cot.shape[0]
    count = 25
    extra = len([v for v in range(2, 10) if (1 << v) < n // 2])
    vmem = pl.BlockSpec(memory_space=pltpu.VMEM)
    anywhere = pl.BlockSpec(memory_space=pl.ANY)
    pair = lambda: pltpu.SemaphoreType.DMA((2, count))
    V = lambda kind, *shape: pltpu.VMEM(shape, kind)
    return pl.pallas_call(
        functools.partial(backward_kernel, n, count),
        name="backward",
        out_shape=(jax.ShapeDtypeStruct((count, CHUNK, D), BF), jax.ShapeDtypeStruct((m, D), BF)),
        in_specs=[vmem] * 6 + [pl.BlockSpec(memory_space=pltpu.SMEM)] + [anywhere] * 14,
        out_specs=[anywhere, vmem],
        scratch_shapes=[
            V(BF, count, 2, CHUNK, D), V(BF, count, CHUNK, D), V(BF, count, CHUNK, 384), V(BF, count, CHUNK // 2, 384),
            V(BF, count, CHUNK // 4, 384), V(BF, count if extra else 1, extra + 1, CHUNK // 4, 384), V(BF, 2, 2, 2, CHUNK, D),
            V(BF, 2, 1536, D), V(BF, 2, m, D), V(BF, 2, m, D), V(BF, m, D), V(F32, m, D), V(F32, m, D), V(F32, m, D),
            V(BF, m, 2304), V(BF, 2, 1536, m), V(BF, 2, STATE_ROWS, 128), V(BF, m, D), V(F32, m, D), V(BF, m, 1536), V(BF, m, D),
            V(F32, m, D), V(BF, 4, m, D), V(F32, m, D), V(F32, 1536, m), V(F32, D, m), V(BF, 2304, m), V(BF, D, m), V(F32, m, D),
            V(F32, 2, 2, 6, 128, 128), V(F32, 8, D), V(F32, 2, 128, 128), V(BF, 2, STATE_ROWS, 128),
            V(BF, n, 2, group, 128), V(BF, n, 2, group, 128), V(BF, 2, STATE_ROWS, 128),
            pair(), pair(), pair(), pair(), pair(), pltpu.SemaphoreType.DMA((2, count, max(extra, 1))), pair(), pair(), pair(),
            pltpu.SemaphoreType.DMA((count,)), pltpu.SemaphoreType.DMA((2, 4)), pltpu.SemaphoreType.DMA((2,)),
            pltpu.SemaphoreType.DMA((2, 2)), pltpu.SemaphoreType.DMA((11,)),
        ],
        compiler_params=pltpu.CompilerParams(collective_id=1, has_side_effects=True, vmem_limit_bytes=63 * 2**20),
    )(cot, norms, maps, mask, chain, last, coef, *saved)


def prologue(lengths, attn_in, attn_out, mlp_in, mlp_out, norm_gains, norm_biases, feature_maps, tok_rows):
    layers = attn_in.shape[0]
    n = lax.axis_size("seq")
    me = lax.axis_index("seq")
    first = me * tok_rows
    starts = jnp.cumsum(lengths, axis=1) - lengths
    seg = lambda p: jnp.sum((starts[:, None, :] <= p[None, :, None]).astype(jnp.int32), axis=2) - 1
    ids = seg(first + jnp.arange(tok_rows, dtype=jnp.int32))
    firsts = jnp.arange(n, dtype=jnp.int32) * tok_rows
    before, final = seg(firsts - 1), seg(firsts + tok_rows - 1)
    prior = seg((first - 1)[None])
    chain = jnp.broadcast_to((ids == prior).astype(F32)[:, :, None], ids.shape + (128,))
    last = (ids == ids[:, -1:]).astype(F32)[:, None, :]
    lower = jnp.tril(jnp.ones((tok_rows, tok_rows), F32))
    mask = (ids[:, :, None] == ids[:, None, :]).astype(F32) * lower[None]
    order = jnp.arange(n)
    coef = ((final[:, None, :] == before[:, :, None]) & (order[None, :] < order[:, None])[None]).astype(F32)
    coef_back = jnp.swapaxes(coef, 1, 2)
    packed = jnp.concatenate(
        [
            jnp.swapaxes(attn_in, 1, 2),
            jnp.swapaxes(attn_out, 1, 2),
            mlp_in,
            jnp.transpose(mlp_out.reshape(layers, 4, 768, 192), (0, 1, 3, 2)).reshape(layers, 768, 768),
        ],
        axis=1,
    )
    small = jnp.concatenate([norm_gains[:, :, None], norm_biases[:, :, None], feature_maps], axis=2)
    small = jnp.pad(small.reshape(layers * 132, 192), ((0, (-layers * 132) % 16), (0, 64)))
    smalls = gather_small(small)[:, : layers * 132, :192].reshape(4, layers, 2, 66, 192)
    smalls = jnp.transpose(smalls, (1, 2, 3, 0, 4)).reshape(layers, 2, 66, 768)
    norms = smalls[:, :, :2].astype(F32)
    maps = jnp.transpose(smalls[:, :, 2:].reshape(layers, 2, 64, 6, 2, 64), (0, 1, 3, 4, 5, 2))
    maps = (maps[:, :, :, :, :, None, :] * jnp.eye(2, dtype=BF)[:, None, :, None]).reshape(layers, 2, 6, 128, 128)
    chain_row = (ids == prior).astype(F32)[:, None, :]
    return packed, norms, maps, jnp.swapaxes(maps, 3, 4), mask, chain, chain_row, last, coef.reshape(-1), coef_back.reshape(-1)


def shards(tokens, cotangent, lengths, attn_in, attn_out, mlp_in, mlp_out, norm_gains, norm_biases, feature_maps):
    tok_rows = tokens.shape[1]
    layers = attn_in.shape[0]
    n = lax.axis_size("seq")
    packed, norms, maps, maps_back, mask, chain, chain_row, last, coef, coef_back = prologue(
        lengths, attn_in, attn_out, mlp_in, mlp_out, norm_gains, norm_biases, feature_maps, tok_rows
    )
    *saved, block_output = forward(n, tokens.reshape(-1, D), packed, norms, maps, mask, chain, last, coef)
    total, grad_tokens = backward(
        n, cotangent.reshape(-1, D), norms, maps_back, mask, chain_row, last, coef_back, saved
    )
    big = total[:-1].reshape(layers, 12, CHUNK, D)[::-1]
    turn = lambda v: jnp.swapaxes(v, -1, -2).astype(F32)
    grad_in = turn(big[:, 9:].reshape(layers, 576, D))
    grad_out = turn(big[:, 8])
    grad_up = big[:, 4:8].reshape(layers, D, D).astype(F32)
    grad_down = turn(big[:, :4]).reshape(layers, 3072, 192)
    b = lax.axis_index("batch")
    norm_rows = lax.dynamic_slice(total[-1, 128:136], (0, b * 192), (8, 192)).astype(F32).reshape(layers, 2, 2, 192)
    tiles = total[-1, :128, :512].astype(F32).reshape(layers, 64, 2, 2, 2, 64)
    even = b % 2 == 0
    first = jnp.where(even, tiles[:, :, :, 0, 0], tiles[:, :, :, 0, 1])
    second = jnp.where(even, tiles[:, :, :, 0, 1], tiles[:, :, :, 0, 0])
    third = jnp.where(even, tiles[:, :, :, 1, 0], tiles[:, :, :, 1, 1])
    grad_maps = jnp.stack([first, second, third], axis=3)
    grad_maps = jnp.transpose(grad_maps, (0, 2, 4, 3, 1)).reshape(layers, 2, 64, 192)
    return (
        block_output.reshape(tokens.shape),
        grad_tokens.reshape(tokens.shape),
        grad_in,
        grad_out,
        grad_up,
        grad_down,
        norm_rows[:, :, 0],
        norm_rows[:, :, 1],
        grad_maps,
        norm_rows[:, 1, 1],
    )


def solution(mesh):
    in_specs = (
        P("batch", "seq", None),
        P("batch", "seq", None),
        P("batch", None),
        P(None, None, "batch"),
        P(None, None, "batch"),
        P(None, None, "batch"),
        P(None, None, "batch"),
        P(None, None, "batch"),
        P(None, None, "batch"),
        P(None, None, None, "batch"),
    )
    out_specs = (
        P("batch", "seq", None),
        P("batch", "seq", None),
        P(None, None, "batch"),
        P(None, None, "batch"),
        P(None, None, "batch"),
        P(None, None, "batch"),
        P(None, None, "batch"),
        P(None, None, "batch"),
        P(None, None, None, "batch"),
        P(None, "batch"),
    )
    return jax.shard_map(shards, mesh=mesh, in_specs=in_specs, out_specs=out_specs, check_vma=False)
```

```python
import functools

import jax
import jax.numpy as jnp
from jax import lax
from jax.experimental import pallas as pl
from jax.experimental.pallas import tpu as pltpu
from jax.sharding import PartitionSpec as P

D = 768
H = 12
HD = 64
EPSILON = 1e-05
GELU = 0.7978845608028654
STATE_ROWS = 896
F32 = jnp.float32
BF = jnp.bfloat16
MESH = pl.DeviceIdType.MESH


def greet(peers):
    bar = pltpu.get_barrier_semaphore()
    for p in peers:
        pl.semaphore_signal(bar, inc=1, device_id=p, device_id_type=MESH)
    pl.semaphore_wait(bar, len(peers))

def remote(src, dst, ss, rs, dev):
    return pltpu.make_async_remote_copy(src_ref=src, dst_ref=dst, send_sem=ss, recv_sem=rs, device_id=dev, device_id_type=MESH)

def arrive(ref, sem):
    pltpu.make_async_copy(ref, ref, sem).wait()

def offsets(c, b):
    if c < 3:
        return b * 576 + c * 192
    if c < 4:
        return 2304 + b * 192
    if c < 8:
        return 3072 + b * 768 + (c - 4) * 192
    return 6144 + (c - 8) * 768 + b * 192


def small_kernel(s_ref, t_ref, sem, here_sem):
    s = lax.axis_index("seq")
    b = lax.axis_index("batch")
    others = [(s, (b + k) % 4) for k in range(1, 4)]
    greet(others)
    copies = [remote(s_ref, t_ref.at[b], sem.at[0, k], sem.at[1, 2 - k], dev) for k, dev in enumerate(others)]
    for copy in copies:
        copy.start()
    t_ref[b] = s_ref[...]
    for copy in copies:
        copy.wait()


def gather_small(small):
    return pl.pallas_call(
        small_kernel,
        name="gather_small",
        out_shape=jax.ShapeDtypeStruct((4,) + small.shape, BF),
        in_specs=[pl.BlockSpec(memory_space=pltpu.VMEM)],
        out_specs=pl.BlockSpec(memory_space=pltpu.VMEM),
        scratch_shapes=[pltpu.SemaphoreType.DMA((2, 3)), pltpu.SemaphoreType.DMA((1,))],
        compiler_params=pltpu.CompilerParams(collective_id=2, has_side_effects=True),
    )(small)


def nn(a, b):
    return lax.dot_general(a, b, (((1,), (0,)), ((), ())), preferred_element_type=F32)


def nt(a, b):
    return lax.dot_general(a, b, (((1,), (1,)), ((), ())), preferred_element_type=F32)


def normalize(v):
    centred = v - jnp.mean(v, axis=-1, keepdims=True)
    return centred * lax.rsqrt(jnp.mean(centred * centred, axis=-1, keepdims=True) + EPSILON)


def span(i, k):
    return pl.ds(pl.multiple_of(i * k, k), k)


def owners(n):
    group = max(16, STATE_ROWS // n)
    return group, STATE_ROWS // group


def parts_of(v):
    high = v.astype(BF)
    return high, (v - high.astype(F32)).astype(BF)


class Exchange:
    def __init__(self, n, seq, batch, state, taken, sums, got, sem):
        self.n, self.seq, self.batch = n, seq, batch
        self.state, self.taken, self.sums, self.got, self.sem = state, taken, sums, got, sem
        self.group, self.count = owners(n)

    def outgoing(self, d):
        peer = (self.seq + d) % self.n
        return peer, remote(
            self.state.at[:, span(peer % self.count, self.group)], self.taken.at[self.seq],
            self.sem.at[0], self.sem.at[1], (peer, self.batch),
        )

    def returning(self, d):
        peer = (self.seq + d) % self.n
        return remote(
            self.sums.at[peer], self.got.at[:, span(self.seq % self.count, self.group)],
            self.sem.at[2], self.sem.at[3], (peer, self.batch),
        )

    def owned(self, fn):
        if self.count == self.n:
            fn()
        else:
            pl.when(self.seq < self.count)(fn)

    def send(self):
        for d in range(1, self.n):
            peer, copy = self.outgoing(d)
            if self.count == self.n:
                copy.start()
            else:
                pl.when(peer < self.count)(copy.start)

        def keep():
            self.taken[self.seq] = self.state[:, span(self.seq % self.count, self.group)]

        self.owned(keep)

    def turn(self, coef):
        def work():
            arrive(self.taken.at[pl.ds(0, self.n - 1)], self.sem.at[1])

            def one(p, carry):
                for r in range(2):
                    def add(k, total):
                        return total + coef[(r * self.n + p) * self.n + k] * self.taken[k, r].astype(F32)

                    zero = jnp.zeros((self.group, 128), F32)
                    if self.n <= 8:
                        total = zero
                        for k in range(self.n):
                            total = add(k, total)
                    else:
                        total = lax.fori_loop(0, self.n, add, zero)
                    self.sums[p, r] = total.astype(BF)
                return carry

            lax.fori_loop(0, self.n, one, 0)
            for d in range(1, self.n):
                self.returning(d).start()
            self.got[:, span(self.seq % self.count, self.group)] = self.sums[self.seq]

        self.owned(work)

    def receive(self):
        if self.count == self.n:
            arrive(self.got.at[:, pl.ds(0, self.group * (self.n - 1))], self.sem.at[3])
        else:
            @pl.when(self.seq < self.count)
            def _():
                arrive(self.got.at[:, pl.ds(0, self.group * (self.count - 1))], self.sem.at[3])

            @pl.when(self.seq >= self.count)
            def _():
                arrive(self.got.at[:, pl.ds(0, self.group * self.count)], self.sem.at[3])

    def finish(self):
        if self.count == self.n:
            arrive(self.state.at[:, pl.ds(0, self.group * (self.n - 1))], self.sem.at[0])
            arrive(self.sums.at[pl.ds(0, self.n - 1)], self.sem.at[2])
        else:
            @pl.when(self.seq < self.count)
            def _():
                arrive(self.state.at[:, pl.ds(0, self.group * (self.count - 1))], self.sem.at[0])
                arrive(self.sums.at[pl.ds(0, self.n - 1)], self.sem.at[2])

            @pl.when(self.seq >= self.count)
            def _():
                arrive(self.state.at[:, pl.ds(0, self.group * self.count)], self.sem.at[0])


def forward_kernel(
    n, tok, w_ref, norms, maps, mask, chain, last, coef,
    o_w, o_h, o_mid, o_na, o_nm, o_qkv, o_phi, o_att, o_rz, o_act, o_dg, o_got, o_lo, o_attl, o_out,
    w, h, mid, na, nm, qkv, phi, att, attl, rz, act, dg, got, proj, pq, num, zz, norm_sum, state, taken, sums, qlo, mu, means,
    lsem, ysem, xsem, own_sem, near_sem, far_sem, esem, msem, ssem,
):
    s = lax.axis_index("seq")
    b = lax.axis_index("batch")
    xl = s % 2
    core = b + 1 - 2 * (b % 2)
    far = (b + 2) % 4
    layers = 2
    core_dev, y_dev, x_dev = (s, core), (s, far), (s + 1 - 2 * xl, b)
    greet([core_dev, y_dev] + [((s + d) % n, b) for d in range(1, n)])

    def rows(c, who, part, size):
        return pl.ds(pl.multiple_of(offsets(c % 12, who) + part * 96, 32), size)

    def same(c, who, part, size, sem, dev):
        place = w.at[c // 12, rows(c, who, part, size)]
        return remote(place, place, sem.at[0, c], sem.at[1, c], dev)

    def here(c):
        return w_ref.at[c // 12, pl.ds((c % 12) * 192, 192)]

    def out_y(c):
        src = w_ref.at[c // 12, pl.ds(pl.multiple_of((c % 12) * 192 + xl * 96, 32), 96)]
        return remote(src, w.at[c // 12, rows(c, b, xl, 96)], ysem.at[0, c], ysem.at[1, c], y_dev)

    def out_core(c):
        return remote(here(c), w.at[c // 12, rows(c, b, 0, 192)], own_sem.at[0, c], own_sem.at[1, c], core_dev)

    def stay(c):
        return pltpu.make_async_copy(here(c), w.at[c // 12, rows(c, b, 0, 192)], lsem.at[c])

    out_x = lambda c: same(c, far, xl, 96, xsem, x_dev)
    near = lambda c: same(c, far, xl, 96, near_sem, core_dev)
    rest = lambda c: same(c, far, 1 - xl, 96, far_sem, core_dev)
    count = layers * 12
    for c in range(count):
        out_y(c).start()
        out_core(c).start()
        stay(c).start()

    place = [0]

    def pump(k=1):
        for _ in range(k):
            c = place[0]
            if c > count:
                return
            if c < count:
                out_y(c).wait_recv()
                out_x(c).start()
                near(c).start()
            if c >= 1:
                out_x(c - 1).wait_recv()
                rest(c - 1).start()
            place[0] += 1

    def need(lo, hi):
        while place[0] <= hi:
            pump()
        for c in range(lo, hi):
            stay(c).wait()
            for copy in (out_core(c), near(c), rest(c)):
                copy.wait_recv()

    def mean_copy(l, d):
        peer = (s + d) % n
        return remote(means.at[l, s], means.at[l, s], msem.at[l, 0], msem.at[l, 1], (peer, b))

    stores = []

    def store(src, dst, i):
        copy = pltpu.make_async_copy(src, dst, ssem.at[i])
        copy.start()
        stores.append(copy)
        return copy

    left = lax.broadcasted_iota(jnp.int32, (128, 128), 1) < 64
    lanes = lax.broadcasted_iota(jnp.int32, (128, 128), 1)
    rows_i = lax.broadcasted_iota(jnp.int32, (128, 128), 0)
    ones = jnp.ones((128, 128), BF)
    h[0] = tok[...].astype(F32)
    phi_store = act_store = dg_store = None
    for l in range(layers):
        base = l * 12
        na[l] = (normalize(h[l]) * norms[l, 0, 0:1] + norms[l, 0, 1:2]).astype(BF)
        own = [jnp.mean(na[l, r * 128 : (r + 1) * 128].astype(F32), axis=0, keepdims=True) for r in range(2)]
        means[l, s] = jnp.concatenate(own + [jnp.zeros((6, D), F32)], axis=0)
        for d in range(1, n):
            mean_copy(l, d).start()
        need(base, base + 3)
        for t in range(9):
            piece = nt(na[l], w[l, t * 256 : (t + 1) * 256])
            if t < 6:
                proj[:, t * 256 : (t + 1) * 256] = piece
            else:
                if t == 6:
                    arrive(means.at[l, pl.ds(0, n - 1)], msem.at[l, 1])
                    mean = lax.fori_loop(0, n, lambda k, v: v + means[l, k], jnp.zeros((8, D), F32)) / n
                    mean = jnp.concatenate([mean, mean], axis=0).astype(BF)
                shift = nt(mean, w[l, t * 256 : (t + 1) * 256])[:8]
                mu[:, (t - 6) * 256 : (t - 5) * 256] = shift
                piece = jnp.concatenate([piece[:128] - shift[:1], piece[128:] - shift[1:2]], axis=0)
            qkv[l, :, t * 256 : (t + 1) * 256] = piece.astype(BF)
            if t == 4:
                pump()
        if phi_store is not None:
            phi_store.wait()
            stores[:] = [c for c in stores if c is not phi_store]
        norm_sum[...] = jnp.zeros_like(norm_sum)

        def value(hp, r):
            return jnp.concatenate([qkv[l, pl.ds(r * 128, 128), pl.ds(pl.multiple_of(1536 + hp * 128, 128), 128)], ones], axis=1)

        def features(hp, carry):
            for which in range(2):
                x = proj[:, pl.ds(pl.multiple_of(which * 768 + hp * 128, 128), 128)]
                high = x.astype(BF)
                low = (x - high.astype(F32)).astype(BF)
                qlo[l, :, pl.ds(pl.multiple_of(which * 768 + hp * 128, 128), 128)] = low
                m = maps[l, which, hp]
                logits = nt(m, high) + nt(m, low)
                for half in range(2):
                    t = logits[64 * half : 64 * half + 64]
                    up = jnp.exp(t - jnp.max(t, axis=0, keepdims=True))
                    down = jnp.exp(jnp.min(t, axis=0, keepdims=True) - t)
                    at = pl.multiple_of(hp * 256 + half * 128, 128)
                    phi[which, pl.ds(at, 64)] = (up * (1.0 / jnp.sum(up, axis=0, keepdims=True))).astype(BF)
                    phi[which, pl.ds(at + 64, 64)] = (down * (1.0 / jnp.sum(down, axis=0, keepdims=True))).astype(BF)
            for r in range(2):
                v = value(hp, r)
                got_ = []
                for half in range(2):
                    key = phi[1, pl.ds(pl.multiple_of(hp * 256 + half * 128, 128), 128), r * 128 : (r + 1) * 128]
                    both = nn((key.astype(F32) * last[r]).astype(BF), v)
                    got_.append(both[:, :128])
                    norm_sum[r] += jnp.where(lanes % 64 == hp * 2 + half, both[:, 128:], 0.0)
                state[l, r, span(hp, 128)] = jnp.where(left, got_[0], got_[1]).astype(BF)
            return carry

        for k in range(3):
            lax.fori_loop(2 * k, 2 * k + 2, features, 0)
            if k < 2:
                pump()
        for r in range(2):
            state[l, r, 768:896] = norm_sum[r].astype(BF)
        swap = Exchange(n, s, b, state.at[l], taken.at[l], sums.at[l], got.at[l], esem.at[l])
        swap.send()
        phi_store = store(phi, o_phi.at[l], l * 16 + 0)
        store(na.at[l], o_na.at[l], l * 16 + 1)
        store(qlo.at[l], o_lo.at[l], l * 16 + 13)
        store(qkv.at[l], o_qkv.at[l], l * 16 + 2)
        store(h.at[l], o_h.at[l], l * 16 + 3)
        pump()

        def scores(hp, carry):
            for r in range(2):
                v = value(hp, r)
                both = []
                for half in range(2):
                    at = pl.ds(pl.multiple_of(hp * 256 + half * 128, 128), 128)
                    query = phi[0, at, r * 128 : (r + 1) * 128].astype(F32).T.astype(BF)
                    pq[r * 128 : (r + 1) * 128, at] = query
                    key = phi[1, at, r * 128 : (r + 1) * 128]
                    both.append(nn((nn(query, key) * mask[r]).astype(BF), v))
                at = span(hp, 128)
                num[r * 128 : (r + 1) * 128, at] = jnp.where(left, both[0][:, :128], both[1][:, :128])
                zz[r * 128 : (r + 1) * 128, at] = jnp.where(left, both[0][:, 128:], both[1][:, 128:])
            return carry

        lax.fori_loop(0, 3, scores, 0)
        pump()
        swap.turn(coef)
        lax.fori_loop(3, 6, scores, 0)
        pump(2)
        swap.receive()

        def finish(hp, carry):
            at = span(hp, 128)
            for r in range(2):
                both = []
                for half in range(2):
                    query = pq[r * 128 : (r + 1) * 128, pl.ds(pl.multiple_of(hp * 256 + half * 128, 128), 128)]
                    pick = (rows_i == hp * 2 + half).astype(BF)
                    column = nn(got[l, r, 768:896], pick).astype(BF)
                    both.append(nn(query, jnp.concatenate([got[l, r, at], column], axis=1)))
                c = chain[r]
                z = zz[r * 128 : (r + 1) * 128, at] + c * jnp.where(left, both[0][:, 128:], both[1][:, 128:])
                top = num[r * 128 : (r + 1) * 128, at] + c * jnp.where(left, both[0][:, :128], both[1][:, :128])
                inverse = 1.0 / z
                out = top * inverse
                rz[l, r * 128 : (r + 1) * 128, at] = inverse
                att[l, r * 128 : (r + 1) * 128, at] = out
                attl[l, r * 128 : (r + 1) * 128, at] = (out + mu[r : r + 1, at]).astype(BF)
            return carry

        lax.fori_loop(0, 6, finish, 0)
        store(got.at[l], o_got.at[l], l * 16 + 4)
        store(rz.at[l], o_rz.at[l], l * 16 + 5)
        store(att.at[l], o_att.at[l], l * 16 + 6)
        store(attl.at[l], o_attl.at[l], l * 16 + 7)
        need(base + 3, base + 4)
        for t in range(3):
            at = slice(t * 256, (t + 1) * 256)
            mid[l, :, at] = h[l, :, at] + nt(attl[l], w[l, 2304 + t * 256 : 2304 + (t + 1) * 256])
        nm[l] = (normalize(mid[l]) * norms[l, 1, 0:1] + norms[l, 1, 1:2]).astype(BF)
        store(mid.at[l], o_mid.at[l], l * 16 + 8)
        store(nm.at[l], o_nm.at[l], l * 16 + 9)
        need(base + 4, base + 8)
        if act_store is not None:
            for copy in (act_store, dg_store):
                copy.wait()
                stores[:] = [c for c in stores if c is not copy]
        for k in range(4):
            for t in range(3):
                at = slice(t * 256, (t + 1) * 256)
                u = nn(nm[l], w[l, 3072 + k * 768 : 3072 + (k + 1) * 768, at])
                square = u * u
                bend = jnp.tanh(GELU * u * (1.0 + 0.044715 * square))
                act[k, :, at] = (0.5 * u * (1.0 + bend)).astype(BF)
                slope = 0.5 * (1.0 + bend) + 0.5 * u * (1.0 - bend * bend) * GELU * (1.0 + 0.134145 * square)
                dg[k, :, at] = slope.astype(BF)
            pump()
        act_store = store(act, o_act.at[l], l * 16 + 10)
        dg_store = store(dg, o_dg.at[l], l * 16 + 11)
        for k in range(4):
            need(base + 8 + k, base + 9 + k)
            for t in range(3):
                at = slice(t * 256, (t + 1) * 256)
                first = 6144 + k * 768 + t * 256
                y = nt(act[k], w[l, first : first + 256])
                before = mid[l, :, at] if k == 0 else h[l + 1, :, at]
                h[l + 1, :, at] = before + y
        store(w.at[l], o_w.at[l], l * 16 + 12)
    o_out[...] = h[layers].astype(BF)
    for copy in stores:
        copy.wait()
    for l in range(layers):
        arrive(means.at[l, pl.ds(0, n - 1)], msem.at[l, 0])
        Exchange(n, s, b, state.at[l], taken.at[l], sums.at[l], got.at[l], esem.at[l]).finish()
    for c in range(count):
        for copy in (out_y(c), out_x(c), out_core(c), near(c), rest(c)):
            copy.wait_send()


def forward(n, tok, w, norms, maps, mask, chain, last, coef):
    group, _ = owners(n)
    m = tok.shape[0]
    hbm = lambda shape, kind: jax.ShapeDtypeStruct(shape, kind)
    outs = (
        hbm((2, 9216, D), BF), hbm((2, m, D), F32), hbm((2, m, D), F32), hbm((2, m, D), BF), hbm((2, m, D), BF),
        hbm((2, m, 2304), BF), hbm((2, 2, 1536, m), BF), hbm((2, m, D), F32), hbm((2, m, D), F32),
        hbm((2, 4, m, D), BF), hbm((2, 4, m, D), BF), hbm((2, 2, STATE_ROWS, 128), BF), hbm((2, m, 1536), BF), hbm((2, m, D), BF), hbm((m, D), BF),
    )
    vmem = pl.BlockSpec(memory_space=pltpu.VMEM)
    anywhere = pl.BlockSpec(memory_space=pl.ANY)
    pair = lambda: pltpu.SemaphoreType.DMA((2, 24))
    V = lambda kind, *shape: pltpu.VMEM(shape, kind)
    return pl.pallas_call(
        functools.partial(forward_kernel, n),
        name="forward",
        out_shape=outs,
        in_specs=[vmem, anywhere, vmem, vmem, vmem, vmem, vmem, pl.BlockSpec(memory_space=pltpu.SMEM)],
        out_specs=[anywhere] * 14 + [vmem],
        scratch_shapes=[
            V(BF, 2, 9216, D), V(F32, 3, m, D), V(F32, 2, m, D), V(BF, 2, m, D), V(BF, 2, m, D), V(BF, 2, m, 2304),
            V(BF, 2, 1536, m), V(F32, 2, m, D), V(BF, 2, m, D), V(F32, 2, m, D), V(BF, 4, m, D), V(BF, 4, m, D),
            V(BF, 2, 2, STATE_ROWS, 128), V(F32, m, 1536), V(BF, m, 1536), V(F32, m, D), V(F32, m, D), V(F32, 2, 128, 128),
            V(BF, 2, 2, STATE_ROWS, 128), V(BF, 2, n, 2, group, 128), V(BF, 2, n, 2, group, 128), V(BF, 2, m, 1536), V(F32, 8, D), V(F32, 2, n, 8, D),
            pltpu.SemaphoreType.DMA((24,)), pair(), pair(), pair(), pair(), pair(),
            pltpu.SemaphoreType.DMA((2, 4)), pltpu.SemaphoreType.DMA((2, 2)), pltpu.SemaphoreType.DMA((32,)),
        ],
        compiler_params=pltpu.CompilerParams(collective_id=0, has_side_effects=True, vmem_limit_bytes=63 * 2**20),
    )(tok, w, norms, maps, mask, chain, last, coef)


def norm_back(y, v, gain):
    centred = v - jnp.mean(v, axis=-1, keepdims=True)
    scale = lax.rsqrt(jnp.mean(centred * centred, axis=-1, keepdims=True) + EPSILON)
    n = centred * scale
    yg = y * gain
    back = scale * (yg - jnp.mean(yg, axis=-1, keepdims=True) - n * jnp.mean(yg * n, axis=-1, keepdims=True))
    return back, jnp.sum(n * y, axis=0, keepdims=True), jnp.sum(y, axis=0, keepdims=True)


def softmax_back(s, g):
    s = s.astype(F32)
    plus, minus = s[:64], s[64:]
    mean = lambda p, v: jnp.sum(p * v, axis=0, keepdims=True) / jnp.sum(p, axis=0, keepdims=True)
    up = plus * (g[:64] - mean(plus, g[:64]))
    down = minus * (g[64:] - mean(minus, g[64:]))
    return up - down


CHUNK = 192
PLAN = {
    1: [0, 0, 0, 0, 0, 1, 0, 1, 2, 2, 0, 1, 0, 1],
    0: [0, 0, 0, 1, 0, 1, 0, 1, 3, 2, 0, 1, 0, 1],
}


def backward_kernel(
    n, count,
    cot, norms, maps, mask, chain, last, coef,
    i_w, i_h, i_mid, i_na, i_nm, i_qkv, i_phi, i_att, i_rz, i_act, i_dg, i_got, i_lo, i_attl,
    o_grad, o_tok,
    recv_c, recv_y, recv_x, recv_1, recv_2, recv_h, g, wbuf, actb, dgb, nm, mid, att, rz, qkv, phi, got, na, h, qlo, attl,
    gh, du, gatt, gphik, gvt, dqkvt, flip, dn, gm, gnorm, norm_sum, state, taken, sums, back,
    csem, ysem, xsem, z1sem, z2sem, hsem, a2sem, a1sem, bsem, osem, esem, wsem, asem, lsem,
):
    s = lax.axis_index("seq")
    b = lax.axis_index("batch")
    xl, z = s % 2, s // 2
    b0, b1 = z % 2, (z // 2) % 2
    par, yy = b % 2, b // 2
    levels = [v for v in range(2, 10) if (1 << v) < n // 2]
    core_dev, y_dev, x_dev = (s, b + 1 - 2 * par), (s, (b + 2) % 4), (s + 1 - 2 * xl, b)
    z1_dev, z2_dev = (s + 2 * (1 - 2 * b0), b), (s + 4 * (1 - 2 * b1), b)
    h_dev = lambda v: (s + (2 << v) * (1 - 2 * ((z // (1 << v)) % 2)), b)
    greet([core_dev, y_dev] + [((s + d) % n, b) for d in range(1, n)])

    quarter_rows = CHUNK // 4
    xc, xo = span(xl, 384), span(1 - xl, 384)
    half = span(b0, CHUNK // 2)
    quarter = pl.ds(pl.multiple_of(b0 * (CHUNK // 2) + b1 * quarter_rows, 16), quarter_rows)
    fin = recv_y
    cC = lambda c: remote(g.at[c % 2, 1 - par], recv_c.at[c], csem.at[0, c], csem.at[1, c], core_dev)
    cY = lambda c: remote(recv_c.at[c, 1 - yy], recv_y.at[c], ysem.at[0, c], ysem.at[1, c], y_dev)
    cX = lambda c: remote(recv_y.at[c, :, xo], recv_x.at[c], xsem.at[0, c], xsem.at[1, c], x_dev)
    cZ1 = lambda c: remote(recv_x.at[c, span(1 - b0, CHUNK // 2)], recv_1.at[c], z1sem.at[0, c], z1sem.at[1, c], z1_dev)
    cZ2 = lambda c: remote(recv_1.at[c, span(1 - b1, quarter_rows)], recv_2.at[c], z2sem.at[0, c], z2sem.at[1, c], z2_dev)
    cH = lambda c, i: remote(recv_h.at[c, len(levels)], recv_h.at[c, i], hsem.at[0, c, i], hsem.at[1, c, i], h_dev(levels[i]))
    cA2 = lambda c: remote(fin.at[c, quarter, xc], fin.at[c, quarter, xc], a2sem.at[0, c], a2sem.at[1, c], z2_dev)
    cA1 = lambda c: remote(fin.at[c, half, xc], fin.at[c, half, xc], a1sem.at[0, c], a1sem.at[1, c], z1_dev)
    cB = lambda c: remote(fin.at[c, :, xc], fin.at[c, :, xc], bsem.at[0, c], bsem.at[1, c], x_dev)
    cO = lambda c: pltpu.make_async_copy(fin.at[c], o_grad.at[c], osem.at[c])

    def add(a, b_):
        return (a.astype(F32) + b_.astype(F32)).astype(BF)

    def absorb(c):
        cC(c).wait_recv()
        recv_c[c, 1 - yy] = add(recv_c[c, 1 - yy], g[c % 2, par, 1 - yy])
        cY(c).start()
        recv_c[c, yy] = add(recv_c[c, yy], g[c % 2, par, yy])

    def stage_x(c):
        cY(c).wait_recv()
        recv_y[c, :, xo] = add(recv_y[c, :, xo], recv_c[c, yy, :, xo])
        cX(c).start()
        recv_y[c, :, xc] = add(recv_y[c, :, xc], recv_c[c, yy, :, xc])

    def stage_z1(c):
        cX(c).wait()
        recv_x[c] = add(recv_x[c], recv_y[c, :, xc])
        cZ1(c).start()

    def stage_z2(c):
        cZ1(c).wait_recv()
        recv_1[c] = add(recv_1[c], recv_x[c, half])
        cZ2(c).start()

    def stage_a2(c):
        cZ2(c).wait_recv()
        t = add(recv_2[c], recv_1[c, span(b1, quarter_rows)])
        for i in range(len(levels)):
            recv_h[c, len(levels)] = t
            cH(c, i).start()
            cH(c, i).wait()
            t = add(t, recv_h[c, i])
        fin[c, quarter, xc] = t
        cA2(c).start()

    def stage_a1(c):
        cA2(c).wait_recv()
        cA1(c).start()

    def stage_b(c):
        cA1(c).wait_recv()
        cB(c).start()

    def stage_o(c):
        cB(c).wait_recv()
        cO(c).start()

    stages = [stage_x, stage_z1, stage_z2, stage_a2, stage_a1, stage_b, stage_o]

    def step(t):
        for i, stage in enumerate(stages):
            c = t - i
            if isinstance(c, int):
                if 0 <= c < count:
                    stage(c)
            else:
                pl.when((c >= 0) & (c < count))(functools.partial(stage, c))

    slot = [0]

    def pump(k=1):
        for _ in range(k):
            step(slot[0])
            slot[0] += 1

    def produce(c, block):
        @pl.when(c >= 2)
        def _():
            cC(c - 2).wait_send()

        for k in range(4):
            g[c % 2, k % 2, k // 2] = block(k).astype(BF)
        cC(c).start()

    def produced(c):
        pl.when(c >= 0)(functools.partial(absorb, c))

    left = lax.broadcasted_iota(jnp.int32, (128, 128), 1) < 64
    lanes = lax.broadcasted_iota(jnp.int32, (128, 128), 1)
    parts = []
    for l in (1, 0):
        parts += [(l, 6144), (l, 7680), (l, 3072), (l, 4608), (l, 1536), (l, 0)]

    def fetch(i):
        if i < len(parts):
            l, first = parts[i]
            return pltpu.make_async_copy(i_w.at[l, pl.ds(first, 1536)], wbuf.at[i % 2], wsem.at[i % 2])
        return None

    def fetch_start(i):
        if i < len(parts):
            fetch(i).start()

    mlp_loads = lambda l: [
        pltpu.make_async_copy(src.at[l], dst, lsem.at[i]) for i, (src, dst) in enumerate(((i_nm, nm), (i_mid, mid)))
    ]
    att_loads = lambda l: [
        pltpu.make_async_copy(src.at[l], dst, lsem.at[i + 2])
        for i, (src, dst) in enumerate(
            ((i_att, att), (i_rz, rz), (i_qkv, qkv), (i_phi, phi), (i_got, got), (i_na, na), (i_h, h), (i_lo, qlo), (i_attl, attl))
        )
    ]
    act_load = lambda l, k: pltpu.make_async_copy(i_act.at[l, k], actb.at[k % 2], asem.at[0, k % 2])
    dg_load = lambda l, k: pltpu.make_async_copy(i_dg.at[l, k], dgb.at[k % 2], asem.at[1, k % 2])

    def start(copies):
        for copy in copies:
            copy.start()

    def wait(copies):
        for copy in copies:
            copy.wait()

    def transposed(src):
        for t in range(6):
            flip[t * 128 : (t + 1) * 128] = src(t).T.astype(BF)

    fetch_start(0)
    fetch_start(1)
    for k in range(2):
        act_load(1, k).start()
        dg_load(1, k).start()
    start(mlp_loads(1))
    start(att_loads(1))
    gh[...] = cot[...].astype(F32)
    for l in (1, 0):
        c0 = (1 - l) * 12
        w0 = (1 - l) * 6
        plan = PLAN[l]
        transposed(lambda t: gh[:, t * 128 : (t + 1) * 128])
        for k in range(4):
            if k % 2 == 0:
                fetch(w0 + k // 2).wait()
            act_load(l, k).wait()
            dg_load(l, k).wait()
            low = gh[...].astype(BF)
            for t in range(3):
                at = slice(t * 256, (t + 1) * 256)
                du[k, :, at] = (nn(low, wbuf[(k // 2) % 2, (k % 2) * 768 : (k % 2 + 1) * 768, at]) * dgb[k % 2, :, at].astype(F32)).astype(BF)
            produce(c0 + k, lambda q, k=k: nn(flip[q * 192 : (q + 1) * 192], actb[k % 2]))
            produced(c0 + k - 1)
            if k < 2:
                act_load(l, k + 2).start()
                dg_load(l, k + 2).start()
            if k % 2 == 1:
                fetch_start(w0 + 2 + k // 2)
            pump(plan[k])
        wait(mlp_loads(l))
        for k in range(4):
            if k % 2 == 0:
                fetch(w0 + 2 + k // 2).wait()
            for t in range(3):
                at = slice(t * 256, (t + 1) * 256)
                term = nt(du[k], wbuf[(k // 2) % 2, (k % 2) * 768 + t * 256 : (k % 2) * 768 + (t + 1) * 256])
                if k == 0:
                    dn[:, at] = term
                else:
                    dn[:, at] += term
            if k % 2 == 1:
                fetch_start(w0 + 4 + k // 2)
        transposed(lambda t: nm[:, t * 128 : (t + 1) * 128].astype(F32))

        def up_chunk(j, carry):
            produce(c0 + 4 + j, lambda q: nn(flip[span(j, 192)], du[q]))
            produced(c0 + 3 + j)
            return carry

        pump(plan[4])
        lax.fori_loop(0, 4, up_chunk, 0)
        pump(plan[5])
        grad, gg, gb = norm_back(dn[...], mid[...], norms[l, 1, 0:1])
        gnorm[l * 4 + 2 : l * 4 + 3] = gg
        gnorm[l * 4 + 3 : l * 4 + 4] = gb
        gh[...] += grad
        if l == 1:
            start(mlp_loads(0))
            for k in range(2):
                act_load(0, k).start()
                dg_load(0, k).start()
        wait(att_loads(l))
        transposed(lambda t: gh[:, t * 128 : (t + 1) * 128])
        produce(c0 + 8, lambda q: nn(flip[q * 192 : (q + 1) * 192], attl[...]))
        produced(c0 + 7)
        fetch(w0 + 4).wait()
        low = gh[...].astype(BF)
        for t in range(3):
            at = slice(t * 256, (t + 1) * 256)
            gatt[:, at] = nn(low, wbuf[0, 768:1536, at]) * rz[:, at]
        norm_sum[...] = jnp.zeros_like(norm_sum)

        def attention(hp, carry):
            at = span(hp, 128)
            deltas = []
            for r in range(2):
                rr = slice(r * 128, (r + 1) * 128)
                gp = gatt[rr, at]
                gpb = gp.astype(BF)
                gpt = gp.T.astype(BF)
                gp = gpb.astype(F32)
                ga = gp * att[rr, at]
                v = qkv[rr, pl.ds(pl.multiple_of(1536 + hp * 128, 128), 128)]
                states, pair = [], []
                for k in range(2):
                    keep = left if k == 0 else jnp.logical_not(left)
                    ghalf = jnp.where(keep, gp, 0.0).astype(BF)
                    c = jnp.sum(jnp.where(keep, ga, 0.0), axis=1, keepdims=True)
                    c_high = c.astype(BF).astype(F32)
                    csel = jnp.where(lanes == hp * 2 + k, -c_high, jnp.where(lanes == hp * 2 + k + 64, c_high - c, 0.0)).astype(BF)
                    fat = pl.ds(pl.multiple_of(hp * 256 + k * 128, 128), 128)
                    phq, phk = phi[0, fat, rr], phi[1, fat, rr]
                    da, da_low = parts_of((nt(ghalf, v) - c) * mask[r])
                    a = (nn(phq.astype(F32).T.astype(BF), phk) * mask[r]).astype(BF)
                    far = nt(
                        jnp.concatenate([got[r, at], got[r, 768:896]], axis=1), jnp.concatenate([ghalf, csel], axis=1)
                    )
                    gq = nt(phk, da) + nt(phk, da_low) + chain[r] * far
                    gphik[fat, rr] = nn(phq, da) + nn(phq, da_low)
                    gvt[pl.ds(pl.multiple_of(hp * 128 + k * 64, 64), 64), rr] = nn(gpt, a)[k * 64 : (k + 1) * 64]
                    here = nn((phq.astype(F32) * chain[r]).astype(BF), jnp.concatenate([gpb, csel], axis=1))
                    states.append(here[:, :128])
                    norm_sum[r] += here[:, 128:]
                    pair.append(softmax_back(phq, gq))
                state[r, at] = jnp.where(left, states[0], states[1]).astype(BF)
                deltas.append(jnp.concatenate(pair, axis=0))
            delta, delta_low = parts_of(jnp.concatenate(deltas, axis=1))
            dqkvt[at] = nn(maps[l, 0, hp], delta).astype(BF)
            gm[l, 0, hp] = nn(delta, qkv[:, at]) + nn(delta_low, qkv[:, at]) + nn(delta, qlo[:, at])
            return carry

        for k in range(3):
            lax.fori_loop(2 * k, 2 * k + 2, attention, 0)
            if k < 2:
                pump(plan[6 + k])
        for r in range(2):
            state[r, 768:896] = norm_sum[r].astype(BF)
        swap = Exchange(n, s, b, state, taken, sums, back, esem.at[l])
        swap.send()
        produced(c0 + 8)
        pump(plan[8])
        swap.turn(coef)
        pump(plan[9])
        swap.receive()

        def keys(hp, carry):
            at = span(hp, 128)
            deltas = []
            for r in range(2):
                rr = slice(r * 128, (r + 1) * 128)
                v = qkv[rr, pl.ds(pl.multiple_of(1536 + hp * 128, 128), 128)].astype(F32)
                turned = back[r, at].astype(F32).T.astype(BF)
                both = jnp.concatenate([back[r, at], back[r, 768:896]], axis=1)
                pair = []
                for k in range(2):
                    keep = left if k == 0 else jnp.logical_not(left)
                    vhalf = jnp.where(keep, v, 0.0).astype(BF)
                    pick = (lanes % 64 == hp * 2 + k).astype(BF)
                    fat = pl.ds(pl.multiple_of(hp * 256 + k * 128, 128), 128)
                    phk = phi[1, fat, rr]
                    gk = gphik[fat, rr] + last[r] * nt(both, jnp.concatenate([vhalf, pick], axis=1))
                    more = last[r] * nn(turned, phk)[k * 64 : (k + 1) * 64]
                    hat = pl.multiple_of(hp * 128 + k * 64, 64)
                    dqkvt[pl.ds(1536 + hat, 64), rr] = (gvt[pl.ds(hat, 64), rr] + more).astype(BF)
                    pair.append(softmax_back(phk, gk))
                deltas.append(jnp.concatenate(pair, axis=0))
            delta, delta_low = parts_of(jnp.concatenate(deltas, axis=1))
            key_at = pl.ds(pl.multiple_of(768 + hp * 128, 128), 128)
            dqkvt[key_at] = nn(maps[l, 1, hp], delta).astype(BF)
            gm[l, 1, hp] = nn(delta, qkv[:, key_at]) + nn(delta_low, qkv[:, key_at]) + nn(delta, qlo[:, key_at])
            return carry

        for k in range(3):
            lax.fori_loop(2 * k, 2 * k + 2, keys, 0)
            if k < 2:
                pump(plan[10 + k])
        swap.finish()

        def in_chunk(j, carry):
            produce(c0 + 9 + j, lambda q: nn(dqkvt[pl.ds(pl.multiple_of(q * 576 + j * 192, 64), 192)], na[...]))

            @pl.when(j > 0)
            def _():
                absorb(c0 + 8 + j)

            return carry

        lax.fori_loop(0, 3, in_chunk, 0)
        pump(plan[12])
        fetch(w0 + 5).wait()
        for t in range(9):
            piece = jnp.concatenate(
                [dqkvt[t * 256 : t * 256 + 128].astype(F32).T, dqkvt[t * 256 + 128 : t * 256 + 256].astype(F32).T], axis=1
            ).astype(BF)
            place = wbuf[1, t * 256 : (t + 1) * 256] if t < 6 else wbuf[0, (t - 6) * 256 : (t - 5) * 256]
            term = nn(piece, place)
            if t == 0:
                dn[...] = term
            else:
                dn[...] += term
        fetch_start(w0 + 6)
        fetch_start(w0 + 7)
        grad, gg, gb = norm_back(dn[...], h[...], norms[l, 0, 0:1])
        gnorm[l * 4 : l * 4 + 1] = gg
        gnorm[l * 4 + 1 : l * 4 + 2] = gb
        gh[...] += grad
        if l == 1:
            start(att_loads(0))
        pump(plan[13])
        assert slot[0] <= c0 + 11
    o_tok[...] = gh[...].astype(BF)
    c = count - 1
    cC(c - 2).wait_send()
    for k in range(4):
        into = g.at[c % 2, k % 2, k // 2]
        into[...] = jnp.zeros((CHUNK, D), BF)
        into[128:144] = jnp.concatenate([gnorm[...], jnp.zeros((8, D), F32)], axis=0).astype(BF)
        for l in range(2):
            for which in range(2):
                tiles = [None, None]
                for head in range(3 * k, 3 * k + 3):
                    side = head % 2
                    block = gm[l, which, head // 2][side * 64 : (side + 1) * 64]
                    block = jnp.where(left[:64] if side == 0 else jnp.logical_not(left[:64]), block, 0.0)
                    tile = (head % 3) // 2
                    tiles[tile] = block if tiles[tile] is None else tiles[tile] + block
                for tile in range(2):
                    first = (which * 2 + tile) * 128
                    into[l * 64 : (l + 1) * 64, first : first + 128] = tiles[tile].astype(BF)
    cC(c).start()
    absorb(c - 1)
    absorb(c)

    def tail(t, carry):
        step(t)
        return carry

    lax.fori_loop(slot[0], count + len(stages) - 1, tail, 0)
    cC(count - 2).wait_send()
    cC(count - 1).wait_send()

    def drain(c, carry):
        for copy in (cY, cZ1, cZ2, cA2, cA1, cB):
            copy(c).wait_send()
        cO(c).wait()
        return carry

    lax.fori_loop(0, count, drain, 0)


def backward(n, cot, norms, maps, mask, chain, last, coef, saved):
    group, _ = owners(n)
    m = cot.shape[0]
    count = 25
    extra = len([v for v in range(2, 10) if (1 << v) < n // 2])
    vmem = pl.BlockSpec(memory_space=pltpu.VMEM)
    anywhere = pl.BlockSpec(memory_space=pl.ANY)
    pair = lambda: pltpu.SemaphoreType.DMA((2, count))
    V = lambda kind, *shape: pltpu.VMEM(shape, kind)
    return pl.pallas_call(
        functools.partial(backward_kernel, n, count),
        name="backward",
        out_shape=(jax.ShapeDtypeStruct((count, CHUNK, D), BF), jax.ShapeDtypeStruct((m, D), BF)),
        in_specs=[vmem] * 6 + [pl.BlockSpec(memory_space=pltpu.SMEM)] + [anywhere] * 14,
        out_specs=[anywhere, vmem],
        scratch_shapes=[
            V(BF, count, 2, CHUNK, D), V(BF, count, CHUNK, D), V(BF, count, CHUNK, 384), V(BF, count, CHUNK // 2, 384),
            V(BF, count, CHUNK // 4, 384), V(BF, count if extra else 1, extra + 1, CHUNK // 4, 384), V(BF, 2, 2, 2, CHUNK, D),
            V(BF, 2, 1536, D), V(BF, 2, m, D), V(BF, 2, m, D), V(BF, m, D), V(F32, m, D), V(F32, m, D), V(F32, m, D),
            V(BF, m, 2304), V(BF, 2, 1536, m), V(BF, 2, STATE_ROWS, 128), V(BF, m, D), V(F32, m, D), V(BF, m, 1536), V(BF, m, D),
            V(F32, m, D), V(BF, 4, m, D), V(F32, m, D), V(F32, 1536, m), V(F32, D, m), V(BF, 2304, m), V(BF, D, m), V(F32, m, D),
            V(F32, 2, 2, 6, 128, 128), V(F32, 8, D), V(F32, 2, 128, 128), V(BF, 2, STATE_ROWS, 128),
            V(BF, n, 2, group, 128), V(BF, n, 2, group, 128), V(BF, 2, STATE_ROWS, 128),
            pair(), pair(), pair(), pair(), pair(), pltpu.SemaphoreType.DMA((2, count, max(extra, 1))), pair(), pair(), pair(),
            pltpu.SemaphoreType.DMA((count,)), pltpu.SemaphoreType.DMA((2, 4)), pltpu.SemaphoreType.DMA((2,)),
            pltpu.SemaphoreType.DMA((2, 2)), pltpu.SemaphoreType.DMA((11,)),
        ],
        compiler_params=pltpu.CompilerParams(collective_id=1, has_side_effects=True, vmem_limit_bytes=63 * 2**20),
    )(cot, norms, maps, mask, chain, last, coef, *saved)


def finish_kernel(x_ref, down, up, out, inner):
    j = pl.program_id(1)

    @pl.when(j == 0)
    def _():
        for k in range(4):
            down[0, :, k * D : (k + 1) * D] = x_ref[k].astype(F32)

    @pl.when(j == 1)
    def _():
        for k in range(4):
            up[0, k * CHUNK : (k + 1) * CHUNK] = x_ref[k].astype(F32)

    @pl.when(j == 2)
    def _():
        out[0] = x_ref[0].astype(F32)
        for k in range(3):
            inner[0, k * CHUNK : (k + 1) * CHUNK] = x_ref[k + 1].astype(F32)


def finish(total, layers):
    shape = lambda *dims: jax.ShapeDtypeStruct((layers,) + dims, F32)
    whole = lambda *dims: pl.BlockSpec((1,) + dims, lambda l, j: (l, 0, 0))
    return pl.pallas_call(
        finish_kernel,
        name="finish",
        grid=(layers, 3),
        out_shape=(shape(CHUNK, 3072), shape(D, D), shape(CHUNK, D), shape(3 * CHUNK, D)),
        in_specs=[pl.BlockSpec((4, CHUNK, D), lambda l, j: ((layers - 1 - l) * 3 + j, 0, 0))],
        out_specs=[whole(CHUNK, 3072), whole(D, D), whole(CHUNK, D), whole(3 * CHUNK, D)],
        compiler_params=pltpu.CompilerParams(vmem_limit_bytes=40 * 2**20),
    )(total)


def prologue(lengths, attn_in, attn_out, mlp_in, mlp_out, norm_gains, norm_biases, feature_maps, tok_rows):
    layers = attn_in.shape[0]
    n = lax.axis_size("seq")
    me = lax.axis_index("seq")
    first = me * tok_rows
    starts = jnp.cumsum(lengths, axis=1) - lengths
    seg = lambda p: jnp.sum((starts[:, None, :] <= p[None, :, None]).astype(jnp.int32), axis=2) - 1
    ids = seg(first + jnp.arange(tok_rows, dtype=jnp.int32))
    firsts = jnp.arange(n, dtype=jnp.int32) * tok_rows
    before, final = seg(firsts - 1), seg(firsts + tok_rows - 1)
    prior = seg((first - 1)[None])
    chain = jnp.broadcast_to((ids == prior).astype(F32)[:, :, None], ids.shape + (128,))
    last = (ids == ids[:, -1:]).astype(F32)[:, None, :]
    lower = jnp.tril(jnp.ones((tok_rows, tok_rows), F32))
    mask = (ids[:, :, None] == ids[:, None, :]).astype(F32) * lower[None]
    order = jnp.arange(n)
    coef = ((final[:, None, :] == before[:, :, None]) & (order[None, :] < order[:, None])[None]).astype(F32)
    coef_back = jnp.swapaxes(coef, 1, 2)
    packed = jnp.concatenate(
        [
            jnp.swapaxes(attn_in, 1, 2),
            jnp.swapaxes(attn_out, 1, 2),
            mlp_in,
            jnp.transpose(mlp_out.reshape(layers, 4, 768, 192), (0, 1, 3, 2)).reshape(layers, 768, 768),
        ],
        axis=1,
    )
    small = jnp.concatenate([norm_gains[:, :, None], norm_biases[:, :, None], feature_maps], axis=2)
    small = jnp.pad(small.reshape(layers * 132, 192), ((0, (-layers * 132) % 16), (0, 64)))
    smalls = gather_small(small)[:, : layers * 132, :192].reshape(4, layers, 2, 66, 192)
    smalls = jnp.transpose(smalls, (1, 2, 3, 0, 4)).reshape(layers, 2, 66, 768)
    norms = smalls[:, :, :2].astype(F32)
    maps = jnp.transpose(smalls[:, :, 2:].reshape(layers, 2, 64, 6, 2, 64), (0, 1, 3, 4, 5, 2))
    maps = (maps[:, :, :, :, :, None, :] * jnp.eye(2, dtype=BF)[:, None, :, None]).reshape(layers, 2, 6, 128, 128)
    chain_row = (ids == prior).astype(F32)[:, None, :]
    return packed, norms, maps, jnp.swapaxes(maps, 3, 4), mask, chain, chain_row, last, coef.reshape(-1), coef_back.reshape(-1)


def shards(tokens, cotangent, lengths, attn_in, attn_out, mlp_in, mlp_out, norm_gains, norm_biases, feature_maps):
    tok_rows = tokens.shape[1]
    layers = attn_in.shape[0]
    n = lax.axis_size("seq")
    packed, norms, maps, maps_back, mask, chain, chain_row, last, coef, coef_back = prologue(
        lengths, attn_in, attn_out, mlp_in, mlp_out, norm_gains, norm_biases, feature_maps, tok_rows
    )
    *saved, block_output = forward(n, tokens.reshape(-1, D), packed, norms, maps, mask, chain, last, coef)
    total, grad_tokens = backward(
        n, cotangent.reshape(-1, D), norms, maps_back, mask, chain_row, last, coef_back, saved
    )
    grad_down, grad_up, grad_out, grad_in = finish(total, layers)
    grad_down, grad_out, grad_in = (jnp.swapaxes(v, 1, 2) for v in (grad_down, grad_out, grad_in))
    b = lax.axis_index("batch")
    norm_rows = lax.dynamic_slice(total[-1, 128:136], (0, b * 192), (8, 192)).astype(F32).reshape(layers, 2, 2, 192)
    tiles = total[-1, :128, :512].astype(F32).reshape(layers, 64, 2, 2, 2, 64)
    even = b % 2 == 0
    first = jnp.where(even, tiles[:, :, :, 0, 0], tiles[:, :, :, 0, 1])
    second = jnp.where(even, tiles[:, :, :, 0, 1], tiles[:, :, :, 0, 0])
    third = jnp.where(even, tiles[:, :, :, 1, 0], tiles[:, :, :, 1, 1])
    grad_maps = jnp.stack([first, second, third], axis=3)
    grad_maps = jnp.transpose(grad_maps, (0, 2, 4, 3, 1)).reshape(layers, 2, 64, 192)
    return (
        block_output.reshape(tokens.shape),
        grad_tokens.reshape(tokens.shape),
        grad_in,
        grad_out,
        grad_up,
        grad_down,
        norm_rows[:, :, 0],
        norm_rows[:, :, 1],
        grad_maps,
        norm_rows[:, 1, 1],
    )


def solution(mesh):
    in_specs = (
        P("batch", "seq", None),
        P("batch", "seq", None),
        P("batch", None),
        P(None, None, "batch"),
        P(None, None, "batch"),
        P(None, None, "batch"),
        P(None, None, "batch"),
        P(None, None, "batch"),
        P(None, None, "batch"),
        P(None, None, None, "batch"),
    )
    out_specs = (
        P("batch", "seq", None),
        P("batch", "seq", None),
        P(None, None, "batch"),
        P(None, None, "batch"),
        P(None, None, "batch"),
        P(None, None, "batch"),
        P(None, None, "batch"),
        P(None, None, "batch"),
        P(None, None, None, "batch"),
        P(None, "batch"),
    )
    return jax.shard_map(shards, mesh=mesh, in_specs=in_specs, out_specs=out_specs, check_vma=False)
```

```python
import functools

import jax
import jax.numpy as jnp
from jax import lax
from jax.experimental import pallas as pl
from jax.experimental.pallas import tpu as pltpu
from jax.sharding import PartitionSpec as P

D = 768
H = 12
HD = 64
EPSILON = 1e-05
GELU = 0.7978845608028654
STATE_ROWS = 896
F32 = jnp.float32
BF = jnp.bfloat16
MESH = pl.DeviceIdType.MESH


def greet(peers):
    bar = pltpu.get_barrier_semaphore()
    for p in peers:
        pl.semaphore_signal(bar, inc=1, device_id=p, device_id_type=MESH)
    pl.semaphore_wait(bar, len(peers))

def remote(src, dst, ss, rs, dev):
    return pltpu.make_async_remote_copy(src_ref=src, dst_ref=dst, send_sem=ss, recv_sem=rs, device_id=dev, device_id_type=MESH)

def arrive(ref, sem):
    pltpu.make_async_copy(ref, ref, sem).wait()

def offsets(c, b):
    if c < 3:
        return b * 576 + c * 192
    if c < 4:
        return 2304 + b * 192
    if c < 8:
        return 3072 + b * 768 + (c - 4) * 192
    return 6144 + (c - 8) * 768 + b * 192


def small_kernel(s_ref, t_ref, sem):
    s = lax.axis_index("seq")
    b = lax.axis_index("batch")
    core, far = b + 1 - 2 * (b % 2), (b + 2) % 4
    greet([(s, core), (s, far)])

    def send(src, who, k, dev):
        return remote(src, t_ref.at[who], sem.at[0, k], sem.at[1, k], dev)

    first = [send(s_ref, b, 0, (s, far)), send(s_ref, b, 1, (s, core))]
    for copy in first:
        copy.start()
    t_ref[b] = s_ref[...]
    first[0].wait_recv()
    second = send(t_ref.at[far], far, 2, (s, core))
    second.start()
    first[0].wait_send()
    first[1].wait()
    second.wait()


def gather_small(small):
    return pl.pallas_call(
        small_kernel,
        name="gather_small",
        out_shape=jax.ShapeDtypeStruct((4,) + small.shape, BF),
        in_specs=[pl.BlockSpec(memory_space=pltpu.VMEM)],
        out_specs=pl.BlockSpec(memory_space=pltpu.VMEM),
        scratch_shapes=[pltpu.SemaphoreType.DMA((2, 3))],
        compiler_params=pltpu.CompilerParams(collective_id=2, has_side_effects=True),
    )(small)


def nn(a, b):
    return lax.dot_general(a, b, (((1,), (0,)), ((), ())), preferred_element_type=F32)


def nt(a, b):
    return lax.dot_general(a, b, (((1,), (1,)), ((), ())), preferred_element_type=F32)


def normalize(v):
    centred = v - jnp.mean(v, axis=-1, keepdims=True)
    return centred * lax.rsqrt(jnp.mean(centred * centred, axis=-1, keepdims=True) + EPSILON)


def span(i, k):
    return pl.ds(pl.multiple_of(i * k, k), k)


def owners(n):
    group = max(16, STATE_ROWS // n)
    return group, STATE_ROWS // group


def parts_of(v):
    high = v.astype(BF)
    return high, (v - high.astype(F32)).astype(BF)


class Exchange:
    def __init__(self, n, seq, batch, row, state, taken, sums, got, sem):
        self.n, self.seq, self.batch, self.row = n, seq, batch, row
        self.state, self.taken, self.sums, self.got, self.sem = state, taken, sums, got, sem
        self.group, self.count = owners(n)

    def outgoing(self, d):
        peer = (self.seq + d) % self.n
        return peer, remote(
            self.state.at[span(peer % self.count, self.group)], self.taken.at[self.seq],
            self.sem.at[0], self.sem.at[1], (peer, self.batch),
        )

    def returning(self, d):
        peer = (self.seq + d) % self.n
        return remote(
            self.sums.at[peer], self.got.at[span(self.seq % self.count, self.group)],
            self.sem.at[2], self.sem.at[3], (peer, self.batch),
        )

    def owned(self, fn):
        if self.count == self.n:
            fn()
        else:
            pl.when(self.seq < self.count)(fn)

    def send(self):
        for d in range(1, self.n):
            peer, copy = self.outgoing(d)
            if self.count == self.n:
                copy.start()
            else:
                pl.when(peer < self.count)(copy.start)

        def keep():
            self.taken[self.seq] = self.state[span(self.seq % self.count, self.group)]

        self.owned(keep)

    def turn(self, coef):
        def work():
            arrive(self.taken.at[pl.ds(0, self.n - 1)], self.sem.at[1])

            def one(p, carry):
                def add(k, total):
                    return total + coef[(self.row * self.n + p) * self.n + k] * self.taken[k].astype(F32)

                total = jnp.zeros((self.group, 128), F32)
                if self.n <= 8:
                    for k in range(self.n):
                        total = add(k, total)
                else:
                    total = lax.fori_loop(0, self.n, add, total)
                self.sums[p] = total.astype(BF)
                return carry

            lax.fori_loop(0, self.n, one, 0)
            for d in range(1, self.n):
                self.returning(d).start()
            self.got[span(self.seq % self.count, self.group)] = self.sums[self.seq]

        self.owned(work)

    def receive(self):
        if self.count == self.n:
            arrive(self.got.at[pl.ds(0, self.group * (self.n - 1))], self.sem.at[3])
        else:
            @pl.when(self.seq < self.count)
            def _():
                arrive(self.got.at[pl.ds(0, self.group * (self.count - 1))], self.sem.at[3])

            @pl.when(self.seq >= self.count)
            def _():
                arrive(self.got.at[pl.ds(0, self.group * self.count)], self.sem.at[3])

    def finish(self):
        if self.count == self.n:
            arrive(self.state.at[pl.ds(0, self.group * (self.n - 1))], self.sem.at[0])
            arrive(self.sums.at[pl.ds(0, self.n - 1)], self.sem.at[2])
        else:
            @pl.when(self.seq < self.count)
            def _():
                arrive(self.state.at[pl.ds(0, self.group * (self.count - 1))], self.sem.at[0])
                arrive(self.sums.at[pl.ds(0, self.n - 1)], self.sem.at[2])

            @pl.when(self.seq >= self.count)
            def _():
                arrive(self.state.at[pl.ds(0, self.group * self.count)], self.sem.at[0])


def forward_kernel(
    n, tok, w_ref, norms, maps, mask, chain, last, coef,
    o_w, o_h, o_mid, o_na, o_nm, o_qkv, o_phi, o_att, o_rz, o_act, o_dg, o_got, o_lo, o_attl, o_out,
    w, h, mid, na, nm, qkv, phi, att, attl, rz, act, dg, got, proj, pq, num, zz, norm_sum, state, taken, sums, qlo, mu, means,
    lsem, ysem, xsem, own_sem, near_sem, far_sem, esem, msem, ssem,
):
    s = lax.axis_index("seq")
    b = lax.axis_index("batch")
    xl = s % 2
    core = b + 1 - 2 * (b % 2)
    far = (b + 2) % 4
    layers = 2
    core_dev, y_dev, x_dev = (s, core), (s, far), (s + 1 - 2 * xl, b)
    greet([core_dev, y_dev] + [((s + d) % n, b) for d in range(1, n)])

    def rows(c, who, part, size):
        return pl.ds(pl.multiple_of(offsets(c % 12, who) + part * 96, 32), size)

    def same(c, who, part, size, sem, dev):
        place = w.at[c // 12, rows(c, who, part, size)]
        return remote(place, place, sem.at[0, c], sem.at[1, c], dev)

    def here(c):
        return w_ref.at[c // 12, pl.ds((c % 12) * 192, 192)]

    def out_y(c):
        src = w_ref.at[c // 12, pl.ds(pl.multiple_of((c % 12) * 192 + xl * 96, 32), 96)]
        return remote(src, w.at[c // 12, rows(c, b, xl, 96)], ysem.at[0, c], ysem.at[1, c], y_dev)

    def out_core(c):
        return remote(here(c), w.at[c // 12, rows(c, b, 0, 192)], own_sem.at[0, c], own_sem.at[1, c], core_dev)

    def stay(c):
        return pltpu.make_async_copy(here(c), w.at[c // 12, rows(c, b, 0, 192)], lsem.at[c])

    out_x = lambda c: same(c, far, xl, 96, xsem, x_dev)
    near = lambda c: same(c, far, xl, 96, near_sem, core_dev)
    rest = lambda c: same(c, far, 1 - xl, 96, far_sem, core_dev)
    count = layers * 12
    for c in range(count):
        out_y(c).start()
        out_core(c).start()
        stay(c).start()

    place = [0]

    def pump(k=1):
        for _ in range(k):
            c = place[0]
            if c > count:
                return
            if c < count:
                out_y(c).wait_recv()
                out_x(c).start()
                near(c).start()
            if c >= 1:
                out_x(c - 1).wait_recv()
                rest(c - 1).start()
            place[0] += 1

    def need(lo, hi):
        while place[0] <= hi:
            pump()
        for c in range(lo, hi):
            stay(c).wait()
            for copy in (out_core(c), near(c), rest(c)):
                copy.wait_recv()

    def exchange_of(l, r):
        return Exchange(n, s, b, r, state.at[l, r], taken.at[l, r], sums.at[l, r], got.at[l, r], esem.at[l, r])

    def mean_copy(l, d):
        peer = (s + d) % n
        return remote(means.at[l, s], means.at[l, s], msem.at[l, 0], msem.at[l, 1], (peer, b))

    stores = []

    def store(src, dst, i):
        copy = pltpu.make_async_copy(src, dst, ssem.at[i])
        copy.start()
        stores.append(copy)
        return copy

    def keep_weights(l, first, size, i):
        at = pl.ds(first, size)
        store(w.at[l, at], o_w.at[l, at], 32 + l * 8 + i)

    left = lax.broadcasted_iota(jnp.int32, (128, 128), 1) < 64
    lanes = lax.broadcasted_iota(jnp.int32, (128, 128), 1)
    rows_i = lax.broadcasted_iota(jnp.int32, (128, 128), 0)
    ones = jnp.ones((128, 128), BF)
    h[0] = tok[...].astype(F32)
    phi_store = act_store = dg_store = None
    for l in range(layers):
        base = l * 12
        na[l] = (normalize(h[l]) * norms[l, 0, 0:1] + norms[l, 0, 1:2]).astype(BF)
        own = [jnp.mean(na[l, r * 128 : (r + 1) * 128].astype(F32), axis=0, keepdims=True) for r in range(2)]
        means[l, s] = jnp.concatenate(own + [jnp.zeros((6, D), F32)], axis=0)
        for d in range(1, n):
            mean_copy(l, d).start()
        need(base, base + 3)
        for t in range(9):
            piece = nt(na[l], w[l, t * 256 : (t + 1) * 256])
            if t < 6:
                proj[:, t * 256 : (t + 1) * 256] = piece
            else:
                if t == 6:
                    arrive(means.at[l, pl.ds(0, n - 1)], msem.at[l, 1])
                    mean = lax.fori_loop(0, n, lambda k, v: v + means[l, k], jnp.zeros((8, D), F32)) / n
                    mean = jnp.concatenate([mean, mean], axis=0).astype(BF)
                shift = nt(mean, w[l, t * 256 : (t + 1) * 256])[:8]
                mu[:, (t - 6) * 256 : (t - 5) * 256] = shift
                piece = jnp.concatenate([piece[:128] - shift[:1], piece[128:] - shift[1:2]], axis=0)
            qkv[l, :, t * 256 : (t + 1) * 256] = piece.astype(BF)
            if t == 4:
                pump()
        if phi_store is not None:
            phi_store.wait()
            stores[:] = [c for c in stores if c is not phi_store]
        norm_sum[...] = jnp.zeros_like(norm_sum)

        def value(hp, r):
            return jnp.concatenate([qkv[l, pl.ds(r * 128, 128), pl.ds(pl.multiple_of(1536 + hp * 128, 128), 128)], ones], axis=1)

        def features(r, hp, carry):
            rr = slice(r * 128, (r + 1) * 128)
            for which in range(2):
                x = proj[rr, pl.ds(pl.multiple_of(which * 768 + hp * 128, 128), 128)]
                high = x.astype(BF)
                low = (x - high.astype(F32)).astype(BF)
                qlo[l, rr, pl.ds(pl.multiple_of(which * 768 + hp * 128, 128), 128)] = low
                m = maps[l, which, hp]
                logits = nt(m, high) + nt(m, low)
                for half in range(2):
                    t = logits[64 * half : 64 * half + 64]
                    up = jnp.exp(t - jnp.max(t, axis=0, keepdims=True))
                    down = jnp.exp(jnp.min(t, axis=0, keepdims=True) - t)
                    at = pl.multiple_of(hp * 256 + half * 128, 128)
                    phi[which, pl.ds(at, 64), rr] = (up * (1.0 / jnp.sum(up, axis=0, keepdims=True))).astype(BF)
                    phi[which, pl.ds(at + 64, 64), rr] = (down * (1.0 / jnp.sum(down, axis=0, keepdims=True))).astype(BF)
            v = value(hp, r)
            sums_ = []
            for half in range(2):
                key = phi[1, pl.ds(pl.multiple_of(hp * 256 + half * 128, 128), 128), rr]
                both = nn((key.astype(F32) * last[r]).astype(BF), v)
                sums_.append(both[:, :128])
                norm_sum[r] += jnp.where(lanes % 64 == hp * 2 + half, both[:, 128:], 0.0)
            state[l, r, span(hp, 128)] = jnp.where(left, sums_[0], sums_[1]).astype(BF)
            return carry

        swaps = [exchange_of(l, r) for r in range(2)]
        for r in range(2):
            for k in range(2):
                lax.fori_loop(3 * k, 3 * k + 3, functools.partial(features, r), 0)
                if k == 0:
                    pump()
            state[l, r, 768:896] = norm_sum[r].astype(BF)
            swaps[r].send()
        phi_store = store(phi, o_phi.at[l], l * 16 + 0)
        store(na.at[l], o_na.at[l], l * 16 + 1)
        store(qlo.at[l], o_lo.at[l], l * 16 + 13)
        store(qkv.at[l], o_qkv.at[l], l * 16 + 2)
        store(h.at[l], o_h.at[l], l * 16 + 3)
        pump()

        def scores(r, hp, carry):
            v = value(hp, r)
            both = []
            for half in range(2):
                at = pl.ds(pl.multiple_of(hp * 256 + half * 128, 128), 128)
                query = phi[0, at, r * 128 : (r + 1) * 128].astype(F32).T.astype(BF)
                pq[r * 128 : (r + 1) * 128, at] = query
                key = phi[1, at, r * 128 : (r + 1) * 128]
                both.append(nn((nn(query, key) * mask[r]).astype(BF), v))
            at = span(hp, 128)
            num[r * 128 : (r + 1) * 128, at] = jnp.where(left, both[0][:, :128], both[1][:, :128])
            zz[r * 128 : (r + 1) * 128, at] = jnp.where(left, both[0][:, 128:], both[1][:, 128:])
            return carry

        def finish_row(r, hp, carry):
            at = span(hp, 128)
            both = []
            for half in range(2):
                query = pq[r * 128 : (r + 1) * 128, pl.ds(pl.multiple_of(hp * 256 + half * 128, 128), 128)]
                pick = (rows_i == hp * 2 + half).astype(BF)
                column = nn(got[l, r, 768:896], pick).astype(BF)
                both.append(nn(query, jnp.concatenate([got[l, r, at], column], axis=1)))
            c = chain[r]
            z = zz[r * 128 : (r + 1) * 128, at] + c * jnp.where(left, both[0][:, 128:], both[1][:, 128:])
            top = num[r * 128 : (r + 1) * 128, at] + c * jnp.where(left, both[0][:, :128], both[1][:, :128])
            inverse = 1.0 / z
            out = top * inverse
            rz[l, r * 128 : (r + 1) * 128, at] = inverse
            att[l, r * 128 : (r + 1) * 128, at] = out
            attl[l, r * 128 : (r + 1) * 128, at] = (out + mu[r : r + 1, at]).astype(BF)
            return carry

        lax.fori_loop(0, 6, functools.partial(scores, 0), 0)
        swaps[0].turn(coef)
        pump()
        lax.fori_loop(0, 6, functools.partial(scores, 1), 0)
        swaps[1].turn(coef)
        pump(2)
        for r in range(2):
            swaps[r].receive()
            lax.fori_loop(0, 6, functools.partial(finish_row, r), 0)
        store(got.at[l], o_got.at[l], l * 16 + 4)
        store(rz.at[l], o_rz.at[l], l * 16 + 5)
        store(att.at[l], o_att.at[l], l * 16 + 6)
        store(attl.at[l], o_attl.at[l], l * 16 + 7)
        need(base + 3, base + 4)
        keep_weights(l, 0, 3072, 0)
        for t in range(3):
            at = slice(t * 256, (t + 1) * 256)
            mid[l, :, at] = h[l, :, at] + nt(attl[l], w[l, 2304 + t * 256 : 2304 + (t + 1) * 256])
        nm[l] = (normalize(mid[l]) * norms[l, 1, 0:1] + norms[l, 1, 1:2]).astype(BF)
        store(mid.at[l], o_mid.at[l], l * 16 + 8)
        store(nm.at[l], o_nm.at[l], l * 16 + 9)
        need(base + 4, base + 8)
        keep_weights(l, 3072, 3072, 1)
        if act_store is not None:
            for copy in (act_store, dg_store):
                copy.wait()
                stores[:] = [c for c in stores if c is not copy]
        for k in range(4):
            for t in range(3):
                at = slice(t * 256, (t + 1) * 256)
                u = nn(nm[l], w[l, 3072 + k * 768 : 3072 + (k + 1) * 768, at])
                square = u * u
                bend = jnp.tanh(GELU * u * (1.0 + 0.044715 * square))
                act[k, :, at] = (0.5 * u * (1.0 + bend)).astype(BF)
                slope = 0.5 * (1.0 + bend) + 0.5 * u * (1.0 - bend * bend) * GELU * (1.0 + 0.134145 * square)
                dg[k, :, at] = slope.astype(BF)
            pump()
        act_store = store(act, o_act.at[l], l * 16 + 10)
        dg_store = store(dg, o_dg.at[l], l * 16 + 11)
        for k in range(4):
            need(base + 8 + k, base + 9 + k)
            keep_weights(l, 6144 + k * 768, 768, 2 + k)
            for t in range(3):
                at = slice(t * 256, (t + 1) * 256)
                first = 6144 + k * 768 + t * 256
                y = nt(act[k], w[l, first : first + 256])
                before = mid[l, :, at] if k == 0 else h[l + 1, :, at]
                h[l + 1, :, at] = before + y
    o_out[...] = h[layers].astype(BF)
    for copy in stores:
        copy.wait()
    for l in range(layers):
        arrive(means.at[l, pl.ds(0, n - 1)], msem.at[l, 0])
        for r in range(2):
            exchange_of(l, r).finish()
    for c in range(count):
        for copy in (out_y(c), out_x(c), out_core(c), near(c), rest(c)):
            copy.wait_send()


def forward(n, tok, w, norms, maps, mask, chain, last, coef):
    group, _ = owners(n)
    m = tok.shape[0]
    hbm = lambda shape, kind: jax.ShapeDtypeStruct(shape, kind)
    outs = (
        hbm((2, 9216, D), BF), hbm((2, m, D), F32), hbm((2, m, D), F32), hbm((2, m, D), BF), hbm((2, m, D), BF),
        hbm((2, m, 2304), BF), hbm((2, 2, 1536, m), BF), hbm((2, m, D), F32), hbm((2, m, D), F32),
        hbm((2, 4, m, D), BF), hbm((2, 4, m, D), BF), hbm((2, 2, STATE_ROWS, 128), BF), hbm((2, m, 1536), BF), hbm((2, m, D), BF), hbm((m, D), BF),
    )
    vmem = pl.BlockSpec(memory_space=pltpu.VMEM)
    anywhere = pl.BlockSpec(memory_space=pl.ANY)
    pair = lambda: pltpu.SemaphoreType.DMA((2, 24))
    V = lambda kind, *shape: pltpu.VMEM(shape, kind)
    return pl.pallas_call(
        functools.partial(forward_kernel, n),
        name="forward",
        out_shape=outs,
        in_specs=[vmem, anywhere, vmem, vmem, vmem, vmem, vmem, pl.BlockSpec(memory_space=pltpu.SMEM)],
        out_specs=[anywhere] * 14 + [vmem],
        scratch_shapes=[
            V(BF, 2, 9216, D), V(F32, 3, m, D), V(F32, 2, m, D), V(BF, 2, m, D), V(BF, 2, m, D), V(BF, 2, m, 2304),
            V(BF, 2, 1536, m), V(F32, 2, m, D), V(BF, 2, m, D), V(F32, 2, m, D), V(BF, 4, m, D), V(BF, 4, m, D),
            V(BF, 2, 2, STATE_ROWS, 128), V(F32, m, 1536), V(BF, m, 1536), V(F32, m, D), V(F32, m, D), V(F32, 2, 128, 128),
            V(BF, 2, 2, STATE_ROWS, 128), V(BF, 2, 2, n, group, 128), V(BF, 2, 2, n, group, 128), V(BF, 2, m, 1536), V(F32, 8, D), V(F32, 2, n, 8, D),
            pltpu.SemaphoreType.DMA((24,)), pair(), pair(), pair(), pair(), pair(),
            pltpu.SemaphoreType.DMA((2, 2, 4)), pltpu.SemaphoreType.DMA((2, 2)), pltpu.SemaphoreType.DMA((48,)),
        ],
        compiler_params=pltpu.CompilerParams(collective_id=0, has_side_effects=True, vmem_limit_bytes=63 * 2**20),
    )(tok, w, norms, maps, mask, chain, last, coef)


def norm_back(y, v, gain):
    centred = v - jnp.mean(v, axis=-1, keepdims=True)
    scale = lax.rsqrt(jnp.mean(centred * centred, axis=-1, keepdims=True) + EPSILON)
    n = centred * scale
    yg = y * gain
    back = scale * (yg - jnp.mean(yg, axis=-1, keepdims=True) - n * jnp.mean(yg * n, axis=-1, keepdims=True))
    return back, jnp.sum(n * y, axis=0, keepdims=True), jnp.sum(y, axis=0, keepdims=True)


def softmax_back(s, g):
    s = s.astype(F32)
    plus, minus = s[:64], s[64:]
    mean = lambda p, v: jnp.sum(p * v, axis=0, keepdims=True) / jnp.sum(p, axis=0, keepdims=True)
    up = plus * (g[:64] - mean(plus, g[:64]))
    down = minus * (g[64:] - mean(minus, g[64:]))
    return up - down


CHUNK = 192
PLAN = {
    1: [0, 0, 0, 0, 0, 1, 0, 1, 2, 2, 0, 1, 0, 1],
    0: [0, 0, 0, 1, 0, 1, 0, 1, 3, 2, 0, 1, 0, 1],
}


def backward_kernel(
    n, count,
    cot, norms, maps, mask, chain, last, coef,
    i_w, i_h, i_mid, i_na, i_nm, i_qkv, i_phi, i_att, i_rz, i_act, i_dg, i_got, i_lo, i_attl,
    o_grad, o_tok,
    recv_c, recv_y, recv_x, recv_1, recv_2, recv_h, g, wbuf, actb, dgb, nm, mid, att, rz, qkv, phi, got, na, h, qlo, attl,
    gh, du, gatt, gphik, gvt, dqkvt, flip, dn, gm, gnorm, norm_sum, state, taken, sums, back,
    csem, ysem, xsem, z1sem, z2sem, hsem, a2sem, a1sem, bsem, osem, esem, wsem, asem, lsem,
):
    s = lax.axis_index("seq")
    b = lax.axis_index("batch")
    xl, z = s % 2, s // 2
    b0, b1 = z % 2, (z // 2) % 2
    par, yy = b % 2, b // 2
    levels = [v for v in range(2, 10) if (1 << v) < n // 2]
    core_dev, y_dev, x_dev = (s, b + 1 - 2 * par), (s, (b + 2) % 4), (s + 1 - 2 * xl, b)
    z1_dev, z2_dev = (s + 2 * (1 - 2 * b0), b), (s + 4 * (1 - 2 * b1), b)
    h_dev = lambda v: (s + (2 << v) * (1 - 2 * ((z // (1 << v)) % 2)), b)
    greet([core_dev, y_dev] + [((s + d) % n, b) for d in range(1, n)])

    quarter_rows = CHUNK // 4
    xc, xo = span(xl, 384), span(1 - xl, 384)
    half = span(b0, CHUNK // 2)
    quarter = pl.ds(pl.multiple_of(b0 * (CHUNK // 2) + b1 * quarter_rows, 16), quarter_rows)
    fin = recv_y
    cC = lambda c: remote(g.at[c % 2, 1 - par], recv_c.at[c], csem.at[0, c], csem.at[1, c], core_dev)
    cY = lambda c: remote(recv_c.at[c, 1 - yy], recv_y.at[c], ysem.at[0, c], ysem.at[1, c], y_dev)
    cX = lambda c: remote(recv_y.at[c, :, xo], recv_x.at[c], xsem.at[0, c], xsem.at[1, c], x_dev)
    cZ1 = lambda c: remote(recv_x.at[c, span(1 - b0, CHUNK // 2)], recv_1.at[c], z1sem.at[0, c], z1sem.at[1, c], z1_dev)
    cZ2 = lambda c: remote(recv_1.at[c, span(1 - b1, quarter_rows)], recv_2.at[c], z2sem.at[0, c], z2sem.at[1, c], z2_dev)
    cH = lambda c, i: remote(recv_h.at[c, len(levels)], recv_h.at[c, i], hsem.at[0, c, i], hsem.at[1, c, i], h_dev(levels[i]))
    cA2 = lambda c: remote(fin.at[c, quarter, xc], fin.at[c, quarter, xc], a2sem.at[0, c], a2sem.at[1, c], z2_dev)
    cA1 = lambda c: remote(fin.at[c, half, xc], fin.at[c, half, xc], a1sem.at[0, c], a1sem.at[1, c], z1_dev)
    cB = lambda c: remote(fin.at[c, :, xc], fin.at[c, :, xc], bsem.at[0, c], bsem.at[1, c], x_dev)
    cO = lambda c: pltpu.make_async_copy(fin.at[c], o_grad.at[c], osem.at[c])

    def add(a, b_):
        return (a.astype(F32) + b_.astype(F32)).astype(BF)

    def absorb(c):
        cC(c).wait_recv()
        recv_c[c, 1 - yy] = add(recv_c[c, 1 - yy], g[c % 2, par, 1 - yy])
        cY(c).start()
        recv_c[c, yy] = add(recv_c[c, yy], g[c % 2, par, yy])

    def stage_x(c):
        cY(c).wait_recv()
        recv_y[c, :, xo] = add(recv_y[c, :, xo], recv_c[c, yy, :, xo])
        cX(c).start()
        recv_y[c, :, xc] = add(recv_y[c, :, xc], recv_c[c, yy, :, xc])

    def stage_z1(c):
        cX(c).wait()
        recv_x[c] = add(recv_x[c], recv_y[c, :, xc])
        cZ1(c).start()

    def stage_z2(c):
        cZ1(c).wait_recv()
        recv_1[c] = add(recv_1[c], recv_x[c, half])
        cZ2(c).start()

    def stage_a2(c):
        cZ2(c).wait_recv()
        t = add(recv_2[c], recv_1[c, span(b1, quarter_rows)])
        for i in range(len(levels)):
            recv_h[c, len(levels)] = t
            cH(c, i).start()
            cH(c, i).wait()
            t = add(t, recv_h[c, i])
        fin[c, quarter, xc] = t
        cA2(c).start()

    def stage_a1(c):
        cA2(c).wait_recv()
        cA1(c).start()

    def stage_b(c):
        cA1(c).wait_recv()
        cB(c).start()

    def stage_o(c):
        cB(c).wait_recv()
        cO(c).start()

    stages = [stage_x, stage_z1, stage_z2, stage_a2, stage_a1, stage_b, stage_o]

    def step(t):
        for i, stage in enumerate(stages):
            c = t - i
            if isinstance(c, int):
                if 0 <= c < count:
                    stage(c)
            else:
                pl.when((c >= 0) & (c < count))(functools.partial(stage, c))

    slot = [0]

    def pump(k=1):
        for _ in range(k):
            step(slot[0])
            slot[0] += 1

    def produce(c, block):
        @pl.when(c >= 2)
        def _():
            cC(c - 2).wait_send()

        for k in range(4):
            g[c % 2, k % 2, k // 2] = block(k).astype(BF)
        cC(c).start()

    def produced(c):
        pl.when(c >= 0)(functools.partial(absorb, c))

    left = lax.broadcasted_iota(jnp.int32, (128, 128), 1) < 64
    lanes = lax.broadcasted_iota(jnp.int32, (128, 128), 1)
    parts = []
    for l in (1, 0):
        parts += [(l, 6144), (l, 7680), (l, 3072), (l, 4608), (l, 1536), (l, 0)]

    def fetch(i):
        if i < len(parts):
            l, first = parts[i]
            return pltpu.make_async_copy(i_w.at[l, pl.ds(first, 1536)], wbuf.at[i % 2], wsem.at[i % 2])
        return None

    def fetch_start(i):
        if i < len(parts):
            fetch(i).start()

    mlp_loads = lambda l: [
        pltpu.make_async_copy(src.at[l], dst, lsem.at[i]) for i, (src, dst) in enumerate(((i_nm, nm), (i_mid, mid)))
    ]
    att_loads = lambda l: [
        pltpu.make_async_copy(src.at[l], dst, lsem.at[i + 2])
        for i, (src, dst) in enumerate(
            ((i_att, att), (i_rz, rz), (i_qkv, qkv), (i_phi, phi), (i_got, got), (i_na, na), (i_h, h), (i_lo, qlo), (i_attl, attl))
        )
    ]
    act_load = lambda l, k: pltpu.make_async_copy(i_act.at[l, k], actb.at[k % 2], asem.at[0, k % 2])
    dg_load = lambda l, k: pltpu.make_async_copy(i_dg.at[l, k], dgb.at[k % 2], asem.at[1, k % 2])

    def start(copies):
        for copy in copies:
            copy.start()

    def wait(copies):
        for copy in copies:
            copy.wait()

    def transposed(src):
        for t in range(6):
            flip[t * 128 : (t + 1) * 128] = src(t).T.astype(BF)

    fetch_start(0)
    for k in range(2):
        act_load(1, k).start()
        dg_load(1, k).start()
    gh[...] = cot[...].astype(F32)
    for l in (1, 0):
        c0 = (1 - l) * 12
        w0 = (1 - l) * 6
        plan = PLAN[l]
        transposed(lambda t: gh[:, t * 128 : (t + 1) * 128])
        for k in range(4):
            if k % 2 == 0:
                fetch(w0 + k // 2).wait()
            if k == 0 and l == 1:
                fetch_start(1)
                start(mlp_loads(1))
                start(att_loads(1))
            act_load(l, k).wait()
            dg_load(l, k).wait()
            low = gh[...].astype(BF)
            for t in range(3):
                at = slice(t * 256, (t + 1) * 256)
                du[k, :, at] = (nn(low, wbuf[(k // 2) % 2, (k % 2) * 768 : (k % 2 + 1) * 768, at]) * dgb[k % 2, :, at].astype(F32)).astype(BF)
            produce(c0 + k, lambda q, k=k: nn(flip[q * 192 : (q + 1) * 192], actb[k % 2]))
            produced(c0 + k - 1)
            if k < 2:
                act_load(l, k + 2).start()
                dg_load(l, k + 2).start()
            if k % 2 == 1:
                fetch_start(w0 + 2 + k // 2)
            pump(plan[k])
        wait(mlp_loads(l))
        for k in range(4):
            if k % 2 == 0:
                fetch(w0 + 2 + k // 2).wait()
            for t in range(3):
                at = slice(t * 256, (t + 1) * 256)
                term = nt(du[k], wbuf[(k // 2) % 2, (k % 2) * 768 + t * 256 : (k % 2) * 768 + (t + 1) * 256])
                if k == 0:
                    dn[:, at] = term
                else:
                    dn[:, at] += term
            if k % 2 == 1:
                fetch_start(w0 + 4 + k // 2)
        transposed(lambda t: nm[:, t * 128 : (t + 1) * 128].astype(F32))

        def up_chunk(j, carry):
            produce(c0 + 4 + j, lambda q: nn(flip[span(j, 192)], du[q]))
            produced(c0 + 3 + j)
            return carry

        pump(plan[4])
        lax.fori_loop(0, 4, up_chunk, 0)
        pump(plan[5])
        grad, gg, gb = norm_back(dn[...], mid[...], norms[l, 1, 0:1])
        gnorm[l * 4 + 2 : l * 4 + 3] = gg
        gnorm[l * 4 + 3 : l * 4 + 4] = gb
        gh[...] += grad
        if l == 1:
            start(mlp_loads(0))
            for k in range(2):
                act_load(0, k).start()
                dg_load(0, k).start()
        wait(att_loads(l))
        transposed(lambda t: gh[:, t * 128 : (t + 1) * 128])
        produce(c0 + 8, lambda q: nn(flip[q * 192 : (q + 1) * 192], attl[...]))
        produced(c0 + 7)
        fetch(w0 + 4).wait()
        low = gh[...].astype(BF)
        for t in range(3):
            at = slice(t * 256, (t + 1) * 256)
            gatt[:, at] = nn(low, wbuf[0, 768:1536, at]) * rz[:, at]
        norm_sum[...] = jnp.zeros_like(norm_sum)

        def attention(hp, carry):
            at = span(hp, 128)
            deltas = []
            for r in range(2):
                rr = slice(r * 128, (r + 1) * 128)
                gp = gatt[rr, at]
                gpb = gp.astype(BF)
                gpt = gp.T.astype(BF)
                gp = gpb.astype(F32)
                ga = gp * att[rr, at]
                v = qkv[rr, pl.ds(pl.multiple_of(1536 + hp * 128, 128), 128)]
                states, pair = [], []
                for k in range(2):
                    keep = left if k == 0 else jnp.logical_not(left)
                    ghalf = jnp.where(keep, gp, 0.0).astype(BF)
                    c = jnp.sum(jnp.where(keep, ga, 0.0), axis=1, keepdims=True)
                    c_high = c.astype(BF).astype(F32)
                    csel = jnp.where(lanes == hp * 2 + k, -c_high, jnp.where(lanes == hp * 2 + k + 64, c_high - c, 0.0)).astype(BF)
                    fat = pl.ds(pl.multiple_of(hp * 256 + k * 128, 128), 128)
                    phq, phk = phi[0, fat, rr], phi[1, fat, rr]
                    da, da_low = parts_of((nt(ghalf, v) - c) * mask[r])
                    a = (nn(phq.astype(F32).T.astype(BF), phk) * mask[r]).astype(BF)
                    far = nt(
                        jnp.concatenate([got[r, at], got[r, 768:896]], axis=1), jnp.concatenate([ghalf, csel], axis=1)
                    )
                    gq = nt(phk, da) + nt(phk, da_low) + chain[r] * far
                    gphik[fat, rr] = nn(phq, da) + nn(phq, da_low)
                    gvt[pl.ds(pl.multiple_of(hp * 128 + k * 64, 64), 64), rr] = nn(gpt, a)[k * 64 : (k + 1) * 64]
                    here = nn((phq.astype(F32) * chain[r]).astype(BF), jnp.concatenate([gpb, csel], axis=1))
                    states.append(here[:, :128])
                    norm_sum[r] += here[:, 128:]
                    pair.append(softmax_back(phq, gq))
                state[r, at] = jnp.where(left, states[0], states[1]).astype(BF)
                deltas.append(jnp.concatenate(pair, axis=0))
            delta, delta_low = parts_of(jnp.concatenate(deltas, axis=1))
            dqkvt[at] = nn(maps[l, 0, hp], delta).astype(BF)
            gm[l, 0, hp] = nn(delta, qkv[:, at]) + nn(delta_low, qkv[:, at]) + nn(delta, qlo[:, at])
            return carry

        for k in range(3):
            lax.fori_loop(2 * k, 2 * k + 2, attention, 0)
            if k < 2:
                pump(plan[6 + k])
        for r in range(2):
            state[r, 768:896] = norm_sum[r].astype(BF)
        swaps = [
            Exchange(n, s, b, r, state.at[r], taken.at[r], sums.at[r], back.at[r], esem.at[l, r]) for r in range(2)
        ]
        for swap in swaps:
            swap.send()
        produced(c0 + 8)
        pump(plan[8])
        for swap in swaps:
            swap.turn(coef)
        pump(plan[9])
        for swap in swaps:
            swap.receive()

        def keys(hp, carry):
            at = span(hp, 128)
            deltas = []
            for r in range(2):
                rr = slice(r * 128, (r + 1) * 128)
                v = qkv[rr, pl.ds(pl.multiple_of(1536 + hp * 128, 128), 128)].astype(F32)
                turned = back[r, at].astype(F32).T.astype(BF)
                both = jnp.concatenate([back[r, at], back[r, 768:896]], axis=1)
                pair = []
                for k in range(2):
                    keep = left if k == 0 else jnp.logical_not(left)
                    vhalf = jnp.where(keep, v, 0.0).astype(BF)
                    pick = (lanes % 64 == hp * 2 + k).astype(BF)
                    fat = pl.ds(pl.multiple_of(hp * 256 + k * 128, 128), 128)
                    phk = phi[1, fat, rr]
                    gk = gphik[fat, rr] + last[r] * nt(both, jnp.concatenate([vhalf, pick], axis=1))
                    more = last[r] * nn(turned, phk)[k * 64 : (k + 1) * 64]
                    hat = pl.multiple_of(hp * 128 + k * 64, 64)
                    dqkvt[pl.ds(1536 + hat, 64), rr] = (gvt[pl.ds(hat, 64), rr] + more).astype(BF)
                    pair.append(softmax_back(phk, gk))
                deltas.append(jnp.concatenate(pair, axis=0))
            delta, delta_low = parts_of(jnp.concatenate(deltas, axis=1))
            key_at = pl.ds(pl.multiple_of(768 + hp * 128, 128), 128)
            dqkvt[key_at] = nn(maps[l, 1, hp], delta).astype(BF)
            gm[l, 1, hp] = nn(delta, qkv[:, key_at]) + nn(delta_low, qkv[:, key_at]) + nn(delta, qlo[:, key_at])
            return carry

        for k in range(3):
            lax.fori_loop(2 * k, 2 * k + 2, keys, 0)
            if k < 2:
                pump(plan[10 + k])
        for swap in swaps:
            swap.finish()

        def in_chunk(j, carry):
            produce(c0 + 9 + j, lambda q: nn(dqkvt[pl.ds(pl.multiple_of(q * 576 + j * 192, 64), 192)], na[...]))

            @pl.when(j > 0)
            def _():
                absorb(c0 + 8 + j)

            return carry

        lax.fori_loop(0, 3, in_chunk, 0)
        pump(plan[12])
        fetch(w0 + 5).wait()
        for t in range(9):
            piece = jnp.concatenate(
                [dqkvt[t * 256 : t * 256 + 128].astype(F32).T, dqkvt[t * 256 + 128 : t * 256 + 256].astype(F32).T], axis=1
            ).astype(BF)
            place = wbuf[1, t * 256 : (t + 1) * 256] if t < 6 else wbuf[0, (t - 6) * 256 : (t - 5) * 256]
            term = nn(piece, place)
            if t == 0:
                dn[...] = term
            else:
                dn[...] += term
        fetch_start(w0 + 6)
        fetch_start(w0 + 7)
        grad, gg, gb = norm_back(dn[...], h[...], norms[l, 0, 0:1])
        gnorm[l * 4 : l * 4 + 1] = gg
        gnorm[l * 4 + 1 : l * 4 + 2] = gb
        gh[...] += grad
        if l == 1:
            start(att_loads(0))
        pump(plan[13])
        assert slot[0] <= c0 + 11
    o_tok[...] = gh[...].astype(BF)
    c = count - 1
    cC(c - 2).wait_send()
    for k in range(4):
        into = g.at[c % 2, k % 2, k // 2]
        into[...] = jnp.zeros((CHUNK, D), BF)
        into[128:144] = jnp.concatenate([gnorm[...], jnp.zeros((8, D), F32)], axis=0).astype(BF)
        for l in range(2):
            for which in range(2):
                tiles = [None, None]
                for head in range(3 * k, 3 * k + 3):
                    side = head % 2
                    block = gm[l, which, head // 2][side * 64 : (side + 1) * 64]
                    block = jnp.where(left[:64] if side == 0 else jnp.logical_not(left[:64]), block, 0.0)
                    tile = (head % 3) // 2
                    tiles[tile] = block if tiles[tile] is None else tiles[tile] + block
                for tile in range(2):
                    first = (which * 2 + tile) * 128
                    into[l * 64 : (l + 1) * 64, first : first + 128] = tiles[tile].astype(BF)
    cC(c).start()
    absorb(c - 1)
    absorb(c)

    def tail(t, carry):
        step(t)
        return carry

    lax.fori_loop(slot[0], count + len(stages) - 1, tail, 0)
    cC(count - 2).wait_send()
    cC(count - 1).wait_send()

    def drain(c, carry):
        for copy in (cY, cZ1, cZ2, cA2, cA1, cB):
            copy(c).wait_send()
        cO(c).wait()
        return carry

    lax.fori_loop(0, count, drain, 0)


def backward(n, cot, norms, maps, mask, chain, last, coef, saved):
    group, _ = owners(n)
    m = cot.shape[0]
    count = 25
    extra = len([v for v in range(2, 10) if (1 << v) < n // 2])
    vmem = pl.BlockSpec(memory_space=pltpu.VMEM)
    anywhere = pl.BlockSpec(memory_space=pl.ANY)
    pair = lambda: pltpu.SemaphoreType.DMA((2, count))
    V = lambda kind, *shape: pltpu.VMEM(shape, kind)
    return pl.pallas_call(
        functools.partial(backward_kernel, n, count),
        name="backward",
        out_shape=(jax.ShapeDtypeStruct((count, CHUNK, D), BF), jax.ShapeDtypeStruct((m, D), BF)),
        in_specs=[vmem] * 6 + [pl.BlockSpec(memory_space=pltpu.SMEM)] + [anywhere] * 14,
        out_specs=[anywhere, vmem],
        scratch_shapes=[
            V(BF, count, 2, CHUNK, D), V(BF, count, CHUNK, D), V(BF, count, CHUNK, 384), V(BF, count, CHUNK // 2, 384),
            V(BF, count, CHUNK // 4, 384), V(BF, count if extra else 1, extra + 1, CHUNK // 4, 384), V(BF, 2, 2, 2, CHUNK, D),
            V(BF, 2, 1536, D), V(BF, 2, m, D), V(BF, 2, m, D), V(BF, m, D), V(F32, m, D), V(F32, m, D), V(F32, m, D),
            V(BF, m, 2304), V(BF, 2, 1536, m), V(BF, 2, STATE_ROWS, 128), V(BF, m, D), V(F32, m, D), V(BF, m, 1536), V(BF, m, D),
            V(F32, m, D), V(BF, 4, m, D), V(F32, m, D), V(F32, 1536, m), V(F32, D, m), V(BF, 2304, m), V(BF, D, m), V(F32, m, D),
            V(F32, 2, 2, 6, 128, 128), V(F32, 8, D), V(F32, 2, 128, 128), V(BF, 2, STATE_ROWS, 128),
            V(BF, 2, n, group, 128), V(BF, 2, n, group, 128), V(BF, 2, STATE_ROWS, 128),
            pair(), pair(), pair(), pair(), pair(), pltpu.SemaphoreType.DMA((2, count, max(extra, 1))), pair(), pair(), pair(),
            pltpu.SemaphoreType.DMA((count,)), pltpu.SemaphoreType.DMA((2, 2, 4)), pltpu.SemaphoreType.DMA((2,)),
            pltpu.SemaphoreType.DMA((2, 2)), pltpu.SemaphoreType.DMA((11,)),
        ],
        compiler_params=pltpu.CompilerParams(collective_id=1, has_side_effects=True, vmem_limit_bytes=63 * 2**20),
    )(cot, norms, maps, mask, chain, last, coef, *saved)


def finish_kernel(x_ref, down, up, out, inner):
    j = pl.program_id(1)

    @pl.when(j == 0)
    def _():
        for k in range(4):
            down[0, :, k * D : (k + 1) * D] = x_ref[k].astype(F32)

    @pl.when(j == 1)
    def _():
        for k in range(4):
            up[0, k * CHUNK : (k + 1) * CHUNK] = x_ref[k].astype(F32)

    @pl.when(j == 2)
    def _():
        out[0] = x_ref[0].astype(F32)
        for k in range(3):
            inner[0, k * CHUNK : (k + 1) * CHUNK] = x_ref[k + 1].astype(F32)


def finish(total, layers):
    shape = lambda *dims: jax.ShapeDtypeStruct((layers,) + dims, F32)
    whole = lambda *dims: pl.BlockSpec((1,) + dims, lambda l, j: (l, 0, 0))
    return pl.pallas_call(
        finish_kernel,
        name="finish",
        grid=(layers, 3),
        out_shape=(shape(CHUNK, 3072), shape(D, D), shape(CHUNK, D), shape(3 * CHUNK, D)),
        in_specs=[pl.BlockSpec((4, CHUNK, D), lambda l, j: ((layers - 1 - l) * 3 + j, 0, 0))],
        out_specs=[whole(CHUNK, 3072), whole(D, D), whole(CHUNK, D), whole(3 * CHUNK, D)],
        compiler_params=pltpu.CompilerParams(vmem_limit_bytes=40 * 2**20),
    )(total)


def prologue(lengths, attn_in, attn_out, mlp_in, mlp_out, norm_gains, norm_biases, feature_maps, tok_rows):
    layers = attn_in.shape[0]
    n = lax.axis_size("seq")
    me = lax.axis_index("seq")
    first = me * tok_rows
    starts = jnp.cumsum(lengths, axis=1) - lengths
    seg = lambda p: jnp.sum((starts[:, None, :] <= p[None, :, None]).astype(jnp.int32), axis=2) - 1
    ids = seg(first + jnp.arange(tok_rows, dtype=jnp.int32))
    firsts = jnp.arange(n, dtype=jnp.int32) * tok_rows
    before, final = seg(firsts - 1), seg(firsts + tok_rows - 1)
    prior = seg((first - 1)[None])
    chain = jnp.broadcast_to((ids == prior).astype(F32)[:, :, None], ids.shape + (128,))
    last = (ids == ids[:, -1:]).astype(F32)[:, None, :]
    lower = jnp.tril(jnp.ones((tok_rows, tok_rows), F32))
    mask = (ids[:, :, None] == ids[:, None, :]).astype(F32) * lower[None]
    order = jnp.arange(n)
    coef = ((final[:, None, :] == before[:, :, None]) & (order[None, :] < order[:, None])[None]).astype(F32)
    coef_back = jnp.swapaxes(coef, 1, 2)
    packed = jnp.concatenate(
        [
            jnp.swapaxes(attn_in, 1, 2),
            jnp.swapaxes(attn_out, 1, 2),
            mlp_in,
            jnp.transpose(mlp_out.reshape(layers, 4, 768, 192), (0, 1, 3, 2)).reshape(layers, 768, 768),
        ],
        axis=1,
    )
    small = jnp.concatenate([norm_gains[:, :, None], norm_biases[:, :, None], feature_maps], axis=2)
    count = layers * 33
    small = jnp.pad(small.reshape(count, 768), ((0, -count % 16), (0, 0)))
    smalls = gather_small(small)[:, :count].reshape(4, layers, 2, 66, 192)
    smalls = jnp.transpose(smalls, (1, 2, 3, 0, 4)).reshape(layers, 2, 66, 768)
    norms = smalls[:, :, :2].astype(F32)
    maps = jnp.transpose(smalls[:, :, 2:].reshape(layers, 2, 64, 6, 2, 64), (0, 1, 3, 4, 5, 2))
    maps = (maps[:, :, :, :, :, None, :] * jnp.eye(2, dtype=BF)[:, None, :, None]).reshape(layers, 2, 6, 128, 128)
    chain_row = (ids == prior).astype(F32)[:, None, :]
    return packed, norms, maps, jnp.swapaxes(maps, 3, 4), mask, chain, chain_row, last, coef.reshape(-1), coef_back.reshape(-1)


def shards(tokens, cotangent, lengths, attn_in, attn_out, mlp_in, mlp_out, norm_gains, norm_biases, feature_maps):
    tok_rows = tokens.shape[1]
    layers = attn_in.shape[0]
    n = lax.axis_size("seq")
    packed, norms, maps, maps_back, mask, chain, chain_row, last, coef, coef_back = prologue(
        lengths, attn_in, attn_out, mlp_in, mlp_out, norm_gains, norm_biases, feature_maps, tok_rows
    )
    *saved, block_output = forward(n, tokens.reshape(-1, D), packed, norms, maps, mask, chain, last, coef)
    total, grad_tokens = backward(
        n, cotangent.reshape(-1, D), norms, maps_back, mask, chain_row, last, coef_back, saved
    )
    grad_down, grad_up, grad_out, grad_in = finish(total, layers)
    grad_down, grad_out, grad_in = (jnp.swapaxes(v, 1, 2) for v in (grad_down, grad_out, grad_in))
    b = lax.axis_index("batch")
    norm_rows = lax.dynamic_slice(total[-1, 128:136], (0, b * 192), (8, 192)).astype(F32).reshape(layers, 2, 2, 192)
    tiles = total[-1, :128, :512].astype(F32).reshape(layers, 64, 2, 2, 2, 64)
    even = b % 2 == 0
    first = jnp.where(even, tiles[:, :, :, 0, 0], tiles[:, :, :, 0, 1])
    second = jnp.where(even, tiles[:, :, :, 0, 1], tiles[:, :, :, 0, 0])
    third = jnp.where(even, tiles[:, :, :, 1, 0], tiles[:, :, :, 1, 1])
    grad_maps = jnp.stack([first, second, third], axis=3)
    grad_maps = jnp.transpose(grad_maps, (0, 2, 4, 3, 1)).reshape(layers, 2, 64, 192)
    return (
        block_output.reshape(tokens.shape),
        grad_tokens.reshape(tokens.shape),
        grad_in,
        grad_out,
        grad_up,
        grad_down,
        norm_rows[:, :, 0],
        norm_rows[:, :, 1],
        grad_maps,
        norm_rows[:, 1, 1],
    )


def solution(mesh):
    in_specs = (
        P("batch", "seq", None),
        P("batch", "seq", None),
        P("batch", None),
        P(None, None, "batch"),
        P(None, None, "batch"),
        P(None, None, "batch"),
        P(None, None, "batch"),
        P(None, None, "batch"),
        P(None, None, "batch"),
        P(None, None, None, "batch"),
    )
    out_specs = (
        P("batch", "seq", None),
        P("batch", "seq", None),
        P(None, None, "batch"),
        P(None, None, "batch"),
        P(None, None, "batch"),
        P(None, None, "batch"),
        P(None, None, "batch"),
        P(None, None, "batch"),
        P(None, None, None, "batch"),
        P(None, "batch"),
    )
    return jax.shard_map(shards, mesh=mesh, in_specs=in_specs, out_specs=out_specs, check_vma=False)
```

```python
import functools

import jax
import jax.numpy as jnp
from jax import lax
from jax.experimental import pallas as pl
from jax.experimental.pallas import tpu as pltpu
from jax.sharding import PartitionSpec as P

D = 768
H = 12
HD = 64
EPSILON = 1e-05
GELU = 0.7978845608028654
STATE_ROWS = 896
F32 = jnp.float32
BF = jnp.bfloat16
MESH = pl.DeviceIdType.MESH


def greet(peers):
    bar = pltpu.get_barrier_semaphore()
    for p in peers:
        pl.semaphore_signal(bar, inc=1, device_id=p, device_id_type=MESH)
    pl.semaphore_wait(bar, len(peers))

def remote(src, dst, ss, rs, dev):
    return pltpu.make_async_remote_copy(src_ref=src, dst_ref=dst, send_sem=ss, recv_sem=rs, device_id=dev, device_id_type=MESH)

def arrive(ref, sem):
    pltpu.make_async_copy(ref, ref, sem).wait()

def offsets(c, b):
    if c < 3:
        return b * 576 + c * 192
    if c < 4:
        return 2304 + b * 192
    if c < 8:
        return 3072 + b * 768 + (c - 4) * 192
    return 6144 + (c - 8) * 768 + b * 192


def small_kernel(s_ref, t_ref, sem):
    s = lax.axis_index("seq")
    b = lax.axis_index("batch")
    core, far = b + 1 - 2 * (b % 2), (b + 2) % 4
    greet([(s, core), (s, far)])

    def send(src, who, k, dev):
        return remote(src, t_ref.at[who], sem.at[0, k], sem.at[1, k], dev)

    first = [send(s_ref, b, 0, (s, far)), send(s_ref, b, 1, (s, core))]
    for copy in first:
        copy.start()
    t_ref[b] = s_ref[...]
    first[0].wait_recv()
    second = send(t_ref.at[far], far, 2, (s, core))
    second.start()
    first[0].wait_send()
    first[1].wait()
    second.wait()


def gather_small(small):
    return pl.pallas_call(
        small_kernel,
        name="gather_small",
        out_shape=jax.ShapeDtypeStruct((4,) + small.shape, BF),
        in_specs=[pl.BlockSpec(memory_space=pltpu.VMEM)],
        out_specs=pl.BlockSpec(memory_space=pltpu.VMEM),
        scratch_shapes=[pltpu.SemaphoreType.DMA((2, 3))],
        compiler_params=pltpu.CompilerParams(collective_id=2, has_side_effects=True),
    )(small)


def nn(a, b):
    return lax.dot_general(a, b, (((1,), (0,)), ((), ())), preferred_element_type=F32)


def nt(a, b):
    return lax.dot_general(a, b, (((1,), (1,)), ((), ())), preferred_element_type=F32)


def normalize(v):
    centred = v - jnp.mean(v, axis=-1, keepdims=True)
    return centred * lax.rsqrt(jnp.mean(centred * centred, axis=-1, keepdims=True) + EPSILON)


def span(i, k):
    return pl.ds(pl.multiple_of(i * k, k), k)


def owners(n):
    group = max(16, STATE_ROWS // n)
    return group, STATE_ROWS // group


def parts_of(v):
    high = v.astype(BF)
    return high, (v - high.astype(F32)).astype(BF)


class Exchange:
    def __init__(self, n, seq, batch, row, state, taken, sums, got, sem):
        self.n, self.seq, self.batch, self.row = n, seq, batch, row
        self.state, self.taken, self.sums, self.got, self.sem = state, taken, sums, got, sem
        self.group, self.count = owners(n)

    def outgoing(self, d):
        peer = (self.seq + d) % self.n
        return peer, remote(
            self.state.at[span(peer % self.count, self.group)], self.taken.at[self.seq],
            self.sem.at[0], self.sem.at[1], (peer, self.batch),
        )

    def returning(self, d):
        peer = (self.seq + d) % self.n
        return remote(
            self.sums.at[peer], self.got.at[span(self.seq % self.count, self.group)],
            self.sem.at[2], self.sem.at[3], (peer, self.batch),
        )

    def owned(self, fn):
        if self.count == self.n:
            fn()
        else:
            pl.when(self.seq < self.count)(fn)

    def send(self):
        for d in range(1, self.n):
            peer, copy = self.outgoing(d)
            if self.count == self.n:
                copy.start()
            else:
                pl.when(peer < self.count)(copy.start)

        def keep():
            self.taken[self.seq] = self.state[span(self.seq % self.count, self.group)]

        self.owned(keep)

    def turn(self, coef):
        def work():
            arrive(self.taken.at[pl.ds(0, self.n - 1)], self.sem.at[1])

            def one(p, carry):
                def add(k, total):
                    return total + coef[(self.row * self.n + p) * self.n + k] * self.taken[k].astype(F32)

                total = jnp.zeros((self.group, 128), F32)
                if self.n <= 8:
                    for k in range(self.n):
                        total = add(k, total)
                else:
                    total = lax.fori_loop(0, self.n, add, total)
                self.sums[p] = total.astype(BF)
                return carry

            lax.fori_loop(0, self.n, one, 0)
            for d in range(1, self.n):
                self.returning(d).start()
            self.got[span(self.seq % self.count, self.group)] = self.sums[self.seq]

        self.owned(work)

    def receive(self):
        if self.count == self.n:
            arrive(self.got.at[pl.ds(0, self.group * (self.n - 1))], self.sem.at[3])
        else:
            @pl.when(self.seq < self.count)
            def _():
                arrive(self.got.at[pl.ds(0, self.group * (self.count - 1))], self.sem.at[3])

            @pl.when(self.seq >= self.count)
            def _():
                arrive(self.got.at[pl.ds(0, self.group * self.count)], self.sem.at[3])

    def finish(self):
        if self.count == self.n:
            arrive(self.state.at[pl.ds(0, self.group * (self.n - 1))], self.sem.at[0])
            arrive(self.sums.at[pl.ds(0, self.n - 1)], self.sem.at[2])
        else:
            @pl.when(self.seq < self.count)
            def _():
                arrive(self.state.at[pl.ds(0, self.group * (self.count - 1))], self.sem.at[0])
                arrive(self.sums.at[pl.ds(0, self.n - 1)], self.sem.at[2])

            @pl.when(self.seq >= self.count)
            def _():
                arrive(self.state.at[pl.ds(0, self.group * self.count)], self.sem.at[0])


def forward_kernel(
    n, tok, w_ref, norms, maps, mask, chain, last, coef,
    o_w, o_h, o_mid, o_na, o_nm, o_qkv, o_phi, o_att, o_rz, o_act, o_dg, o_got, o_lo, o_attl, o_out,
    w, h, mid, na, nm, qkv, phi, att, attl, rz, act, dg, got, proj, pq, num, zz, norm_sum, state, taken, sums, qlo, mu, means,
    lsem, ysem, xsem, own_sem, near_sem, far_sem, esem, msem, ssem,
):
    s = lax.axis_index("seq")
    b = lax.axis_index("batch")
    xl = s % 2
    core = b + 1 - 2 * (b % 2)
    far = (b + 2) % 4
    layers = 2
    core_dev, y_dev, x_dev = (s, core), (s, far), (s + 1 - 2 * xl, b)
    greet([core_dev, y_dev] + [((s + d) % n, b) for d in range(1, n)])

    def rows(c, who, part, size):
        return pl.ds(pl.multiple_of(offsets(c % 12, who) + part * 96, 32), size)

    def same(c, who, part, size, sem, dev):
        place = w.at[c // 12, rows(c, who, part, size)]
        return remote(place, place, sem.at[0, c], sem.at[1, c], dev)

    def here(c):
        return w_ref.at[c // 12, pl.ds((c % 12) * 192, 192)]

    def out_y(c):
        src = w_ref.at[c // 12, pl.ds(pl.multiple_of((c % 12) * 192 + xl * 96, 32), 96)]
        return remote(src, w.at[c // 12, rows(c, b, xl, 96)], ysem.at[0, c], ysem.at[1, c], y_dev)

    def out_core(c):
        return remote(here(c), w.at[c // 12, rows(c, b, 0, 192)], own_sem.at[0, c], own_sem.at[1, c], core_dev)

    def stay(c):
        return pltpu.make_async_copy(here(c), w.at[c // 12, rows(c, b, 0, 192)], lsem.at[c])

    out_x = lambda c: same(c, far, xl, 96, xsem, x_dev)
    near = lambda c: same(c, far, xl, 96, near_sem, core_dev)
    rest = lambda c: same(c, far, 1 - xl, 96, far_sem, core_dev)
    count = layers * 12
    for c in range(count):
        out_y(c).start()
        out_core(c).start()
        stay(c).start()

    place = [0]

    def pump(k=1):
        for _ in range(k):
            c = place[0]
            if c > count:
                return
            if c < count:
                out_y(c).wait_recv()
                out_x(c).start()
                near(c).start()
            if c >= 1:
                out_x(c - 1).wait_recv()
                rest(c - 1).start()
            place[0] += 1

    def need(lo, hi):
        while place[0] <= hi:
            pump()
        for c in range(lo, hi):
            stay(c).wait()
            for copy in (out_core(c), near(c), rest(c)):
                copy.wait_recv()

    def exchange_of(l, r):
        return Exchange(n, s, b, r, state.at[l, r], taken.at[l, r], sums.at[l, r], got.at[l, r], esem.at[l, r])

    def mean_copy(l, d):
        peer = (s + d) % n
        return remote(means.at[l, s], means.at[l, s], msem.at[l, 0], msem.at[l, 1], (peer, b))

    stores = []

    def store(src, dst, i):
        copy = pltpu.make_async_copy(src, dst, ssem.at[i])
        copy.start()
        stores.append(copy)
        return copy

    def keep_weights(l, first, size, i):
        at = pl.ds(first, size)
        store(w.at[l, at], o_w.at[l, at], 32 + l * 8 + i)

    left = lax.broadcasted_iota(jnp.int32, (128, 128), 1) < 64
    lanes = lax.broadcasted_iota(jnp.int32, (128, 128), 1)
    rows_i = lax.broadcasted_iota(jnp.int32, (128, 128), 0)
    ones = jnp.ones((128, 128), BF)
    h[0] = tok[...].astype(F32)
    phi_store = act_store = dg_store = None
    for l in range(layers):
        base = l * 12
        na[l] = (normalize(h[l]) * norms[l, 0, 0:1] + norms[l, 0, 1:2]).astype(BF)
        own = [jnp.mean(na[l, r * 128 : (r + 1) * 128].astype(F32), axis=0, keepdims=True) for r in range(2)]
        means[l, s] = jnp.concatenate(own + [jnp.zeros((6, D), F32)], axis=0)
        for d in range(1, n):
            mean_copy(l, d).start()
        need(base, base + 3)
        for t in range(9):
            piece = nt(na[l], w[l, t * 256 : (t + 1) * 256])
            if t < 6:
                proj[:, t * 256 : (t + 1) * 256] = piece
            else:
                if t == 6:
                    arrive(means.at[l, pl.ds(0, n - 1)], msem.at[l, 1])
                    mean = lax.fori_loop(0, n, lambda k, v: v + means[l, k], jnp.zeros((8, D), F32)) / n
                    mean = jnp.concatenate([mean, mean], axis=0).astype(BF)
                shift = nt(mean, w[l, t * 256 : (t + 1) * 256])[:8]
                mu[:, (t - 6) * 256 : (t - 5) * 256] = shift
                piece = jnp.concatenate([piece[:128] - shift[:1], piece[128:] - shift[1:2]], axis=0)
            qkv[l, :, t * 256 : (t + 1) * 256] = piece.astype(BF)
            if t == 4:
                pump()
        if phi_store is not None:
            phi_store.wait()
            stores[:] = [c for c in stores if c is not phi_store]
        norm_sum[...] = jnp.zeros_like(norm_sum)

        def value(hp, r):
            return jnp.concatenate([qkv[l, pl.ds(r * 128, 128), pl.ds(pl.multiple_of(1536 + hp * 128, 128), 128)], ones], axis=1)

        def features(r, hp, carry):
            rr = slice(r * 128, (r + 1) * 128)
            for which in range(2):
                x = proj[rr, pl.ds(pl.multiple_of(which * 768 + hp * 128, 128), 128)]
                high = x.astype(BF)
                low = (x - high.astype(F32)).astype(BF)
                qlo[l, rr, pl.ds(pl.multiple_of(which * 768 + hp * 128, 128), 128)] = low
                m = maps[l, which, hp]
                logits = nt(m, high) + nt(m, low)
                for half in range(2):
                    t = logits[64 * half : 64 * half + 64]
                    up = jnp.exp(t - jnp.max(t, axis=0, keepdims=True))
                    down = jnp.exp(jnp.min(t, axis=0, keepdims=True) - t)
                    at = pl.multiple_of(hp * 256 + half * 128, 128)
                    phi[which, pl.ds(at, 64), rr] = (up * (1.0 / jnp.sum(up, axis=0, keepdims=True))).astype(BF)
                    phi[which, pl.ds(at + 64, 64), rr] = (down * (1.0 / jnp.sum(down, axis=0, keepdims=True))).astype(BF)
            v = value(hp, r)
            sums_ = []
            for half in range(2):
                key = phi[1, pl.ds(pl.multiple_of(hp * 256 + half * 128, 128), 128), rr]
                both = nn((key.astype(F32) * last[r]).astype(BF), v)
                sums_.append(both[:, :128])
                norm_sum[r] += jnp.where(lanes % 64 == hp * 2 + half, both[:, 128:], 0.0)
            state[l, r, span(hp, 128)] = jnp.where(left, sums_[0], sums_[1]).astype(BF)
            return carry

        swaps = [exchange_of(l, r) for r in range(2)]
        for r in range(2):
            for k in range(2):
                lax.fori_loop(3 * k, 3 * k + 3, functools.partial(features, r), 0)
                if k == 0:
                    pump()
            state[l, r, 768:896] = norm_sum[r].astype(BF)
            swaps[r].send()
        phi_store = store(phi, o_phi.at[l], l * 16 + 0)
        store(na.at[l], o_na.at[l], l * 16 + 1)
        store(qlo.at[l], o_lo.at[l], l * 16 + 13)
        store(qkv.at[l], o_qkv.at[l], l * 16 + 2)
        store(h.at[l], o_h.at[l], l * 16 + 3)
        pump()

        def scores(r, hp, carry):
            v = value(hp, r)
            both = []
            for half in range(2):
                at = pl.ds(pl.multiple_of(hp * 256 + half * 128, 128), 128)
                query = phi[0, at, r * 128 : (r + 1) * 128].astype(F32).T.astype(BF)
                pq[r * 128 : (r + 1) * 128, at] = query
                key = phi[1, at, r * 128 : (r + 1) * 128]
                both.append(nn((nn(query, key) * mask[r]).astype(BF), v))
            at = span(hp, 128)
            num[r * 128 : (r + 1) * 128, at] = jnp.where(left, both[0][:, :128], both[1][:, :128])
            zz[r * 128 : (r + 1) * 128, at] = jnp.where(left, both[0][:, 128:], both[1][:, 128:])
            return carry

        def finish_row(r, hp, carry):
            at = span(hp, 128)
            both = []
            for half in range(2):
                query = pq[r * 128 : (r + 1) * 128, pl.ds(pl.multiple_of(hp * 256 + half * 128, 128), 128)]
                pick = (rows_i == hp * 2 + half).astype(BF)
                column = nn(got[l, r, 768:896], pick).astype(BF)
                both.append(nn(query, jnp.concatenate([got[l, r, at], column], axis=1)))
            c = chain[r]
            z = zz[r * 128 : (r + 1) * 128, at] + c * jnp.where(left, both[0][:, 128:], both[1][:, 128:])
            top = num[r * 128 : (r + 1) * 128, at] + c * jnp.where(left, both[0][:, :128], both[1][:, :128])
            inverse = 1.0 / z
            out = top * inverse
            rz[l, r * 128 : (r + 1) * 128, at] = inverse
            att[l, r * 128 : (r + 1) * 128, at] = out
            attl[l, r * 128 : (r + 1) * 128, at] = (out + mu[r : r + 1, at]).astype(BF)
            return carry

        lax.fori_loop(0, 6, functools.partial(scores, 0), 0)
        swaps[0].turn(coef)
        pump()
        lax.fori_loop(0, 6, functools.partial(scores, 1), 0)
        swaps[1].turn(coef)
        pump(2)
        for r in range(2):
            swaps[r].receive()
            lax.fori_loop(0, 6, functools.partial(finish_row, r), 0)
        store(got.at[l], o_got.at[l], l * 16 + 4)
        store(rz.at[l], o_rz.at[l], l * 16 + 5)
        store(att.at[l], o_att.at[l], l * 16 + 6)
        store(attl.at[l], o_attl.at[l], l * 16 + 7)
        need(base + 3, base + 4)
        keep_weights(l, 0, 3072, 0)
        for t in range(3):
            at = slice(t * 256, (t + 1) * 256)
            mid[l, :, at] = h[l, :, at] + nt(attl[l], w[l, 2304 + t * 256 : 2304 + (t + 1) * 256])
        nm[l] = (normalize(mid[l]) * norms[l, 1, 0:1] + norms[l, 1, 1:2]).astype(BF)
        store(mid.at[l], o_mid.at[l], l * 16 + 8)
        store(nm.at[l], o_nm.at[l], l * 16 + 9)
        need(base + 4, base + 8)
        keep_weights(l, 3072, 3072, 1)
        if act_store is not None:
            for copy in (act_store, dg_store):
                copy.wait()
                stores[:] = [c for c in stores if c is not copy]
        for k in range(4):
            for t in range(3):
                at = slice(t * 256, (t + 1) * 256)
                u = nn(nm[l], w[l, 3072 + k * 768 : 3072 + (k + 1) * 768, at])
                square = u * u
                bend = jnp.tanh(GELU * u * (1.0 + 0.044715 * square))
                act[k, :, at] = (0.5 * u * (1.0 + bend)).astype(BF)
                slope = 0.5 * (1.0 + bend) + 0.5 * u * (1.0 - bend * bend) * GELU * (1.0 + 0.134145 * square)
                dg[k, :, at] = slope.astype(BF)
            pump()
        act_store = store(act, o_act.at[l], l * 16 + 10)
        dg_store = store(dg, o_dg.at[l], l * 16 + 11)
        for k in range(4):
            need(base + 8 + k, base + 9 + k)
            keep_weights(l, 6144 + k * 768, 768, 2 + k)
            for t in range(3):
                at = slice(t * 256, (t + 1) * 256)
                first = 6144 + k * 768 + t * 256
                y = nt(act[k], w[l, first : first + 256])
                before = mid[l, :, at] if k == 0 else h[l + 1, :, at]
                h[l + 1, :, at] = before + y
    o_out[...] = h[layers].astype(BF)
    for copy in stores:
        copy.wait()
    for l in range(layers):
        arrive(means.at[l, pl.ds(0, n - 1)], msem.at[l, 0])
        for r in range(2):
            exchange_of(l, r).finish()
    for c in range(count):
        for copy in (out_y(c), out_x(c), out_core(c), near(c), rest(c)):
            copy.wait_send()


def forward(n, tok, w, norms, maps, mask, chain, last, coef):
    group, _ = owners(n)
    m = tok.shape[0]
    hbm = lambda shape, kind: jax.ShapeDtypeStruct(shape, kind)
    outs = (
        hbm((2, 9216, D), BF), hbm((2, m, D), F32), hbm((2, m, D), F32), hbm((2, m, D), BF), hbm((2, m, D), BF),
        hbm((2, m, 2304), BF), hbm((2, 2, 1536, m), BF), hbm((2, m, D), F32), hbm((2, m, D), F32),
        hbm((2, 4, m, D), BF), hbm((2, 4, m, D), BF), hbm((2, 2, STATE_ROWS, 128), BF), hbm((2, m, 1536), BF), hbm((2, m, D), BF), hbm((m, D), BF),
    )
    vmem = pl.BlockSpec(memory_space=pltpu.VMEM)
    anywhere = pl.BlockSpec(memory_space=pl.ANY)
    pair = lambda: pltpu.SemaphoreType.DMA((2, 24))
    V = lambda kind, *shape: pltpu.VMEM(shape, kind)
    return pl.pallas_call(
        functools.partial(forward_kernel, n),
        name="forward",
        out_shape=outs,
        in_specs=[vmem, anywhere, vmem, vmem, vmem, vmem, vmem, pl.BlockSpec(memory_space=pltpu.SMEM)],
        out_specs=[anywhere] * 14 + [vmem],
        scratch_shapes=[
            V(BF, 2, 9216, D), V(F32, 3, m, D), V(F32, 2, m, D), V(BF, 2, m, D), V(BF, 2, m, D), V(BF, 2, m, 2304),
            V(BF, 2, 1536, m), V(F32, 2, m, D), V(BF, 2, m, D), V(F32, 2, m, D), V(BF, 4, m, D), V(BF, 4, m, D),
            V(BF, 2, 2, STATE_ROWS, 128), V(F32, m, 1536), V(BF, m, 1536), V(F32, m, D), V(F32, m, D), V(F32, 2, 128, 128),
            V(BF, 2, 2, STATE_ROWS, 128), V(BF, 2, 2, n, group, 128), V(BF, 2, 2, n, group, 128), V(BF, 2, m, 1536), V(F32, 8, D), V(F32, 2, n, 8, D),
            pltpu.SemaphoreType.DMA((24,)), pair(), pair(), pair(), pair(), pair(),
            pltpu.SemaphoreType.DMA((2, 2, 4)), pltpu.SemaphoreType.DMA((2, 2)), pltpu.SemaphoreType.DMA((48,)),
        ],
        compiler_params=pltpu.CompilerParams(collective_id=0, has_side_effects=True, vmem_limit_bytes=63 * 2**20),
    )(tok, w, norms, maps, mask, chain, last, coef)


def norm_back(y, v, gain):
    centred = v - jnp.mean(v, axis=-1, keepdims=True)
    scale = lax.rsqrt(jnp.mean(centred * centred, axis=-1, keepdims=True) + EPSILON)
    n = centred * scale
    yg = y * gain
    back = scale * (yg - jnp.mean(yg, axis=-1, keepdims=True) - n * jnp.mean(yg * n, axis=-1, keepdims=True))
    return back, jnp.sum(n * y, axis=0, keepdims=True), jnp.sum(y, axis=0, keepdims=True)


def softmax_back(s, g):
    s = s.astype(F32)
    plus, minus = s[:64], s[64:]
    mean = lambda p, v: jnp.sum(p * v, axis=0, keepdims=True) / jnp.sum(p, axis=0, keepdims=True)
    up = plus * (g[:64] - mean(plus, g[:64]))
    down = minus * (g[64:] - mean(minus, g[64:]))
    return up - down


CHUNK = 192
PLAN = {
    1: [0, 0, 0, 0, 0, 1, 0, 1, 2, 2, 1, 1, 0, 1],
    0: [0, 0, 0, 1, 0, 1, 1, 1, 3, 2, 1, 0, 0, 2],
}


def backward_kernel(
    n, count,
    cot, norms, maps, mask, chain, last, coef,
    i_w, i_h, i_mid, i_na, i_nm, i_qkv, i_phi, i_att, i_rz, i_act, i_dg, i_got, i_lo, i_attl,
    o_grad, o_tok,
    recv_c, recv_y, recv_x, recv_1, recv_2, recv_h, g, wbuf, actb, dgb, nm, mid, att, rz, qkv, phi, got, na, h, qlo, attl,
    gh, du, gatt, gphik, gvt, dqkvt, flip, dn, gm, gnorm, norm_sum, state, taken, sums, back,
    csem, ysem, xsem, z1sem, z2sem, hsem, a2sem, a1sem, bsem, osem, esem, wsem, asem, lsem,
):
    s = lax.axis_index("seq")
    b = lax.axis_index("batch")
    xl, z = s % 2, s // 2
    b0, b1 = z % 2, (z // 2) % 2
    par, yy = b % 2, b // 2
    levels = [v for v in range(2, 10) if (1 << v) < n // 2]
    core_dev, y_dev, x_dev = (s, b + 1 - 2 * par), (s, (b + 2) % 4), (s + 1 - 2 * xl, b)
    z1_dev, z2_dev = (s + 2 * (1 - 2 * b0), b), (s + 4 * (1 - 2 * b1), b)
    h_dev = lambda v: (s + (2 << v) * (1 - 2 * ((z // (1 << v)) % 2)), b)
    greet([core_dev, y_dev] + [((s + d) % n, b) for d in range(1, n)])

    quarter_rows = CHUNK // 4
    xc, xo = span(xl, 384), span(1 - xl, 384)
    half = span(b0, CHUNK // 2)
    quarter = pl.ds(pl.multiple_of(b0 * (CHUNK // 2) + b1 * quarter_rows, 16), quarter_rows)
    fin = recv_y
    cC = lambda c: remote(g.at[c % 2, 1 - par], recv_c.at[c], csem.at[0, c], csem.at[1, c], core_dev)
    cY = lambda c: remote(recv_c.at[c, 1 - yy], recv_y.at[c], ysem.at[0, c], ysem.at[1, c], y_dev)
    cX = lambda c: remote(recv_y.at[c, :, xo], recv_x.at[c], xsem.at[0, c], xsem.at[1, c], x_dev)
    cZ1 = lambda c: remote(recv_x.at[c, span(1 - b0, CHUNK // 2)], recv_1.at[c], z1sem.at[0, c], z1sem.at[1, c], z1_dev)
    cZ2 = lambda c: remote(recv_1.at[c, span(1 - b1, quarter_rows)], recv_2.at[c], z2sem.at[0, c], z2sem.at[1, c], z2_dev)
    cH = lambda c, i: remote(recv_h.at[c, len(levels)], recv_h.at[c, i], hsem.at[0, c, i], hsem.at[1, c, i], h_dev(levels[i]))
    cA2 = lambda c: remote(fin.at[c, quarter, xc], fin.at[c, quarter, xc], a2sem.at[0, c], a2sem.at[1, c], z2_dev)
    cA1 = lambda c: remote(fin.at[c, half, xc], fin.at[c, half, xc], a1sem.at[0, c], a1sem.at[1, c], z1_dev)
    cB = lambda c: remote(fin.at[c, :, xc], fin.at[c, :, xc], bsem.at[0, c], bsem.at[1, c], x_dev)
    cO = lambda c: pltpu.make_async_copy(fin.at[c], o_grad.at[c], osem.at[c])

    def add(a, b_):
        return (a.astype(F32) + b_.astype(F32)).astype(BF)

    def absorb(c):
        cC(c).wait_recv()
        recv_c[c, 1 - yy] = add(recv_c[c, 1 - yy], g[c % 2, par, 1 - yy])
        cY(c).start()
        recv_c[c, yy] = add(recv_c[c, yy], g[c % 2, par, yy])

    def stage_x(c):
        cY(c).wait_recv()
        recv_y[c, :, xo] = add(recv_y[c, :, xo], recv_c[c, yy, :, xo])
        cX(c).start()
        recv_y[c, :, xc] = add(recv_y[c, :, xc], recv_c[c, yy, :, xc])

    def stage_z1(c):
        cX(c).wait()
        recv_x[c] = add(recv_x[c], recv_y[c, :, xc])
        cZ1(c).start()

    def stage_z2(c):
        cZ1(c).wait_recv()
        recv_1[c] = add(recv_1[c], recv_x[c, half])
        cZ2(c).start()

    def stage_a2(c):
        cZ2(c).wait_recv()
        t = add(recv_2[c], recv_1[c, span(b1, quarter_rows)])
        for i in range(len(levels)):
            recv_h[c, len(levels)] = t
            cH(c, i).start()
            cH(c, i).wait()
            t = add(t, recv_h[c, i])
        fin[c, quarter, xc] = t
        cA2(c).start()

    def stage_a1(c):
        cA2(c).wait_recv()
        cA1(c).start()

    def stage_b(c):
        cA1(c).wait_recv()
        cB(c).start()

    def stage_o(c):
        cB(c).wait_recv()
        cO(c).start()

    stages = [stage_x, stage_z1, stage_z2, stage_a2, stage_a1, stage_b, stage_o]

    def step(t):
        for i, stage in enumerate(stages):
            c = t - i
            if isinstance(c, int):
                if 0 <= c < count:
                    stage(c)
            else:
                pl.when((c >= 0) & (c < count))(functools.partial(stage, c))

    slot = [0]

    def pump(k=1):
        for _ in range(k):
            step(slot[0])
            slot[0] += 1

    def produce(c, block):
        @pl.when(c >= 2)
        def _():
            cC(c - 2).wait_send()

        for k in range(4):
            g[c % 2, k % 2, k // 2] = block(k).astype(BF)
        cC(c).start()

    def produced(c):
        pl.when(c >= 0)(functools.partial(absorb, c))

    left = lax.broadcasted_iota(jnp.int32, (128, 128), 1) < 64
    lanes = lax.broadcasted_iota(jnp.int32, (128, 128), 1)
    parts = []
    for l in (1, 0):
        parts += [(l, 6144), (l, 7680), (l, 3072), (l, 4608), (l, 1536), (l, 0)]

    def fetch(i):
        if i < len(parts):
            l, first = parts[i]
            return pltpu.make_async_copy(i_w.at[l, pl.ds(first, 1536)], wbuf.at[i % 2], wsem.at[i % 2])
        return None

    def fetch_start(i):
        if i < len(parts):
            fetch(i).start()

    mlp_loads = lambda l: [
        pltpu.make_async_copy(src.at[l], dst, lsem.at[i]) for i, (src, dst) in enumerate(((i_nm, nm), (i_mid, mid)))
    ]
    att_loads = lambda l: [
        pltpu.make_async_copy(src.at[l], dst, lsem.at[i + 2])
        for i, (src, dst) in enumerate(
            ((i_att, att), (i_rz, rz), (i_qkv, qkv), (i_phi, phi), (i_got, got), (i_na, na), (i_h, h), (i_lo, qlo), (i_attl, attl))
        )
    ]
    act_load = lambda l, k: pltpu.make_async_copy(i_act.at[l, k], actb.at[k % 2], asem.at[0, k % 2])
    dg_load = lambda l, k: pltpu.make_async_copy(i_dg.at[l, k], dgb.at[k % 2], asem.at[1, k % 2])

    def start(copies):
        for copy in copies:
            copy.start()

    def wait(copies):
        for copy in copies:
            copy.wait()

    def transposed(src):
        for t in range(6):
            flip[t * 128 : (t + 1) * 128] = src(t).T.astype(BF)

    fetch_start(0)
    for k in range(2):
        act_load(1, k).start()
        dg_load(1, k).start()
    gh[...] = cot[...].astype(F32)
    for l in (1, 0):
        c0 = (1 - l) * 12
        w0 = (1 - l) * 6
        plan = PLAN[l]
        transposed(lambda t: gh[:, t * 128 : (t + 1) * 128])
        for k in range(4):
            if k % 2 == 0:
                fetch(w0 + k // 2).wait()
            if k == 0 and l == 1:
                fetch_start(1)
                start(mlp_loads(1))
                start(att_loads(1))
            act_load(l, k).wait()
            dg_load(l, k).wait()
            low = gh[...].astype(BF)
            for t in range(3):
                at = slice(t * 256, (t + 1) * 256)
                du[k, :, at] = (nn(low, wbuf[(k // 2) % 2, (k % 2) * 768 : (k % 2 + 1) * 768, at]) * dgb[k % 2, :, at].astype(F32)).astype(BF)
            produce(c0 + k, lambda q, k=k: nn(flip[q * 192 : (q + 1) * 192], actb[k % 2]))
            produced(c0 + k - 1)
            if k < 2:
                act_load(l, k + 2).start()
                dg_load(l, k + 2).start()
            if k % 2 == 1:
                fetch_start(w0 + 2 + k // 2)
            pump(plan[k])
        wait(mlp_loads(l))
        for k in range(4):
            if k % 2 == 0:
                fetch(w0 + 2 + k // 2).wait()
            for t in range(3):
                at = slice(t * 256, (t + 1) * 256)
                term = nt(du[k], wbuf[(k // 2) % 2, (k % 2) * 768 + t * 256 : (k % 2) * 768 + (t + 1) * 256])
                if k == 0:
                    dn[:, at] = term
                else:
                    dn[:, at] += term
            if k % 2 == 1:
                fetch_start(w0 + 4 + k // 2)
        transposed(lambda t: nm[:, t * 128 : (t + 1) * 128].astype(F32))

        def up_chunk(j, carry):
            produce(c0 + 4 + j, lambda q: nn(flip[span(j, 192)], du[q]))
            produced(c0 + 3 + j)
            return carry

        pump(plan[4])
        lax.fori_loop(0, 4, up_chunk, 0)
        pump(plan[5])
        grad, gg, gb = norm_back(dn[...], mid[...], norms[l, 1, 0:1])
        gnorm[l * 4 + 2 : l * 4 + 3] = gg
        gnorm[l * 4 + 3 : l * 4 + 4] = gb
        gh[...] += grad
        if l == 1:
            start(mlp_loads(0))
            for k in range(2):
                act_load(0, k).start()
                dg_load(0, k).start()
        wait(att_loads(l))
        transposed(lambda t: gh[:, t * 128 : (t + 1) * 128])
        produce(c0 + 8, lambda q: nn(flip[q * 192 : (q + 1) * 192], attl[...]))
        produced(c0 + 7)
        fetch(w0 + 4).wait()
        low = gh[...].astype(BF)
        for t in range(3):
            at = slice(t * 256, (t + 1) * 256)
            gatt[:, at] = nn(low, wbuf[0, 768:1536, at]) * rz[:, at]
        norm_sum[...] = jnp.zeros_like(norm_sum)

        def attention(hp, carry):
            at = span(hp, 128)
            deltas = []
            for r in range(2):
                rr = slice(r * 128, (r + 1) * 128)
                gp = gatt[rr, at]
                gpb = gp.astype(BF)
                gpt = gp.T.astype(BF)
                gp = gpb.astype(F32)
                ga = gp * att[rr, at]
                v = qkv[rr, pl.ds(pl.multiple_of(1536 + hp * 128, 128), 128)]
                states, pair = [], []
                for k in range(2):
                    keep = left if k == 0 else jnp.logical_not(left)
                    ghalf = jnp.where(keep, gp, 0.0).astype(BF)
                    c = jnp.sum(jnp.where(keep, ga, 0.0), axis=1, keepdims=True)
                    c_high = c.astype(BF).astype(F32)
                    csel = jnp.where(lanes == hp * 2 + k, -c_high, jnp.where(lanes == hp * 2 + k + 64, c_high - c, 0.0)).astype(BF)
                    fat = pl.ds(pl.multiple_of(hp * 256 + k * 128, 128), 128)
                    phq, phk = phi[0, fat, rr], phi[1, fat, rr]
                    da, da_low = parts_of((nt(ghalf, v) - c) * mask[r])
                    a = (nn(phq.astype(F32).T.astype(BF), phk) * mask[r]).astype(BF)
                    far = nt(
                        jnp.concatenate([got[r, at], got[r, 768:896]], axis=1), jnp.concatenate([ghalf, csel], axis=1)
                    )
                    gq = nt(phk, da) + nt(phk, da_low) + chain[r] * far
                    gphik[fat, rr] = nn(phq, da) + nn(phq, da_low)
                    gvt[pl.ds(pl.multiple_of(hp * 128 + k * 64, 64), 64), rr] = nn(gpt, a)[k * 64 : (k + 1) * 64]
                    here = nn((phq.astype(F32) * chain[r]).astype(BF), jnp.concatenate([gpb, csel], axis=1))
                    states.append(here[:, :128])
                    norm_sum[r] += here[:, 128:]
                    pair.append(softmax_back(phq, gq))
                state[r, at] = jnp.where(left, states[0], states[1]).astype(BF)
                deltas.append(jnp.concatenate(pair, axis=0))
            delta, delta_low = parts_of(jnp.concatenate(deltas, axis=1))
            dqkvt[at] = nn(maps[l, 0, hp], delta).astype(BF)
            gm[l, 0, hp] = nn(delta, qkv[:, at]) + nn(delta_low, qkv[:, at]) + nn(delta, qlo[:, at])
            return carry

        for k in range(3):
            lax.fori_loop(2 * k, 2 * k + 2, attention, 0)
            if k < 2:
                pump(plan[6 + k])
        for r in range(2):
            state[r, 768:896] = norm_sum[r].astype(BF)
        swaps = [
            Exchange(n, s, b, r, state.at[r], taken.at[r], sums.at[r], back.at[r], esem.at[l, r]) for r in range(2)
        ]
        for swap in swaps:
            swap.send()
        produced(c0 + 8)
        pump(plan[8])
        for swap in swaps:
            swap.turn(coef)
        pump(plan[9])
        for swap in swaps:
            swap.receive()

        def keys(hp, carry):
            at = span(hp, 128)
            deltas = []
            for r in range(2):
                rr = slice(r * 128, (r + 1) * 128)
                v = qkv[rr, pl.ds(pl.multiple_of(1536 + hp * 128, 128), 128)].astype(F32)
                turned = back[r, at].astype(F32).T.astype(BF)
                both = jnp.concatenate([back[r, at], back[r, 768:896]], axis=1)
                pair = []
                for k in range(2):
                    keep = left if k == 0 else jnp.logical_not(left)
                    vhalf = jnp.where(keep, v, 0.0).astype(BF)
                    pick = (lanes % 64 == hp * 2 + k).astype(BF)
                    fat = pl.ds(pl.multiple_of(hp * 256 + k * 128, 128), 128)
                    phk = phi[1, fat, rr]
                    gk = gphik[fat, rr] + last[r] * nt(both, jnp.concatenate([vhalf, pick], axis=1))
                    more = last[r] * nn(turned, phk)[k * 64 : (k + 1) * 64]
                    hat = pl.multiple_of(hp * 128 + k * 64, 64)
                    dqkvt[pl.ds(1536 + hat, 64), rr] = (gvt[pl.ds(hat, 64), rr] + more).astype(BF)
                    pair.append(softmax_back(phk, gk))
                deltas.append(jnp.concatenate(pair, axis=0))
            delta, delta_low = parts_of(jnp.concatenate(deltas, axis=1))
            key_at = pl.ds(pl.multiple_of(768 + hp * 128, 128), 128)
            dqkvt[key_at] = nn(maps[l, 1, hp], delta).astype(BF)
            gm[l, 1, hp] = nn(delta, qkv[:, key_at]) + nn(delta_low, qkv[:, key_at]) + nn(delta, qlo[:, key_at])
            return carry

        for k in range(3):
            lax.fori_loop(2 * k, 2 * k + 2, keys, 0)
            if k < 2:
                pump(plan[10 + k])
        for swap in swaps:
            swap.finish()

        def in_chunk(j, carry):
            produce(c0 + 9 + j, lambda q: nn(dqkvt[pl.ds(pl.multiple_of(q * 576 + j * 192, 64), 192)], na[...]))

            @pl.when(j > 0)
            def _():
                absorb(c0 + 8 + j)

            return carry

        lax.fori_loop(0, 3, in_chunk, 0)
        pump(plan[12])
        fetch(w0 + 5).wait()
        for t in range(9):
            piece = jnp.concatenate(
                [dqkvt[t * 256 : t * 256 + 128].astype(F32).T, dqkvt[t * 256 + 128 : t * 256 + 256].astype(F32).T], axis=1
            ).astype(BF)
            place = wbuf[1, t * 256 : (t + 1) * 256] if t < 6 else wbuf[0, (t - 6) * 256 : (t - 5) * 256]
            term = nn(piece, place)
            if t == 0:
                dn[...] = term
            else:
                dn[...] += term
        fetch_start(w0 + 6)
        fetch_start(w0 + 7)
        grad, gg, gb = norm_back(dn[...], h[...], norms[l, 0, 0:1])
        gnorm[l * 4 : l * 4 + 1] = gg
        gnorm[l * 4 + 1 : l * 4 + 2] = gb
        gh[...] += grad
        if l == 1:
            start(att_loads(0))
        pump(plan[13])
        assert slot[0] <= c0 + 11
    o_tok[...] = gh[...].astype(BF)
    c = count - 1
    cC(c - 2).wait_send()
    for k in range(4):
        into = g.at[c % 2, k % 2, k // 2]
        into[...] = jnp.zeros((CHUNK, D), BF)
        into[128:144] = jnp.concatenate([gnorm[...], jnp.zeros((8, D), F32)], axis=0).astype(BF)
        for l in range(2):
            for which in range(2):
                tiles = [None, None]
                for head in range(3 * k, 3 * k + 3):
                    side = head % 2
                    block = gm[l, which, head // 2][side * 64 : (side + 1) * 64]
                    block = jnp.where(left[:64] if side == 0 else jnp.logical_not(left[:64]), block, 0.0)
                    tile = (head % 3) // 2
                    tiles[tile] = block if tiles[tile] is None else tiles[tile] + block
                for tile in range(2):
                    first = (which * 2 + tile) * 128
                    into[l * 64 : (l + 1) * 64, first : first + 128] = tiles[tile].astype(BF)
    cC(c).start()
    absorb(c - 1)
    absorb(c)

    def tail(t, carry):
        step(t)
        return carry

    lax.fori_loop(slot[0], count + len(stages) - 1, tail, 0)
    cC(count - 2).wait_send()
    cC(count - 1).wait_send()

    def drain(c, carry):
        for copy in (cY, cZ1, cZ2, cA2, cA1, cB):
            copy(c).wait_send()
        cO(c).wait()
        return carry

    lax.fori_loop(0, count, drain, 0)


def backward(n, cot, norms, maps, mask, chain, last, coef, saved):
    group, _ = owners(n)
    m = cot.shape[0]
    count = 25
    extra = len([v for v in range(2, 10) if (1 << v) < n // 2])
    vmem = pl.BlockSpec(memory_space=pltpu.VMEM)
    anywhere = pl.BlockSpec(memory_space=pl.ANY)
    pair = lambda: pltpu.SemaphoreType.DMA((2, count))
    V = lambda kind, *shape: pltpu.VMEM(shape, kind)
    return pl.pallas_call(
        functools.partial(backward_kernel, n, count),
        name="backward",
        out_shape=(jax.ShapeDtypeStruct((count, CHUNK, D), BF), jax.ShapeDtypeStruct((m, D), BF)),
        in_specs=[vmem] * 6 + [pl.BlockSpec(memory_space=pltpu.SMEM)] + [anywhere] * 14,
        out_specs=[anywhere, vmem],
        scratch_shapes=[
            V(BF, count, 2, CHUNK, D), V(BF, count, CHUNK, D), V(BF, count, CHUNK, 384), V(BF, count, CHUNK // 2, 384),
            V(BF, count, CHUNK // 4, 384), V(BF, count if extra else 1, extra + 1, CHUNK // 4, 384), V(BF, 2, 2, 2, CHUNK, D),
            V(BF, 2, 1536, D), V(BF, 2, m, D), V(BF, 2, m, D), V(BF, m, D), V(F32, m, D), V(F32, m, D), V(F32, m, D),
            V(BF, m, 2304), V(BF, 2, 1536, m), V(BF, 2, STATE_ROWS, 128), V(BF, m, D), V(F32, m, D), V(BF, m, 1536), V(BF, m, D),
            V(F32, m, D), V(BF, 4, m, D), V(F32, m, D), V(F32, 1536, m), V(F32, D, m), V(BF, 2304, m), V(BF, D, m), V(F32, m, D),
            V(F32, 2, 2, 6, 128, 128), V(F32, 8, D), V(F32, 2, 128, 128), V(BF, 2, STATE_ROWS, 128),
            V(BF, 2, n, group, 128), V(BF, 2, n, group, 128), V(BF, 2, STATE_ROWS, 128),
            pair(), pair(), pair(), pair(), pair(), pltpu.SemaphoreType.DMA((2, count, max(extra, 1))), pair(), pair(), pair(),
            pltpu.SemaphoreType.DMA((count,)), pltpu.SemaphoreType.DMA((2, 2, 4)), pltpu.SemaphoreType.DMA((2,)),
            pltpu.SemaphoreType.DMA((2, 2)), pltpu.SemaphoreType.DMA((11,)),
        ],
        compiler_params=pltpu.CompilerParams(collective_id=1, has_side_effects=True, vmem_limit_bytes=63 * 2**20),
    )(cot, norms, maps, mask, chain, last, coef, *saved)


def finish_kernel(x_ref, down, up, out, inner):
    j = pl.program_id(1)

    @pl.when(j == 0)
    def _():
        for k in range(4):
            down[0, :, k * D : (k + 1) * D] = x_ref[k].astype(F32)

    @pl.when(j == 1)
    def _():
        for k in range(4):
            up[0, k * CHUNK : (k + 1) * CHUNK] = x_ref[k].astype(F32)

    @pl.when(j == 2)
    def _():
        out[0] = x_ref[0].astype(F32)
        for k in range(3):
            inner[0, k * CHUNK : (k + 1) * CHUNK] = x_ref[k + 1].astype(F32)


def finish(total, layers):
    shape = lambda *dims: jax.ShapeDtypeStruct((layers,) + dims, F32)
    whole = lambda *dims: pl.BlockSpec((1,) + dims, lambda l, j: (l, 0, 0))
    return pl.pallas_call(
        finish_kernel,
        name="finish",
        grid=(layers, 3),
        out_shape=(shape(CHUNK, 3072), shape(D, D), shape(CHUNK, D), shape(3 * CHUNK, D)),
        in_specs=[pl.BlockSpec((4, CHUNK, D), lambda l, j: ((layers - 1 - l) * 3 + j, 0, 0))],
        out_specs=[whole(CHUNK, 3072), whole(D, D), whole(CHUNK, D), whole(3 * CHUNK, D)],
        compiler_params=pltpu.CompilerParams(vmem_limit_bytes=40 * 2**20),
    )(total)


def prologue(lengths, attn_in, attn_out, mlp_in, mlp_out, norm_gains, norm_biases, feature_maps, tok_rows):
    layers = attn_in.shape[0]
    n = lax.axis_size("seq")
    me = lax.axis_index("seq")
    first = me * tok_rows
    starts = jnp.cumsum(lengths, axis=1) - lengths
    seg = lambda p: jnp.sum((starts[:, None, :] <= p[None, :, None]).astype(jnp.int32), axis=2) - 1
    ids = seg(first + jnp.arange(tok_rows, dtype=jnp.int32))
    firsts = jnp.arange(n, dtype=jnp.int32) * tok_rows
    before, final = seg(firsts - 1), seg(firsts + tok_rows - 1)
    prior = seg((first - 1)[None])
    chain = jnp.broadcast_to((ids == prior).astype(F32)[:, :, None], ids.shape + (128,))
    last = (ids == ids[:, -1:]).astype(F32)[:, None, :]
    lower = jnp.tril(jnp.ones((tok_rows, tok_rows), F32))
    mask = (ids[:, :, None] == ids[:, None, :]).astype(F32) * lower[None]
    order = jnp.arange(n)
    coef = ((final[:, None, :] == before[:, :, None]) & (order[None, :] < order[:, None])[None]).astype(F32)
    coef_back = jnp.swapaxes(coef, 1, 2)
    packed = jnp.concatenate(
        [
            jnp.swapaxes(attn_in, 1, 2),
            jnp.swapaxes(attn_out, 1, 2),
            mlp_in,
            jnp.transpose(mlp_out.reshape(layers, 4, 768, 192), (0, 1, 3, 2)).reshape(layers, 768, 768),
        ],
        axis=1,
    )
    small = jnp.concatenate([norm_gains[:, :, None], norm_biases[:, :, None], feature_maps], axis=2)
    count = layers * 33
    small = jnp.pad(small.reshape(count, 768), ((0, -count % 16), (0, 0)))
    smalls = gather_small(small)[:, :count].reshape(4, layers, 2, 66, 192)
    smalls = jnp.transpose(smalls, (1, 2, 3, 0, 4)).reshape(layers, 2, 66, 768)
    norms = smalls[:, :, :2].astype(F32)
    maps = jnp.transpose(smalls[:, :, 2:].reshape(layers, 2, 64, 6, 2, 64), (0, 1, 3, 4, 5, 2))
    maps = (maps[:, :, :, :, :, None, :] * jnp.eye(2, dtype=BF)[:, None, :, None]).reshape(layers, 2, 6, 128, 128)
    chain_row = (ids == prior).astype(F32)[:, None, :]
    return packed, norms, maps, jnp.swapaxes(maps, 3, 4), mask, chain, chain_row, last, coef.reshape(-1), coef_back.reshape(-1)


def shards(tokens, cotangent, lengths, attn_in, attn_out, mlp_in, mlp_out, norm_gains, norm_biases, feature_maps):
    tok_rows = tokens.shape[1]
    layers = attn_in.shape[0]
    n = lax.axis_size("seq")
    packed, norms, maps, maps_back, mask, chain, chain_row, last, coef, coef_back = prologue(
        lengths, attn_in, attn_out, mlp_in, mlp_out, norm_gains, norm_biases, feature_maps, tok_rows
    )
    *saved, block_output = forward(n, tokens.reshape(-1, D), packed, norms, maps, mask, chain, last, coef)
    total, grad_tokens = backward(
        n, cotangent.reshape(-1, D), norms, maps_back, mask, chain_row, last, coef_back, saved
    )
    grad_down, grad_up, grad_out, grad_in = finish(total, layers)
    grad_down, grad_out, grad_in = (jnp.swapaxes(v, 1, 2) for v in (grad_down, grad_out, grad_in))
    b = lax.axis_index("batch")
    norm_rows = lax.dynamic_slice(total[-1, 128:136], (0, b * 192), (8, 192)).astype(F32).reshape(layers, 2, 2, 192)
    tiles = total[-1, :128, :512].astype(F32).reshape(layers, 64, 2, 2, 2, 64)
    even = b % 2 == 0
    first = jnp.where(even, tiles[:, :, :, 0, 0], tiles[:, :, :, 0, 1])
    second = jnp.where(even, tiles[:, :, :, 0, 1], tiles[:, :, :, 0, 0])
    third = jnp.where(even, tiles[:, :, :, 1, 0], tiles[:, :, :, 1, 1])
    grad_maps = jnp.stack([first, second, third], axis=3)
    grad_maps = jnp.transpose(grad_maps, (0, 2, 4, 3, 1)).reshape(layers, 2, 64, 192)
    return (
        block_output.reshape(tokens.shape),
        grad_tokens.reshape(tokens.shape),
        grad_in,
        grad_out,
        grad_up,
        grad_down,
        norm_rows[:, :, 0],
        norm_rows[:, :, 1],
        grad_maps,
        norm_rows[:, 1, 1],
    )


def solution(mesh):
    in_specs = (
        P("batch", "seq", None),
        P("batch", "seq", None),
        P("batch", None),
        P(None, None, "batch"),
        P(None, None, "batch"),
        P(None, None, "batch"),
        P(None, None, "batch"),
        P(None, None, "batch"),
        P(None, None, "batch"),
        P(None, None, None, "batch"),
    )
    out_specs = (
        P("batch", "seq", None),
        P("batch", "seq", None),
        P(None, None, "batch"),
        P(None, None, "batch"),
        P(None, None, "batch"),
        P(None, None, "batch"),
        P(None, None, "batch"),
        P(None, None, "batch"),
        P(None, None, None, "batch"),
        P(None, "batch"),
    )
    return jax.shard_map(shards, mesh=mesh, in_specs=in_specs, out_specs=out_specs, check_vma=False)
```
